256 devices in a mesh: dp: 32 (over y_lo, z, core), ctx: 8 (over x, y_hi).
Axes of the slice: x: 4, y: 4 (y_hi: 2, y_lo: 2; y = y_hi * 2 + y_lo), z: 8, core: 2. Of those that a mesh axis runs over, the one named last changes fastest.
Arguments:
- queries: bfloat16 [32, 1024, 4096], P('dp', 'ctx'), may hold values from -10 to 10
- key_states: bfloat16 [32, 1024, 512], P('dp', 'ctx'), may hold values from -10 to 10
- value_states: bfloat16 [32, 1024, 512], P('dp', 'ctx'), may hold values from -6 to 6
- out_grad: bfloat16 [32, 1024, 4096], P('dp', 'ctx'), may hold values from -6 to 6
- destinations: int32 [32, 256], P('dp', 'ctx'), may hold values from 0 to 31, as said below
- documents: int32 [32, 1024], P('dp'), may hold values from 0 to 512, as said below
Outputs:
- attended: bfloat16 [32, 1024, 4096], P('dp', 'ctx')
- query_grad: bfloat16 [32, 1024, 4096], P('dp', 'ctx')
- key_grad: bfloat16 [32, 1024, 512], P('dp', 'ctx')
- value_grad: bfloat16 [32, 1024, 512], P('dp', 'ctx')
The draws below stay inside these ranges and needn't reach their ends.
Inputs may be any that keep to these rules, and one draw needn't show every extreme that they name: `destinations`: for each pack and each block of 128 positions, the 32 entries of the block are a permutation of the pack numbers: every block sends exactly one unit to every pack, its own included. `documents`: document numbers start at 0 and never fall along a pack, by one at most from position to position; the longest document of each pack has exactly 512 positions; in pack 0 every other document has one position.
All inputs are finite; a program needn't handle non-finite values.
Results may differ from the reference program's by a relative error of at most 0.019.
Values may be sent and summed in bfloat16 or wider, within the bound.
No kernel may reach another device: no remote copies, remote signals or barrier semaphores. Data moves between devices by JAX's collectives and lax.ppermute only.
A program may use at most 128 MiB of HBM per device.

```python
import jax
import jax.numpy as jnp
from jax import lax

HEAD_DIM = 128
KV_HEADS = 4
GROUP = 8
UNIT = 4
Q_HEADS = 32
PACKS = 32
TOK_DEV = 128
PACK_LEN = 1024
N_CTX = 8


def pack_layout(key):
    route_key = jax.random.fold_in(key, 11)
    layout_key = jax.random.fold_in(key, 12)
    route_keys = jax.random.split(route_key, PACKS * N_CTX)
    routes = jax.vmap(lambda subkey: jax.random.permutation(subkey, PACKS))(route_keys)
    routes = routes.reshape(PACKS, N_CTX * PACKS).astype(jnp.int32)
    boundary_key, opening_key = jax.random.split(layout_key)
    half_pack = PACK_LEN // 2
    position = jnp.arange(PACK_LEN, dtype=jnp.int32)[None, :]
    pack_index = jnp.arange(PACKS, dtype=jnp.int32)[:, None]
    opening = jax.random.randint(opening_key, (PACKS, 1), 0, PACK_LEN - half_pack + 1)
    boundary = jax.random.randint(boundary_key, (PACKS, PACK_LEN), 0, TOK_DEV) < 3
    boundary = boundary | (pack_index == 0)
    inside = (position > opening) & (position < opening + half_pack)
    boundary = boundary & jnp.logical_not(inside) | (position == opening) | (position == opening + half_pack)
    boundary = boundary & (position > 0)
    documents = jnp.cumsum(boundary.astype(jnp.int32), axis=1).astype(jnp.int32)
    return (routes, documents)


def draw_queries(key, part):
    key = jax.random.fold_in(key, 3)
    values = jax.random.truncated_normal(key, -6.0, 6.0, (PACKS, PACK_LEN, KV_HEADS * GROUP * HEAD_DIM))
    return values.astype(jnp.bfloat16)


def draw_key_states(key, part):
    key = jax.random.fold_in(key, 4)
    values = jax.random.truncated_normal(key, -6.0, 6.0, (PACKS, PACK_LEN, KV_HEADS * HEAD_DIM))
    return values.astype(jnp.bfloat16)


def draw_destinations(key, part):
    routes, documents = pack_layout(key)
    return routes


def draw_documents(key, part):
    routes, documents = pack_layout(key)
    return documents


def levels(rng, dims, shards, low, largest):
    def one(dim, parts):
        steps = jax.random.uniform(jax.random.fold_in(jax.random.fold_in(rng, 6), dim), (parts,), jnp.float32, low / len(shards), largest / len(shards))
        return jnp.repeat(jnp.exp(steps), dims[dim] // parts).reshape((-1,) + (1,) * (len(dims) - dim - 1))

    gain = one(*shards[0])
    for cut in shards[1:]:
        gain = gain * one(*cut)
    return gain


def gaussian(rng, shape, deviation, reach, cuts=(), kind=jnp.bfloat16):
    factor_of = levels(rng, shape, cuts, -0.22, 0.18) if cuts else 1.0
    array = jax.random.normal(rng, shape, jnp.float32) * deviation * factor_of
    return jnp.minimum(jnp.maximum(array, -reach), reach).astype(kind)


def setup_inputs(seed: int = 0) -> dict:
    key_of = jax.random.split(jax.random.key(seed), 7)
    return {
        "queries": draw_queries(jax.random.fold_in(key_of[6], 71), 0),
        "key_states": draw_key_states(jax.random.fold_in(key_of[6], 71), 0),
        "value_states": gaussian(key_of[2], (PACKS, PACK_LEN, KV_HEADS * HEAD_DIM), 1.0, 6.0, ((0, 32), (1, 8))),
        "out_grad": gaussian(key_of[3], (PACKS, PACK_LEN, Q_HEADS * HEAD_DIM), 1.0, 6.0, ((0, 32), (1, 8))),
        "destinations": draw_destinations(jax.random.fold_in(key_of[6], 71), 0),
        "documents": draw_documents(jax.random.fold_in(key_of[6], 71), 0),
    }


def to_moved(source, route):
    width = source.shape[-1]
    blocks = source.reshape(PACKS, N_CTX, PACKS, UNIT, width)
    slots = jnp.arange(PACKS, dtype=jnp.int32)
    owner = jnp.sum(jnp.where(route[:, :, :, None] == slots[None, None, None, :], slots[None, None, :, None], 0), axis=2).astype(jnp.int32)
    sender = slots[None, None, :]
    context = jnp.arange(N_CTX, dtype=jnp.int32)[None, :, None]
    unit_index = jnp.transpose(owner, (2, 1, 0))
    moved = blocks[sender, context, unit_index]
    return moved.reshape(PACKS, PACK_LEN, width)


def to_source(moved, route):
    width = moved.shape[-1]
    blocks = moved.reshape(PACKS, N_CTX, PACKS, UNIT, width)
    context = jnp.arange(N_CTX, dtype=jnp.int32)[None, :, None]
    sender = jnp.arange(PACKS, dtype=jnp.int32)[:, None, None]
    return blocks[route, context, sender].reshape(PACKS, PACK_LEN, width)


def head_group(query_rows, key_rows, value_rows, grad_rows, documents):
    query_wide = query_rows.astype(jnp.float32)
    key_wide = key_rows.astype(jnp.float32)
    value_wide = value_rows.astype(jnp.float32)
    grad_wide = grad_rows.astype(jnp.float32)
    factor = HEAD_DIM ** -0.5
    position = jnp.arange(documents.shape[0], dtype=jnp.int32)
    allowed = (documents[:, None] == documents[None, :]) & (position[None, :] <= position[:, None])
    allowed = allowed[:, None, :]
    scores = jnp.einsum("qgd,kd->qgk", query_wide, key_wide) * factor
    row_max = jnp.max(jnp.where(allowed, scores, -jnp.inf), axis=2, keepdims=True)
    weights = jnp.where(allowed, jnp.exp(scores - row_max), 0.0)
    weight_sum = jnp.sum(weights, axis=2, keepdims=True)
    rounded = weights.astype(jnp.bfloat16).astype(jnp.float32)
    output = (jnp.einsum("qgk,kd->qgd", rounded, value_wide) / weight_sum).astype(jnp.bfloat16)
    log_total = row_max + jnp.log(weight_sum)
    row_dot = jnp.sum(grad_wide * output.astype(jnp.float32), axis=2, keepdims=True)
    chances = jnp.where(allowed, jnp.exp(scores - log_total), 0.0)
    pushes = jnp.einsum("qgd,kd->qgk", grad_wide, value_wide)
    slopes = (chances * (pushes - row_dot)).astype(jnp.bfloat16).astype(jnp.float32)
    query_sum = (jnp.einsum("qgk,kd->qgd", slopes, key_wide) * factor).astype(jnp.bfloat16)
    key_sum = (jnp.einsum("qgk,qgd->kd", slopes, query_wide) * factor).astype(jnp.bfloat16)
    rounded_chances = chances.astype(jnp.bfloat16).astype(jnp.float32)
    value_sum = jnp.einsum("qgk,qgd->kd", rounded_chances, grad_wide).astype(jnp.bfloat16)
    return output, query_sum, key_sum, value_sum


def one_pack(arrays):
    query_rows, key_rows, value_rows, grad_rows, documents = arrays
    query_rows = query_rows.reshape(PACK_LEN, KV_HEADS, GROUP, HEAD_DIM).transpose(1, 0, 2, 3)
    grad_rows = grad_rows.reshape(PACK_LEN, KV_HEADS, GROUP, HEAD_DIM).transpose(1, 0, 2, 3)
    key_rows = key_rows.reshape(PACK_LEN, KV_HEADS, HEAD_DIM).transpose(1, 0, 2)
    value_rows = value_rows.reshape(PACK_LEN, KV_HEADS, HEAD_DIM).transpose(1, 0, 2)
    output, query_sum, key_sum, value_sum = lax.map(
        lambda bundle: head_group(bundle[0], bundle[1], bundle[2], bundle[3], documents),
        (query_rows, key_rows, value_rows, grad_rows))
    return (output.transpose(1, 0, 2, 3).reshape(PACK_LEN, KV_HEADS * GROUP * HEAD_DIM),
            query_sum.transpose(1, 0, 2, 3).reshape(PACK_LEN, KV_HEADS * GROUP * HEAD_DIM),
            key_sum.transpose(1, 0, 2).reshape(PACK_LEN, KV_HEADS * HEAD_DIM),
            value_sum.transpose(1, 0, 2).reshape(PACK_LEN, KV_HEADS * HEAD_DIM))


def reference(queries, key_states, value_states, out_grad, destinations, documents):
    route = destinations.reshape(PACKS, N_CTX, PACKS)
    moved = lax.map(one_pack, (to_moved(queries, route), to_moved(key_states, route),
                               to_moved(value_states, route), to_moved(out_grad, route), documents))
    return (to_source(moved[0], route), to_source(moved[1], route),
            to_source(moved[2], route), to_source(moved[3], route))
```

```python
import jax
import jax.numpy as jnp
from jax import lax
from jax.experimental import pallas as pl
from jax.experimental.pallas import tpu as pltpu
from jax.sharding import PartitionSpec as P

HEAD_DIM = 128
GROUP = 8
HALF = 4
UNIT = 4
BLOCK = 128
REACH = 512
ROWS = 40
FAR_BELOW = -1e30
FACTOR = HEAD_DIM**-0.5
LOG2E = 1.4426950408889634

f32 = jnp.float32
bf16 = jnp.bfloat16


def dot(a, b):
    return jnp.dot(a, b, preferred_element_type=f32)


def dot_nt(a, b):
    return lax.dot_general(a, b, (((1,), (1,)), ((), ())), preferred_element_type=f32)


def key_row(route, heads):
    units = BLOCK // UNIT
    wide = heads * BLOCK
    unit = lax.broadcasted_iota(jnp.int32, (units, wide), 0)
    col = lax.broadcasted_iota(jnp.int32, (units, wide), 1)
    spread = ((col % BLOCK) // UNIT == unit).astype(f32).astype(bf16)
    packs = jnp.broadcast_to(route.astype(f32), (8, units)).astype(bf16)
    where = dot(packs, spread)
    col = lax.broadcasted_iota(jnp.int32, (8, wide), 1)
    inner = (col // BLOCK) * UNIT + col % UNIT
    return where * (heads * UNIT) + inner.astype(f32)


def key_column(route, heads):
    units = BLOCK // UNIT
    tall = heads * BLOCK
    row = lax.broadcasted_iota(jnp.int32, (tall, units), 0)
    unit = lax.broadcasted_iota(jnp.int32, (tall, units), 1)
    packs = jnp.broadcast_to(route.astype(f32), (tall, units))
    where = jnp.sum(
        jnp.where((row % BLOCK) // UNIT == unit, packs, 0.0), axis=1, keepdims=True
    )
    row = lax.broadcasted_iota(jnp.int32, (tall, 1), 0)
    inner = (row // BLOCK) * UNIT + row % UNIT
    return where * (heads * UNIT) + inner.astype(f32)


def sending_matrix(route, heads):
    size = heads * BLOCK
    rows = lax.broadcasted_iota(jnp.int32, (size, size), 0).astype(f32)
    return (key_row(route, heads)[0:1] == rows).astype(f32).astype(bf16)


def returning_matrix(route, heads):
    size = heads * BLOCK
    cols = lax.broadcasted_iota(jnp.int32, (size, size), 1).astype(f32)
    return (key_column(route, heads) == cols).astype(f32).astype(bf16)


def send_kernel(route_ref, q_ref, k_ref, v_ref, do_ref, out_ref, move_q, move_kv):
    @pl.when(pl.program_id(0) == 0)
    def _():
        move_q[...] = sending_matrix(route_ref[...], HALF)
        move_kv[...] = sending_matrix(route_ref[...], 2)

    packs = BLOCK // UNIT
    pair = jnp.concatenate([k_ref[...], v_ref[...]], axis=0)
    kv = dot(move_kv[...], pair).astype(bf16).reshape(packs, 2 * UNIT, HEAD_DIM)
    for half in range(2):
        heads = [
            slice((half * HALF + h) * HEAD_DIM, (half * HALF + h + 1) * HEAD_DIM)
            for h in range(HALF)
        ]
        both = jnp.concatenate(
            [
                jnp.concatenate([q_ref[:, at] for at in heads], axis=0),
                jnp.concatenate([do_ref[:, at] for at in heads], axis=0),
            ],
            axis=1,
        )
        moved = dot(move_q[...], both).astype(bf16)
        base = half * packs
        wide = HALF * UNIT
        out_ref[base : base + packs, 0:wide, :] = moved[:, :HEAD_DIM].reshape(
            packs, wide, HEAD_DIM
        )
        out_ref[base : base + packs, wide : 2 * wide, :] = moved[:, HEAD_DIM:].reshape(
            packs, wide, HEAD_DIM
        )
        out_ref[base : base + packs, 2 * wide :, :] = kv


def return_kernel(route_ref, in_ref, o_ref, dq_ref, dk_ref, dv_ref, move_q, move_kv):
    @pl.when(pl.program_id(0) == 0)
    def _():
        move_q[...] = returning_matrix(route_ref[...], HALF)
        move_kv[...] = returning_matrix(route_ref[...], 2)

    packs = BLOCK // UNIT
    wide = HALF * UNIT
    pair = jnp.zeros((2 * BLOCK, HEAD_DIM), f32)
    for half in range(2):
        base = half * packs
        o = in_ref[base : base + packs, 0:wide, :].reshape(packs * wide, HEAD_DIM)
        dq = in_ref[base : base + packs, wide : 2 * wide, :].reshape(packs * wide, HEAD_DIM)
        back = dot(move_q[...], jnp.concatenate([o, dq], axis=1)).astype(bf16)
        for h in range(HALF):
            at = slice((half * HALF + h) * HEAD_DIM, (half * HALF + h + 1) * HEAD_DIM)
            rows = slice(h * BLOCK, (h + 1) * BLOCK)
            o_ref[:, at] = back[rows, :HEAD_DIM]
            dq_ref[:, at] = back[rows, HEAD_DIM:]
        kv = in_ref[base : base + packs, 2 * wide :, :].reshape(2 * BLOCK, HEAD_DIM)
        pair = pair + dot(move_kv[...], kv)
    dk_ref[...] = pair[:BLOCK].astype(bf16)
    dv_ref[...] = pair[BLOCK:].astype(bf16)


def attend_kernel(
    row_docs, col_docs, in_ref, out_ref, keys, values, keys_t, values_t, dkeys, dvalues
):
    blocks = row_docs.shape[0]
    packs = BLOCK // UNIT
    wide = HALF * UNIT
    tall = HALF * BLOCK
    r = lax.broadcasted_iota(jnp.int32, (2 * BLOCK, 2 * BLOCK), 0)
    c = lax.broadcasted_iota(jnp.int32, (2 * BLOCK, 2 * BLOCK), 1)

    def place(x):
        return ((x % BLOCK) // UNIT) * (2 * UNIT) + (x // BLOCK) * UNIT + x % UNIT

    apart = (place(r) == c).astype(f32).astype(bf16)
    together = (place(c) == r).astype(f32).astype(bf16)
    lane = lax.broadcasted_iota(jnp.int32, (BLOCK, tall), 1)
    earlier = lax.broadcasted_iota(jnp.int32, (BLOCK, tall), 0) <= (
        (lane // wide) * UNIT + lane % UNIT
    )
    back = (REACH + BLOCK - 2) // BLOCK

    for b in range(blocks):
        here = slice(b * BLOCK, (b + 1) * BLOCK)
        mine = slice(b * packs, (b + 1) * packs)
        low = max(0, b - back)
        seen = slice(low * BLOCK, (b + 1) * BLOCK)
        count = b + 1 - low
        kv = in_ref[mine, 2 * wide :, :].reshape(2 * BLOCK, HEAD_DIM)
        kv = dot(apart, kv)
        keys[here, :] = kv[:BLOCK].astype(bf16)
        values[here, :] = kv[BLOCK:].astype(bf16)
        keys_t[:, here] = kv[:BLOCK].T.astype(bf16)
        values_t[:, here] = kv[BLOCK:].T.astype(bf16)
        dkeys[here, :] = jnp.zeros((BLOCK, HEAD_DIM), f32)
        dvalues[here, :] = jnp.zeros((BLOCK, HEAD_DIM), f32)

        q = in_ref[mine, 0:wide, :].reshape(tall, HEAD_DIM)
        do = in_ref[mine, wide : 2 * wide, :].reshape(tall, HEAD_DIM)
        do_t = do.astype(f32).T
        docs = row_docs[b : b + 1, :]
        scores = dot_nt(keys[seen, :], q)
        parts = []
        for n in range(count):
            at = slice((low + n) * BLOCK, (low + n + 1) * BLOCK)
            allowed = col_docs[at, 0:1] == docs
            if n == count - 1:
                allowed = allowed & earlier
            parts.append(
                jnp.where(allowed, scores[n * BLOCK : (n + 1) * BLOCK], FAR_BELOW)
            )
        scores = jnp.concatenate(parts, axis=0)
        row_max = jnp.max(scores, axis=0, keepdims=True)
        weights = jnp.exp2((scores - row_max) * (FACTOR * LOG2E))
        inverse = 1.0 / jnp.sum(weights, axis=0, keepdims=True)
        chances = weights * inverse
        rounded = chances.astype(bf16)
        out_t = dot(values_t[:, seen], rounded).astype(bf16).astype(f32)
        row_dot = jnp.sum(out_t * do_t, axis=0, keepdims=True)
        pushes = dot_nt(values[seen, :], do)
        slopes = (chances * (pushes - row_dot)).astype(bf16)
        dq_t = dot(keys_t[:, seen], slopes) * FACTOR
        dkeys[seen, :] += dot(slopes, q)
        dvalues[seen, :] += dot(rounded, do)
        out_ref[mine, 0:wide, :] = out_t.T.astype(bf16).reshape(packs, wide, HEAD_DIM)
        out_ref[mine, wide : 2 * wide, :] = (
            dq_t.T.astype(bf16).reshape(packs, wide, HEAD_DIM)
        )

    for b in range(blocks):
        here = slice(b * BLOCK, (b + 1) * BLOCK)
        mine = slice(b * packs, (b + 1) * packs)
        pair = jnp.concatenate(
            [(dkeys[here, :] * FACTOR).astype(bf16), dvalues[here, :].astype(bf16)], axis=0
        )
        pair = dot(together, pair).astype(bf16)
        out_ref[mine, 2 * wide :, :] = pair.reshape(packs, 2 * UNIT, HEAD_DIM)


def local(queries, key_states, value_states, out_grad, destinations, documents):
    contexts = lax.axis_size("ctx")
    packs = lax.axis_size("dp")
    kv_heads = key_states.shape[2] // HEAD_DIM
    wide = GROUP * HEAD_DIM
    moved_shape = jax.ShapeDtypeStruct((contexts * packs, ROWS, HEAD_DIM), bf16)
    route_spec = pl.BlockSpec((1, packs), lambda m: (0, 0))
    wide_spec = pl.BlockSpec((None, BLOCK, wide), lambda m: (0, 0, m))
    narrow_spec = pl.BlockSpec((None, BLOCK, HEAD_DIM), lambda m: (0, 0, m))
    moved_spec = pl.BlockSpec((2 * packs, ROWS, HEAD_DIM), lambda m: (m, 0, 0))
    matrices = [
        pltpu.VMEM((HALF * BLOCK, HALF * BLOCK), bf16),
        pltpu.VMEM((2 * BLOCK, 2 * BLOCK), bf16),
    ]
    params = pltpu.CompilerParams(vmem_limit_bytes=48 * 1024 * 1024)
    sending = pl.pallas_call(
        send_kernel,
        grid=(kv_heads,),
        in_specs=[route_spec, wide_spec, narrow_spec, narrow_spec, wide_spec],
        out_specs=moved_spec,
        out_shape=moved_shape,
        scratch_shapes=matrices,
        compiler_params=params,
    )(destinations, queries, key_states, value_states, out_grad)

    received = lax.all_to_all(sending, ("ctx", "dp"), split_axis=0, concat_axis=0, tiled=True)

    length = documents.shape[1]
    row_docs = jnp.broadcast_to(
        documents.reshape(contexts, packs, 1, UNIT), (contexts, packs, HALF, UNIT)
    ).reshape(contexts, HALF * BLOCK)
    col_docs = jnp.broadcast_to(documents.reshape(length, 1), (length, HEAD_DIM))
    whole = pl.BlockSpec(memory_space=pltpu.VMEM)
    results = pl.pallas_call(
        attend_kernel,
        in_specs=[whole, whole, whole],
        out_specs=whole,
        out_shape=moved_shape,
        scratch_shapes=[
            pltpu.VMEM((length, HEAD_DIM), bf16),
            pltpu.VMEM((length, HEAD_DIM), bf16),
            pltpu.VMEM((HEAD_DIM, length), bf16),
            pltpu.VMEM((HEAD_DIM, length), bf16),
            pltpu.VMEM((length, HEAD_DIM), f32),
            pltpu.VMEM((length, HEAD_DIM), f32),
        ],
        compiler_params=params,
    )(row_docs, col_docs, received)

    returned = lax.all_to_all(results, ("ctx", "dp"), split_axis=0, concat_axis=0, tiled=True)

    return pl.pallas_call(
        return_kernel,
        grid=(kv_heads,),
        in_specs=[route_spec, moved_spec],
        out_specs=[wide_spec, wide_spec, narrow_spec, narrow_spec],
        out_shape=[
            jax.ShapeDtypeStruct(queries.shape, bf16),
            jax.ShapeDtypeStruct(queries.shape, bf16),
            jax.ShapeDtypeStruct(key_states.shape, bf16),
            jax.ShapeDtypeStruct(key_states.shape, bf16),
        ],
        scratch_shapes=matrices,
        compiler_params=params,
    )(destinations, returned)


def solution(mesh):
    spec = P("dp", "ctx", None)
    return jax.shard_map(
        local,
        mesh=mesh,
        in_specs=(spec, spec, spec, spec, P("dp", "ctx"), P("dp", None)),
        out_specs=(spec, spec, spec, spec),
        check_vma=False,
    )
```

```python
import jax
import jax.numpy as jnp
from jax import lax
from jax.experimental import pallas as pl
from jax.experimental.pallas import tpu as pltpu
from jax.sharding import PartitionSpec as P

HEAD_DIM = 128
GROUP = 8
HALF = 4
UNIT = 4
BLOCK = 128
REACH = 512
HEADS = GROUP * UNIT
ROWS = 2 * HEADS + 2 * UNIT
FAR_BELOW = -1e30
FACTOR = HEAD_DIM**-0.5
LOG2E = 1.4426950408889634

f32 = jnp.float32
bf16 = jnp.bfloat16


def dot(a, b):
    return jnp.dot(a, b, preferred_element_type=f32)


def dot_nt(a, b):
    return lax.dot_general(a, b, (((1,), (1,)), ((), ())), preferred_element_type=f32)


def key_row(route, heads):
    units = BLOCK // UNIT
    wide = heads * BLOCK
    unit = lax.broadcasted_iota(jnp.int32, (units, wide), 0)
    col = lax.broadcasted_iota(jnp.int32, (units, wide), 1)
    spread = ((col % BLOCK) // UNIT == unit).astype(f32).astype(bf16)
    packs = jnp.broadcast_to(route.astype(f32), (8, units)).astype(bf16)
    where = dot(packs, spread)
    col = lax.broadcasted_iota(jnp.int32, (8, wide), 1)
    inner = (col // BLOCK) * UNIT + col % UNIT
    return where * (heads * UNIT) + inner.astype(f32)


def key_column(route, heads):
    units = BLOCK // UNIT
    tall = heads * BLOCK
    row = lax.broadcasted_iota(jnp.int32, (tall, units), 0)
    unit = lax.broadcasted_iota(jnp.int32, (tall, units), 1)
    packs = jnp.broadcast_to(route.astype(f32), (tall, units))
    where = jnp.sum(
        jnp.where((row % BLOCK) // UNIT == unit, packs, 0.0), axis=1, keepdims=True
    )
    row = lax.broadcasted_iota(jnp.int32, (tall, 1), 0)
    inner = (row // BLOCK) * UNIT + row % UNIT
    return where * (heads * UNIT) + inner.astype(f32)


def sending_matrix(route, heads):
    size = heads * BLOCK
    rows = lax.broadcasted_iota(jnp.int32, (size, size), 0).astype(f32)
    return (key_row(route, heads)[0:1] == rows).astype(f32).astype(bf16)


def returning_matrix(route, heads):
    size = heads * BLOCK
    cols = lax.broadcasted_iota(jnp.int32, (size, size), 1).astype(f32)
    return (key_column(route, heads) == cols).astype(f32).astype(bf16)


def slots_of(route):
    return (route % 2) * (BLOCK // UNIT // 2) + route // 2


def send_kernel(route_ref, q_ref, k_ref, v_ref, do_ref, out_ref, move_q, move_kv):
    @pl.when(pl.program_id(0) == 0)
    def _():
        slots = slots_of(route_ref[...])
        move_q[...] = sending_matrix(slots, HALF)
        move_kv[...] = sending_matrix(slots, 2)

    packs = BLOCK // UNIT
    wide = HALF * UNIT
    for half in range(2):
        heads = [
            slice((half * HALF + h) * HEAD_DIM, (half * HALF + h + 1) * HEAD_DIM)
            for h in range(HALF)
        ]
        both = jnp.concatenate(
            [
                jnp.concatenate([q_ref[:, at] for at in heads], axis=0),
                jnp.concatenate([do_ref[:, at] for at in heads], axis=0),
            ],
            axis=1,
        )
        moved = dot(move_q[...], both).astype(bf16)
        low = half * wide
        out_ref[:, low : low + wide, :] = moved[:, :HEAD_DIM].reshape(packs, wide, HEAD_DIM)
        low = HEADS + half * wide
        out_ref[:, low : low + wide, :] = moved[:, HEAD_DIM:].reshape(packs, wide, HEAD_DIM)
    pair = jnp.concatenate([k_ref[...], v_ref[...]], axis=0)
    out_ref[:, 2 * HEADS :, :] = (
        dot(move_kv[...], pair).astype(bf16).reshape(packs, 2 * UNIT, HEAD_DIM)
    )


def return_kernel(route_ref, in_ref, o_ref, dq_ref, dk_ref, dv_ref, move_q, move_kv):
    @pl.when(pl.program_id(0) == 0)
    def _():
        slots = slots_of(route_ref[...])
        move_q[...] = returning_matrix(slots, HALF)
        move_kv[...] = returning_matrix(slots, 2)

    packs = BLOCK // UNIT
    wide = HALF * UNIT
    for half in range(2):
        low = half * wide
        o = in_ref[:, low : low + wide, :].reshape(packs * wide, HEAD_DIM)
        low = HEADS + half * wide
        dq = in_ref[:, low : low + wide, :].reshape(packs * wide, HEAD_DIM)
        back = dot(move_q[...], jnp.concatenate([o, dq], axis=1)).astype(bf16)
        for h in range(HALF):
            at = slice((half * HALF + h) * HEAD_DIM, (half * HALF + h + 1) * HEAD_DIM)
            rows = slice(h * BLOCK, (h + 1) * BLOCK)
            o_ref[:, at] = back[rows, :HEAD_DIM]
            dq_ref[:, at] = back[rows, HEAD_DIM:]
    kv = in_ref[:, 2 * HEADS :, :].reshape(2 * BLOCK, HEAD_DIM)
    pair = dot(move_kv[...], kv).astype(bf16)
    dk_ref[...] = pair[:BLOCK]
    dv_ref[...] = pair[BLOCK:]


def attend_kernel(
    core_ref, row_docs, col_docs, in_ref, far_ref, out_ref, near_grad, far_grad,
    keys, values, keys_t, values_t, dkeys, dvalues,
):
    blocks = row_docs.shape[0]
    units = BLOCK // UNIT // 2
    tall = units * HEADS
    r = lax.broadcasted_iota(jnp.int32, (2 * BLOCK, 2 * BLOCK), 0)
    c = lax.broadcasted_iota(jnp.int32, (2 * BLOCK, 2 * BLOCK), 1)

    def place(x):
        inside = x % BLOCK
        unit = (inside % (BLOCK // 2)) // UNIT
        return (inside // (BLOCK // 2)) * BLOCK + unit * 2 * UNIT + (x // BLOCK) * UNIT + x % UNIT

    apart = (place(r) == c).astype(f32).astype(bf16)
    together = (place(c) == r).astype(f32).astype(bf16)
    core = core_ref[0, 0]
    key = lax.broadcasted_iota(jnp.int32, (BLOCK, tall), 0)
    lane = lax.broadcasted_iota(jnp.int32, (BLOCK, tall), 1)
    owner = jnp.where(key < BLOCK // 2, core, 1 - core)
    key_pos = (2 * ((key % (BLOCK // 2)) // UNIT) + owner) * UNIT + key % UNIT
    row_pos = (2 * (lane // HEADS) + core) * UNIT + lane % UNIT
    earlier = key_pos <= row_pos
    back = (REACH + BLOCK - 2) // BLOCK

    for b in range(blocks):
        here = slice(b * BLOCK, (b + 1) * BLOCK)
        mine = slice(b * units, (b + 1) * units)
        low = max(0, b - back)
        seen = slice(low * BLOCK, (b + 1) * BLOCK)
        count = b + 1 - low
        kv = jnp.concatenate(
            [
                in_ref[mine, 2 * HEADS :, :].reshape(BLOCK, HEAD_DIM),
                far_ref[mine, :, :].reshape(BLOCK, HEAD_DIM),
            ],
            axis=0,
        )
        kv = dot(apart, kv)
        keys[here, :] = kv[:BLOCK].astype(bf16)
        values[here, :] = kv[BLOCK:].astype(bf16)
        keys_t[:, here] = kv[:BLOCK].T.astype(bf16)
        values_t[:, here] = kv[BLOCK:].T.astype(bf16)
        dkeys[here, :] = jnp.zeros((BLOCK, HEAD_DIM), f32)
        dvalues[here, :] = jnp.zeros((BLOCK, HEAD_DIM), f32)

        q = in_ref[mine, 0:HEADS, :].reshape(tall, HEAD_DIM)
        do = in_ref[mine, HEADS : 2 * HEADS, :].reshape(tall, HEAD_DIM)
        do_t = do.astype(f32).T
        docs = row_docs[b : b + 1, :]
        scores = dot_nt(keys[seen, :], q)
        parts = []
        for n in range(count):
            at = slice((low + n) * BLOCK, (low + n + 1) * BLOCK)
            allowed = col_docs[at, 0:1] == docs
            if n == count - 1:
                allowed = allowed & earlier
            parts.append(
                jnp.where(allowed, scores[n * BLOCK : (n + 1) * BLOCK], FAR_BELOW)
            )
        scores = jnp.concatenate(parts, axis=0)
        row_max = jnp.max(scores, axis=0, keepdims=True)
        weights = jnp.exp2((scores - row_max) * (FACTOR * LOG2E))
        inverse = 1.0 / jnp.sum(weights, axis=0, keepdims=True)
        chances = weights * inverse
        rounded = chances.astype(bf16)
        out_t = dot(values_t[:, seen], rounded).astype(bf16).astype(f32)
        row_dot = jnp.sum(out_t * do_t, axis=0, keepdims=True)
        pushes = dot_nt(values[seen, :], do)
        slopes = (chances * (pushes - row_dot)).astype(bf16)
        dq_t = dot(keys_t[:, seen], slopes) * FACTOR
        dkeys[seen, :] += dot(slopes, q)
        dvalues[seen, :] += dot(rounded, do)
        out_ref[mine, 0:HEADS, :] = out_t.T.astype(bf16).reshape(units, HEADS, HEAD_DIM)
        out_ref[mine, HEADS : 2 * HEADS, :] = (
            dq_t.T.astype(bf16).reshape(units, HEADS, HEAD_DIM)
        )

    for b in range(blocks):
        here = slice(b * BLOCK, (b + 1) * BLOCK)
        mine = slice(b * units, (b + 1) * units)
        pair = jnp.concatenate(
            [(dkeys[here, :] * FACTOR).astype(bf16), dvalues[here, :].astype(bf16)], axis=0
        )
        pair = dot(together, pair).astype(bf16)
        near_grad[mine, :, :] = pair[:BLOCK].reshape(units, 2 * UNIT, HEAD_DIM)
        far_grad[mine, :, :] = pair[BLOCK:].reshape(units, 2 * UNIT, HEAD_DIM)


def local(queries, key_states, value_states, out_grad, destinations, documents):
    contexts = lax.axis_size("ctx")
    pairs = lax.axis_size("pair")
    packs = 2 * pairs
    kv_heads = key_states.shape[2] // HEAD_DIM
    wide = GROUP * HEAD_DIM
    swap = [(0, 1), (1, 0)]
    core = lax.axis_index("core")

    moved_shape = jax.ShapeDtypeStruct((kv_heads * packs, ROWS, HEAD_DIM), bf16)
    route_spec = pl.BlockSpec((1, packs), lambda m: (0, 0))
    wide_spec = pl.BlockSpec((None, BLOCK, wide), lambda m: (0, 0, m))
    narrow_spec = pl.BlockSpec((None, BLOCK, HEAD_DIM), lambda m: (0, 0, m))
    moved_spec = pl.BlockSpec((packs, ROWS, HEAD_DIM), lambda m: (m, 0, 0))
    matrices = [
        pltpu.VMEM((HALF * BLOCK, HALF * BLOCK), bf16),
        pltpu.VMEM((2 * BLOCK, 2 * BLOCK), bf16),
    ]
    sending = pl.pallas_call(
        send_kernel,
        grid=(kv_heads,),
        in_specs=[route_spec, wide_spec, narrow_spec, narrow_spec, wide_spec],
        out_specs=moved_spec,
        out_shape=moved_shape,
        scratch_shapes=matrices,
        compiler_params=pltpu.CompilerParams(vmem_limit_bytes=63 * 1024 * 1024),
    )(destinations, queries, key_states, value_states, out_grad)

    received = lax.all_to_all(sending, ("ctx", "pair"), split_axis=0, concat_axis=0, tiled=True)
    far = lax.ppermute(received[:, 2 * HEADS :, :], "core", swap)

    other_documents = lax.ppermute(documents, "core", swap)
    docs = jnp.where(lax.axis_index("ctx") % 2 == core, documents, other_documents)
    docs = docs.reshape(contexts, pairs, 2, UNIT)
    near_docs = jnp.where(core == 0, docs[:, :, 0], docs[:, :, 1])
    far_docs = jnp.where(core == 0, docs[:, :, 1], docs[:, :, 0])
    row_docs = jnp.broadcast_to(
        near_docs[:, :, None, :], (contexts, pairs, GROUP, UNIT)
    ).reshape(contexts, GROUP * BLOCK // 2)
    col_docs = jnp.concatenate(
        [near_docs.reshape(contexts, BLOCK // 2), far_docs.reshape(contexts, BLOCK // 2)], axis=1
    ).reshape(contexts * BLOCK, 1)
    length = contexts * BLOCK
    col_docs = jnp.broadcast_to(col_docs, (length, HEAD_DIM))

    whole = pl.BlockSpec(memory_space=pltpu.VMEM)
    grad_shape = jax.ShapeDtypeStruct((kv_heads * packs, 2 * UNIT, HEAD_DIM), bf16)
    results, near_grad, far_grad = pl.pallas_call(
        attend_kernel,
        in_specs=[pl.BlockSpec(memory_space=pltpu.SMEM)] + [whole] * 4,
        out_specs=[whole] * 3,
        out_shape=[moved_shape, grad_shape, grad_shape],
        scratch_shapes=[
            pltpu.VMEM((length, HEAD_DIM), bf16),
            pltpu.VMEM((length, HEAD_DIM), bf16),
            pltpu.VMEM((HEAD_DIM, length), bf16),
            pltpu.VMEM((HEAD_DIM, length), bf16),
            pltpu.VMEM((length, HEAD_DIM), f32),
            pltpu.VMEM((length, HEAD_DIM), f32),
        ],
        compiler_params=pltpu.CompilerParams(vmem_limit_bytes=40 * 1024 * 1024),
    )(core.astype(jnp.int32).reshape(1, 1), row_docs, col_docs, received, far)

    grads = near_grad.astype(f32) + lax.ppermute(far_grad, "core", swap).astype(f32)
    results = lax.dynamic_update_slice(results, grads.astype(bf16), (0, 2 * HEADS, 0))
    returned = lax.all_to_all(results, ("ctx", "pair"), split_axis=0, concat_axis=0, tiled=True)

    return pl.pallas_call(
        return_kernel,
        grid=(kv_heads,),
        in_specs=[route_spec, moved_spec],
        out_specs=[wide_spec, wide_spec, narrow_spec, narrow_spec],
        out_shape=[
            jax.ShapeDtypeStruct(queries.shape, bf16),
            jax.ShapeDtypeStruct(queries.shape, bf16),
            jax.ShapeDtypeStruct(key_states.shape, bf16),
            jax.ShapeDtypeStruct(key_states.shape, bf16),
        ],
        scratch_shapes=matrices,
        compiler_params=pltpu.CompilerParams(vmem_limit_bytes=40 * 1024 * 1024),
    )(destinations, returned)


def solution(mesh):
    split = jax.sharding.Mesh(
        mesh.devices.reshape(-1, 2, mesh.shape["ctx"]), ("pair", "core", "ctx")
    )
    spec = P(("pair", "core"), "ctx", None)
    return jax.shard_map(
        local,
        mesh=split,
        in_specs=(spec, spec, spec, spec, P(("pair", "core"), "ctx"), P(("pair", "core"), None)),
        out_specs=(spec, spec, spec, spec),
        check_vma=False,
    )
```

```python
import jax
import jax.numpy as jnp
from jax import lax
from jax.experimental import pallas as pl
from jax.experimental.pallas import tpu as pltpu
from jax.sharding import PartitionSpec as P

HEAD_DIM = 128
GROUP = 8
HALF = 4
UNIT = 4
BLOCK = 128
REACH = 512
HEADS = GROUP * UNIT
ROWS = 2 * HEADS + 2 * UNIT
FAR_BELOW = -1e30
FACTOR = HEAD_DIM**-0.5
LOG2E = 1.4426950408889634

f32 = jnp.float32
bf16 = jnp.bfloat16


def dot(a, b):
    return jnp.dot(a, b, preferred_element_type=f32)


def dot_nt(a, b):
    return lax.dot_general(a, b, (((1,), (1,)), ((), ())), preferred_element_type=f32)


def sending_matrix(slots, heads):
    units = BLOCK // UNIT
    size = heads * BLOCK
    unit = lax.broadcasted_iota(jnp.int32, (units, size), 0)
    col = lax.broadcasted_iota(jnp.int32, (units, size), 1)
    spread = ((col % BLOCK) // UNIT == unit).astype(f32).astype(bf16)
    packs = jnp.broadcast_to(slots.astype(f32), (8, units)).astype(bf16)
    where = dot(packs, spread)
    col = lax.broadcasted_iota(jnp.int32, (8, size), 1)
    inner = (col // BLOCK) * UNIT + col % UNIT
    place = where * (heads * UNIT) + inner.astype(f32)
    rows = lax.broadcasted_iota(jnp.int32, (size, size), 0).astype(f32)
    return (place[0:1] == rows).astype(f32).astype(bf16)


def returning_matrix(slots, heads):
    units = BLOCK // UNIT
    size = heads * BLOCK
    row = lax.broadcasted_iota(jnp.int32, (size, units), 0)
    unit = lax.broadcasted_iota(jnp.int32, (size, units), 1)
    packs = jnp.broadcast_to(slots.astype(f32), (size, units))
    where = jnp.sum(
        jnp.where((row % BLOCK) // UNIT == unit, packs, 0.0), axis=1, keepdims=True
    )
    row = lax.broadcasted_iota(jnp.int32, (size, 1), 0)
    inner = (row // BLOCK) * UNIT + row % UNIT
    place = where * (heads * UNIT) + inner.astype(f32)
    cols = lax.broadcasted_iota(jnp.int32, (size, size), 1).astype(f32)
    return (place == cols).astype(f32).astype(bf16)


def slots_of(route):
    return (route % 2) * (BLOCK // UNIT // 2) + route // 2


def send_kernel(
    route_ref, q_hbm, k_hbm, v_hbm, do_hbm, out_hbm,
    q_buf, k_buf, v_buf, do_buf, out_buf, in_sems, out_sems,
):
    packs = BLOCK // UNIT
    kv_heads = k_buf.shape[1] // HEAD_DIM
    group = GROUP * HEAD_DIM
    cut = 2
    share = kv_heads // cut
    loads = []
    for n in range(cut):
        at = pl.ds(n * share * group, share * group)
        pair = [
            pltpu.make_async_copy(q_hbm.at[0, :, at], q_buf.at[:, at], in_sems.at[2 * n]),
            pltpu.make_async_copy(do_hbm.at[0, :, at], do_buf.at[:, at], in_sems.at[2 * n + 1]),
        ]
        if n == 0:
            pair += [
                pltpu.make_async_copy(k_hbm.at[0], k_buf, in_sems.at[2 * cut]),
                pltpu.make_async_copy(v_hbm.at[0], v_buf, in_sems.at[2 * cut + 1]),
            ]
        for copy in pair:
            copy.start()
        loads.append(pair)
    slots = slots_of(route_ref[...])
    move_q = sending_matrix(slots, HALF)
    move_kv = sending_matrix(slots, 2)
    wide = HALF * UNIT
    stores = []
    for m in range(kv_heads):
        if m % share == 0:
            for copy in loads[m // share]:
                copy.wait()
        out = out_buf.at[pl.ds(m * packs, packs)]
        for half in range(2):
            first = m * group + half * HALF * HEAD_DIM
            heads = [slice(first + h * HEAD_DIM, first + (h + 1) * HEAD_DIM) for h in range(HALF)]
            both = jnp.concatenate(
                [
                    jnp.concatenate([q_buf[:, at] for at in heads], axis=0),
                    jnp.concatenate([do_buf[:, at] for at in heads], axis=0),
                ],
                axis=1,
            )
            moved = dot(move_q, both).astype(bf16)
            low = half * wide
            out[:, low : low + wide, :] = moved[:, :HEAD_DIM].reshape(packs, wide, HEAD_DIM)
            low = HEADS + half * wide
            out[:, low : low + wide, :] = moved[:, HEAD_DIM:].reshape(packs, wide, HEAD_DIM)
        at = slice(m * HEAD_DIM, (m + 1) * HEAD_DIM)
        pair = jnp.concatenate([k_buf[:, at], v_buf[:, at]], axis=0)
        out[:, 2 * HEADS :, :] = (
            dot(move_kv, pair).astype(bf16).reshape(packs, 2 * UNIT, HEAD_DIM)
        )
        store = pltpu.make_async_copy(out, out_hbm.at[pl.ds(m * packs, packs)], out_sems.at[m])
        store.start()
        stores.append(store)
    for store in stores:
        store.wait()


def return_kernel(
    move_q, move_kv, in_ref, o_hbm, dq_hbm, dk_hbm, dv_hbm, o_buf, dq_buf, dk_buf, dv_buf, sems
):
    packs = BLOCK // UNIT
    wide = HALF * UNIT
    kv_heads = dk_buf.shape[1] // HEAD_DIM
    stores = []

    def store(buf, hbm, at):
        copy = pltpu.make_async_copy(buf.at[:, at], hbm.at[0, :, at], sems.at[len(stores)])
        copy.start()
        stores.append(copy)

    for m in range(kv_heads):
        block = in_ref.at[pl.ds(m * packs, packs)]
        kv = block[:, 2 * HEADS :, :].reshape(2 * BLOCK, HEAD_DIM)
        pair = dot(move_kv[...], kv).astype(bf16)
        at = slice(m * HEAD_DIM, (m + 1) * HEAD_DIM)
        dk_buf[:, at] = pair[:BLOCK]
        dv_buf[:, at] = pair[BLOCK:]
        if m == kv_heads - 1:
            every = pl.ds(0, dk_buf.shape[1])
            store(dk_buf, dk_hbm, every)
            store(dv_buf, dv_hbm, every)
        for half in range(2):
            low = half * wide
            o = block[:, low : low + wide, :].reshape(packs * wide, HEAD_DIM)
            low = HEADS + half * wide
            dq = block[:, low : low + wide, :].reshape(packs * wide, HEAD_DIM)
            back = dot(move_q[...], jnp.concatenate([o, dq], axis=1)).astype(bf16)
            first = (m * GROUP + half * HALF) * HEAD_DIM
            for h in range(HALF):
                at = slice(first + h * HEAD_DIM, first + (h + 1) * HEAD_DIM)
                rows = slice(h * BLOCK, (h + 1) * BLOCK)
                o_buf[:, at] = back[rows, :HEAD_DIM]
                dq_buf[:, at] = back[rows, HEAD_DIM:]
        at = pl.ds(m * GROUP * HEAD_DIM, GROUP * HEAD_DIM)
        store(o_buf, o_hbm, at)
        store(dq_buf, dq_hbm, at)
    for copy in stores:
        copy.wait()


def prepare_kernel(
    flags, route_ref, docs_ref, other_ref,
    row_docs, col_docs, row_pos, key_pos, apart, together, move_q, move_kv,
):
    slots = slots_of(route_ref[...])
    move_q[...] = returning_matrix(slots, HALF)
    move_kv[...] = returning_matrix(slots, 2)
    r = lax.broadcasted_iota(jnp.int32, (2 * BLOCK, 2 * BLOCK), 0)
    c = lax.broadcasted_iota(jnp.int32, (2 * BLOCK, 2 * BLOCK), 1)

    def place(x):
        inside = x % BLOCK
        unit = (inside % (BLOCK // 2)) // UNIT
        return (inside // (BLOCK // 2)) * BLOCK + unit * 2 * UNIT + (x // BLOCK) * UNIT + x % UNIT

    apart[...] = (place(r) == c).astype(f32).astype(bf16)
    together[...] = (place(c) == r).astype(f32).astype(bf16)
    core = flags[0, 0]
    half = BLOCK // 2

    def key_at(x):
        owner = jnp.where(x < half, core, 1 - core)
        return (2 * ((x % half) // UNIT) + owner) * UNIT + x % UNIT

    def row_at(x):
        return (2 * (x // HEADS) + core) * UNIT + x % UNIT

    key_pos[...] = key_at(lax.broadcasted_iota(jnp.int32, key_pos.shape, 0)).astype(f32)
    row_pos[...] = row_at(lax.broadcasted_iota(jnp.int32, row_pos.shape, 1)).astype(f32)
    docs = jnp.where(flags[0, 1] == 1, docs_ref[...], other_ref[...])
    high = (docs // 32).astype(f32).astype(bf16)
    low = (docs % 32).astype(f32).astype(bf16)
    tall = row_docs.shape[1]
    pos = lax.broadcasted_iota(jnp.int32, (BLOCK, tall), 0)
    to_row = (row_at(lax.broadcasted_iota(jnp.int32, (BLOCK, tall), 1)) == pos).astype(f32).astype(bf16)
    row_docs[...] = dot(high, to_row) * 32 + dot(low, to_row)
    pos = lax.broadcasted_iota(jnp.int32, (BLOCK, BLOCK), 1)
    to_key = (key_at(lax.broadcasted_iota(jnp.int32, (BLOCK, BLOCK), 0)) == pos).astype(f32).astype(bf16)
    for b in range(docs.shape[0]):
        wide_high = jnp.broadcast_to(high[b : b + 1, :], (BLOCK, BLOCK))
        wide_low = jnp.broadcast_to(low[b : b + 1, :], (BLOCK, BLOCK))
        col_docs[b * BLOCK : (b + 1) * BLOCK, :] = (
            dot_nt(to_key, wide_high) * 32 + dot_nt(to_key, wide_low)
        )


def attend_kernel(
    row_docs, col_docs, row_pos, key_pos, apart, together, in_ref, far_ref,
    out_ref, near_grad, far_grad,
    keys, values, keys_t, values_t, dkeys, dvalues, held, pushed, rounded, slopes,
):
    blocks = row_docs.shape[0]
    units = BLOCK // UNIT // 2
    tall = units * HEADS
    back = (REACH + BLOCK - 2) // BLOCK
    at = [slice(b * BLOCK, (b + 1) * BLOCK) for b in range(blocks)]
    mine = [slice(b * units, (b + 1) * units) for b in range(blocks)]
    across = lax.broadcasted_iota(jnp.int32, (BLOCK, BLOCK), 1)
    eye = (lax.broadcasted_iota(jnp.int32, (BLOCK, BLOCK), 0) == across).astype(f32).astype(bf16)

    for b in range(blocks):
        kv = jnp.concatenate(
            [
                in_ref[mine[b], 2 * HEADS :, :].reshape(BLOCK, HEAD_DIM),
                far_ref[mine[b], :, :].reshape(BLOCK, HEAD_DIM),
            ],
            axis=0,
        )
        kv = dot(apart[...], kv)
        keys[at[b], :] = kv[:BLOCK].astype(bf16)
        values[at[b], :] = kv[BLOCK:].astype(bf16)
        keys_t[:, at[b]] = dot_nt(eye, keys[at[b], :]).astype(bf16)
        values_t[:, at[b]] = dot_nt(eye, values[at[b], :]).astype(bf16)
    dkeys[...] = jnp.zeros_like(dkeys)
    dvalues[...] = jnp.zeros_like(dvalues)

    for b in range(blocks):
        low = max(0, b - back)
        seen = slice(low * BLOCK, (b + 1) * BLOCK)
        count = b + 1 - low
        slot = b % 2
        q = in_ref[mine[b], 0:HEADS, :].reshape(tall, HEAD_DIM)
        do = in_ref[mine[b], HEADS : 2 * HEADS, :].reshape(tall, HEAD_DIM)
        docs = row_docs[b : b + 1, :]
        row_max = jnp.full((8, tall), FAR_BELOW, f32)
        for n in range(count):
            scores = dot_nt(keys[at[low + n], :], q)
            allowed = col_docs[at[low + n], 0:1] == docs
            if n == count - 1:
                allowed = allowed & (key_pos[:, 0:1] <= row_pos[0:1, :])
            scores = jnp.where(allowed, scores, FAR_BELOW)
            held[slot, at[n], :] = scores
            row_max = jnp.maximum(row_max, jnp.max(scores.reshape(BLOCK // 8, 8, tall), axis=0))
        row_max = jnp.max(row_max, axis=0, keepdims=True)
        weight_sum = jnp.zeros((8, tall), f32)
        for n in range(count):
            weights = jnp.exp2((held[slot, at[n], :] - row_max) * (FACTOR * LOG2E))
            held[slot, at[n], :] = weights
            weight_sum = weight_sum + jnp.sum(weights.reshape(BLOCK // 8, 8, tall), axis=0)
        inverse = 1.0 / jnp.sum(weight_sum, axis=0, keepdims=True)
        row_dot = jnp.zeros((8, tall), f32)
        for n in range(count):
            pushes = dot_nt(values[at[low + n], :], do)
            pushed[slot, at[n], :] = pushes
            chances = held[slot, at[n], :] * inverse
            rounded[slot, at[n], :] = chances.astype(bf16)
            row_dot = row_dot + jnp.sum((chances * pushes).reshape(BLOCK // 8, 8, tall), axis=0)
        row_dot = jnp.sum(row_dot, axis=0, keepdims=True)
        chances = rounded.at[slot, pl.ds(0, count * BLOCK), :]
        out_t = dot(values_t[:, seen], chances[...]).astype(bf16)
        for n in range(count):
            slopes[slot, at[n], :] = (
                (held[slot, at[n], :] * inverse) * (pushed[slot, at[n], :] - row_dot)
            ).astype(bf16)
        slope = slopes.at[slot, pl.ds(0, count * BLOCK), :]
        dq_t = (dot(keys_t[:, seen], slope[...]) * FACTOR).astype(bf16)
        dkeys[seen, :] += dot(slope[...], q)
        dvalues[seen, :] += dot(chances[...], do)
        out_ref[mine[b], 0:HEADS, :] = out_t.T.reshape(units, HEADS, HEAD_DIM)
        out_ref[mine[b], HEADS : 2 * HEADS, :] = (
            dq_t.T.reshape(units, HEADS, HEAD_DIM)
        )

    for b in range(blocks):
        pair = jnp.concatenate(
            [(dkeys[at[b], :] * FACTOR).astype(bf16), dvalues[at[b], :].astype(bf16)], axis=0
        )
        pair = dot(together[...], pair).astype(bf16)
        near_grad[mine[b], :, :] = pair[:BLOCK].reshape(units, 2 * UNIT, HEAD_DIM)
        far_grad[mine[b], :, :] = pair[BLOCK:].reshape(units, 2 * UNIT, HEAD_DIM)


def local(queries, key_states, value_states, out_grad, destinations, documents):
    contexts = lax.axis_size("ctx")
    pairs = lax.axis_size("pair")
    packs = 2 * pairs
    kv_heads = key_states.shape[2] // HEAD_DIM
    swap = [(0, 1), (1, 0)]
    core = lax.axis_index("core")

    shape = jax.ShapeDtypeStruct
    whole = pl.BlockSpec(memory_space=pltpu.VMEM)
    away = pl.BlockSpec(memory_space=pl.ANY)
    scalars = pl.BlockSpec(memory_space=pltpu.SMEM)
    small = pltpu.CompilerParams(vmem_limit_bytes=40 * 1024 * 1024)
    moved_shape = shape((kv_heads * packs, ROWS, HEAD_DIM), bf16)
    sending = pl.pallas_call(
        send_kernel,
        in_specs=[whole] + [away] * 4,
        out_specs=away,
        out_shape=moved_shape,
        scratch_shapes=[
            pltpu.VMEM(queries.shape[1:], bf16),
            pltpu.VMEM(key_states.shape[1:], bf16),
            pltpu.VMEM(key_states.shape[1:], bf16),
            pltpu.VMEM(queries.shape[1:], bf16),
            pltpu.VMEM(moved_shape.shape, bf16),
            pltpu.SemaphoreType.DMA((2 * kv_heads + 2,)),
            pltpu.SemaphoreType.DMA((kv_heads,)),
        ],
        compiler_params=pltpu.CompilerParams(vmem_limit_bytes=63 * 1024 * 1024),
    )(destinations, queries, key_states, value_states, out_grad)

    received = lax.all_to_all(sending, ("ctx", "pair"), split_axis=0, concat_axis=0, tiled=True)

    other_documents = lax.ppermute(documents, "core", swap)
    length = contexts * BLOCK
    tall = GROUP * BLOCK // 2
    flags = jnp.stack([core, (lax.axis_index("ctx") % 2 == core).astype(core.dtype)])
    square = shape((2 * BLOCK, 2 * BLOCK), bf16)
    *prepared, move_q, move_kv = pl.pallas_call(
        prepare_kernel,
        in_specs=[scalars, whole, whole, whole],
        out_specs=[whole] * 8,
        out_shape=[
            shape((contexts, tall), f32),
            shape((length, HEAD_DIM), f32),
            shape((8, tall), f32),
            shape((BLOCK, HEAD_DIM), f32),
            square,
            square,
            shape((HALF * BLOCK, HALF * BLOCK), bf16),
            square,
        ],
        compiler_params=small,
    )(
        flags.astype(jnp.int32).reshape(1, 2),
        destinations,
        documents.reshape(contexts, BLOCK),
        other_documents.reshape(contexts, BLOCK),
    )

    near, *prepared = lax.optimization_barrier((received[:, 2 * HEADS :, :], *prepared))
    far = lax.ppermute(near, "core", swap)
    grad_shape = shape((kv_heads * packs, 2 * UNIT, HEAD_DIM), bf16)
    window = min(contexts, (REACH + BLOCK - 2) // BLOCK + 1) * BLOCK
    results, near_grad, far_grad = pl.pallas_call(
        attend_kernel,
        in_specs=[whole] * 8,
        out_specs=[whole] * 3,
        out_shape=[moved_shape, grad_shape, grad_shape],
        scratch_shapes=[
            pltpu.VMEM((length, HEAD_DIM), bf16),
            pltpu.VMEM((length, HEAD_DIM), bf16),
            pltpu.VMEM((HEAD_DIM, length), bf16),
            pltpu.VMEM((HEAD_DIM, length), bf16),
            pltpu.VMEM((length, HEAD_DIM), f32),
            pltpu.VMEM((length, HEAD_DIM), f32),
            pltpu.VMEM((2, window, tall), f32),
            pltpu.VMEM((2, window, tall), f32),
            pltpu.VMEM((2, window, tall), bf16),
            pltpu.VMEM((2, window, tall), bf16),
        ],
        compiler_params=small,
    )(*prepared, received, far)

    grads = near_grad.astype(f32) + lax.ppermute(far_grad, "core", swap).astype(f32)
    results = lax.dynamic_update_slice(results, grads.astype(bf16), (0, 2 * HEADS, 0))
    returned = lax.all_to_all(results, ("ctx", "pair"), split_axis=0, concat_axis=0, tiled=True)

    outs = (queries, queries, key_states, value_states)
    return pl.pallas_call(
        return_kernel,
        in_specs=[whole] * 3,
        out_specs=[away] * 4,
        out_shape=[shape(out.shape, bf16) for out in outs],
        scratch_shapes=[pltpu.VMEM(out.shape[1:], bf16) for out in outs]
        + [pltpu.SemaphoreType.DMA((4 * kv_heads + 2,))],
        compiler_params=small,
    )(move_q, move_kv, returned)


def solution(mesh):
    split = jax.sharding.Mesh(
        mesh.devices.reshape(-1, 2, mesh.shape["ctx"]), ("pair", "core", "ctx")
    )
    spec = P(("pair", "core"), "ctx", None)
    return jax.shard_map(
        local,
        mesh=split,
        in_specs=(spec, spec, spec, spec, P(("pair", "core"), "ctx"), P(("pair", "core"), None)),
        out_specs=(spec, spec, spec, spec),
        check_vma=False,
    )
```

```python
import jax
import jax.numpy as jnp
from jax import lax
from jax.experimental import pallas as pl
from jax.experimental.pallas import tpu as pltpu
from jax.sharding import PartitionSpec as P

HEAD_DIM = 128
GROUP = 8
HALF = 4
UNIT = 4
BLOCK = 128
REACH = 512
HEADS = GROUP * UNIT
ROWS = 2 * HEADS + 2 * UNIT
FAR_BELOW = -1e30
FACTOR = HEAD_DIM**-0.5
LOG2E = 1.4426950408889634

f32 = jnp.float32
bf16 = jnp.bfloat16


def dot(a, b):
    return jnp.dot(a, b, preferred_element_type=f32)


def dot_nt(a, b):
    return lax.dot_general(a, b, (((1,), (1,)), ((), ())), preferred_element_type=f32)


def sending_matrix(slots, heads):
    units = BLOCK // UNIT
    size = heads * BLOCK
    unit = lax.broadcasted_iota(jnp.int32, (units, size), 0)
    col = lax.broadcasted_iota(jnp.int32, (units, size), 1)
    spread = ((col % BLOCK) // UNIT == unit).astype(f32).astype(bf16)
    packs = jnp.broadcast_to(slots.astype(f32), (8, units)).astype(bf16)
    where = dot(packs, spread)
    col = lax.broadcasted_iota(jnp.int32, (8, size), 1)
    inner = (col // BLOCK) * UNIT + col % UNIT
    place = where * (heads * UNIT) + inner.astype(f32)
    rows = lax.broadcasted_iota(jnp.int32, (size, size), 0).astype(f32)
    return (place[0:1] == rows).astype(f32).astype(bf16)


def returning_matrix(slots, heads):
    units = BLOCK // UNIT
    size = heads * BLOCK
    row = lax.broadcasted_iota(jnp.int32, (size, units), 0)
    unit = lax.broadcasted_iota(jnp.int32, (size, units), 1)
    packs = jnp.broadcast_to(slots.astype(f32), (size, units))
    where = jnp.sum(
        jnp.where((row % BLOCK) // UNIT == unit, packs, 0.0), axis=1, keepdims=True
    )
    row = lax.broadcasted_iota(jnp.int32, (size, 1), 0)
    inner = (row // BLOCK) * UNIT + row % UNIT
    place = where * (heads * UNIT) + inner.astype(f32)
    cols = lax.broadcasted_iota(jnp.int32, (size, size), 1).astype(f32)
    return (place == cols).astype(f32).astype(bf16)


def slots_of(route):
    return (route % 2) * (BLOCK // UNIT // 2) + route // 2


def send_kernel(
    route_ref, q_hbm, k_hbm, v_hbm, do_hbm, out_hbm,
    q_buf, k_buf, v_buf, do_buf, out_buf, in_sems, out_sems,
):
    packs = BLOCK // UNIT
    kv_heads = k_buf.shape[1] // HEAD_DIM
    group = GROUP * HEAD_DIM
    cut = 2
    share = kv_heads // cut
    loads = []
    for n in range(cut):
        at = pl.ds(n * share * group, share * group)
        pair = [
            pltpu.make_async_copy(q_hbm.at[0, :, at], q_buf.at[:, at], in_sems.at[2 * n]),
            pltpu.make_async_copy(do_hbm.at[0, :, at], do_buf.at[:, at], in_sems.at[2 * n + 1]),
        ]
        if n == 0:
            pair += [
                pltpu.make_async_copy(k_hbm.at[0], k_buf, in_sems.at[2 * cut]),
                pltpu.make_async_copy(v_hbm.at[0], v_buf, in_sems.at[2 * cut + 1]),
            ]
        for copy in pair:
            copy.start()
        loads.append(pair)
    slots = slots_of(route_ref[...])
    move_q = sending_matrix(slots, HALF)
    move_kv = sending_matrix(slots, 2)
    wide = HALF * UNIT
    stores = []
    for m in range(kv_heads):
        if m % share == 0:
            for copy in loads[m // share]:
                copy.wait()
        out = out_buf.at[pl.ds(m * packs, packs)]
        for half in range(2):
            first = m * group + half * HALF * HEAD_DIM
            heads = [slice(first + h * HEAD_DIM, first + (h + 1) * HEAD_DIM) for h in range(HALF)]
            both = jnp.concatenate(
                [
                    jnp.concatenate([q_buf[:, at] for at in heads], axis=0),
                    jnp.concatenate([do_buf[:, at] for at in heads], axis=0),
                ],
                axis=1,
            )
            moved = dot(move_q, both).astype(bf16)
            low = half * wide
            out[:, low : low + wide, :] = moved[:, :HEAD_DIM].reshape(packs, wide, HEAD_DIM)
            low = HEADS + half * wide
            out[:, low : low + wide, :] = moved[:, HEAD_DIM:].reshape(packs, wide, HEAD_DIM)
        at = slice(m * HEAD_DIM, (m + 1) * HEAD_DIM)
        pair = jnp.concatenate([k_buf[:, at], v_buf[:, at]], axis=0)
        out[:, 2 * HEADS :, :] = (
            dot(move_kv, pair).astype(bf16).reshape(packs, 2 * UNIT, HEAD_DIM)
        )
        store = pltpu.make_async_copy(out, out_hbm.at[pl.ds(m * packs, packs)], out_sems.at[m])
        store.start()
        stores.append(store)
    for store in stores:
        store.wait()


def return_kernel(
    move_q, move_kv, in_ref, o_hbm, dq_hbm, dk_hbm, dv_hbm, o_buf, dq_buf, dk_buf, dv_buf, sems
):
    packs = BLOCK // UNIT
    wide = HALF * UNIT
    kv_heads = dk_buf.shape[1] // HEAD_DIM
    stores = []

    def store(buf, hbm, at):
        copy = pltpu.make_async_copy(buf.at[:, at], hbm.at[0, :, at], sems.at[len(stores)])
        copy.start()
        stores.append(copy)

    for m in range(kv_heads):
        block = in_ref.at[pl.ds(m * packs, packs)]
        kv = block[:, 2 * HEADS :, :].reshape(2 * BLOCK, HEAD_DIM)
        pair = dot(move_kv[...], kv).astype(bf16)
        at = slice(m * HEAD_DIM, (m + 1) * HEAD_DIM)
        dk_buf[:, at] = pair[:BLOCK]
        dv_buf[:, at] = pair[BLOCK:]
        if m == kv_heads - 1:
            every = pl.ds(0, dk_buf.shape[1])
            store(dk_buf, dk_hbm, every)
            store(dv_buf, dv_hbm, every)
        for half in range(2):
            low = half * wide
            o = block[:, low : low + wide, :].reshape(packs * wide, HEAD_DIM)
            low = HEADS + half * wide
            dq = block[:, low : low + wide, :].reshape(packs * wide, HEAD_DIM)
            back = dot(move_q[...], jnp.concatenate([o, dq], axis=1)).astype(bf16)
            first = (m * GROUP + half * HALF) * HEAD_DIM
            for h in range(HALF):
                at = slice(first + h * HEAD_DIM, first + (h + 1) * HEAD_DIM)
                rows = slice(h * BLOCK, (h + 1) * BLOCK)
                o_buf[:, at] = back[rows, :HEAD_DIM]
                dq_buf[:, at] = back[rows, HEAD_DIM:]
        at = pl.ds(m * GROUP * HEAD_DIM, GROUP * HEAD_DIM)
        store(o_buf, o_hbm, at)
        store(dq_buf, dq_hbm, at)
    for copy in stores:
        copy.wait()


def prepare_kernel(
    flags, route_ref, docs_ref, other_ref, near_hbm,
    row_docs, col_docs, row_pos, key_pos, apart, together, move_q, move_kv,
):
    slots = slots_of(route_ref[...])
    move_q[...] = returning_matrix(slots, HALF)
    move_kv[...] = returning_matrix(slots, 2)
    r = lax.broadcasted_iota(jnp.int32, (2 * BLOCK, 2 * BLOCK), 0)
    c = lax.broadcasted_iota(jnp.int32, (2 * BLOCK, 2 * BLOCK), 1)

    def place(x):
        inside = x % BLOCK
        unit = (inside % (BLOCK // 2)) // UNIT
        return (inside // (BLOCK // 2)) * BLOCK + unit * 2 * UNIT + (x // BLOCK) * UNIT + x % UNIT

    apart[...] = (place(r) == c).astype(f32).astype(bf16)
    together[...] = (place(c) == r).astype(f32).astype(bf16)
    core = flags[0, 0]
    half = BLOCK // 2

    def key_at(x):
        owner = jnp.where(x < half, core, 1 - core)
        return (2 * ((x % half) // UNIT) + owner) * UNIT + x % UNIT

    def row_at(x):
        return (2 * (x // HEADS) + core) * UNIT + x % UNIT

    key_pos[...] = key_at(lax.broadcasted_iota(jnp.int32, key_pos.shape, 0)).astype(f32)
    row_pos[...] = row_at(lax.broadcasted_iota(jnp.int32, row_pos.shape, 1)).astype(f32)
    docs = jnp.where(flags[0, 1] == 1, docs_ref[...], other_ref[...])
    high = (docs // 32).astype(f32).astype(bf16)
    low = (docs % 32).astype(f32).astype(bf16)
    tall = row_docs.shape[1]
    pos = lax.broadcasted_iota(jnp.int32, (BLOCK, tall), 0)
    to_row = (row_at(lax.broadcasted_iota(jnp.int32, (BLOCK, tall), 1)) == pos).astype(f32).astype(bf16)
    row_docs[...] = dot(high, to_row) * 32 + dot(low, to_row)
    pos = lax.broadcasted_iota(jnp.int32, (BLOCK, BLOCK), 1)
    to_key = (key_at(lax.broadcasted_iota(jnp.int32, (BLOCK, BLOCK), 0)) == pos).astype(f32).astype(bf16)
    for b in range(docs.shape[0]):
        wide_high = jnp.broadcast_to(high[b : b + 1, :], (BLOCK, BLOCK))
        wide_low = jnp.broadcast_to(low[b : b + 1, :], (BLOCK, BLOCK))
        col_docs[b * BLOCK : (b + 1) * BLOCK, :] = (
            dot_nt(to_key, wide_high) * 32 + dot_nt(to_key, wide_low)
        )


def attend_kernel(
    row_docs, col_docs, row_pos, key_pos, apart, together, in_ref, far_ref,
    out_ref, near_grad, far_grad,
    keys, values, keys_t, values_t, dkeys, dvalues, held, pushed, rounded, slopes,
):
    blocks = row_docs.shape[0]
    units = BLOCK // UNIT // 2
    tall = units * HEADS
    back = (REACH + BLOCK - 2) // BLOCK
    at = [slice(b * BLOCK, (b + 1) * BLOCK) for b in range(blocks)]
    mine = [slice(b * units, (b + 1) * units) for b in range(blocks)]
    across = lax.broadcasted_iota(jnp.int32, (BLOCK, BLOCK), 1)
    eye = (lax.broadcasted_iota(jnp.int32, (BLOCK, BLOCK), 0) == across).astype(f32).astype(bf16)

    for b in range(blocks):
        kv = jnp.concatenate(
            [
                in_ref[mine[b], 2 * HEADS :, :].reshape(BLOCK, HEAD_DIM),
                far_ref[mine[b], :, :].reshape(BLOCK, HEAD_DIM),
            ],
            axis=0,
        )
        kv = dot(apart[...], kv)
        keys[at[b], :] = kv[:BLOCK].astype(bf16)
        values[at[b], :] = kv[BLOCK:].astype(bf16)
        keys_t[:, at[b]] = dot_nt(eye, keys[at[b], :]).astype(bf16)
        values_t[:, at[b]] = dot_nt(eye, values[at[b], :]).astype(bf16)
    dkeys[...] = jnp.zeros_like(dkeys)
    dvalues[...] = jnp.zeros_like(dvalues)

    for b in range(blocks):
        low = max(0, b - back)
        seen = slice(low * BLOCK, (b + 1) * BLOCK)
        count = b + 1 - low
        slot = b % 2
        q = in_ref[mine[b], 0:HEADS, :].reshape(tall, HEAD_DIM)
        do = in_ref[mine[b], HEADS : 2 * HEADS, :].reshape(tall, HEAD_DIM)
        docs = row_docs[b : b + 1, :]
        row_max = jnp.full((8, tall), FAR_BELOW, f32)
        for n in range(count):
            scores = dot_nt(keys[at[low + n], :], q)
            allowed = col_docs[at[low + n], 0:1] == docs
            if n == count - 1:
                allowed = allowed & (key_pos[:, 0:1] <= row_pos[0:1, :])
            scores = jnp.where(allowed, scores, FAR_BELOW)
            held[slot, at[n], :] = scores
            row_max = jnp.maximum(row_max, jnp.max(scores.reshape(BLOCK // 8, 8, tall), axis=0))
        row_max = jnp.max(row_max, axis=0, keepdims=True)
        weight_sum = jnp.zeros((8, tall), f32)
        for n in range(count):
            weights = jnp.exp2((held[slot, at[n], :] - row_max) * (FACTOR * LOG2E))
            held[slot, at[n], :] = weights
            weight_sum = weight_sum + jnp.sum(weights.reshape(BLOCK // 8, 8, tall), axis=0)
        inverse = 1.0 / jnp.sum(weight_sum, axis=0, keepdims=True)
        row_dot = jnp.zeros((8, tall), f32)
        for n in range(count):
            pushes = dot_nt(values[at[low + n], :], do)
            pushed[slot, at[n], :] = pushes
            chances = held[slot, at[n], :] * inverse
            rounded[slot, at[n], :] = chances.astype(bf16)
            row_dot = row_dot + jnp.sum((chances * pushes).reshape(BLOCK // 8, 8, tall), axis=0)
        row_dot = jnp.sum(row_dot, axis=0, keepdims=True)
        chances = rounded.at[slot, pl.ds(0, count * BLOCK), :]
        out_t = dot(values_t[:, seen], chances[...]).astype(bf16)
        for n in range(count):
            slopes[slot, at[n], :] = (
                (held[slot, at[n], :] * inverse) * (pushed[slot, at[n], :] - row_dot)
            ).astype(bf16)
        slope = slopes.at[slot, pl.ds(0, count * BLOCK), :]
        dq_t = (dot(keys_t[:, seen], slope[...]) * FACTOR).astype(bf16)
        dkeys[seen, :] += dot(slope[...], q)
        dvalues[seen, :] += dot(chances[...], do)
        out_ref[mine[b], 0:HEADS, :] = out_t.T.reshape(units, HEADS, HEAD_DIM)
        out_ref[mine[b], HEADS : 2 * HEADS, :] = (
            dq_t.T.reshape(units, HEADS, HEAD_DIM)
        )

    for b in range(blocks):
        pair = jnp.concatenate(
            [(dkeys[at[b], :] * FACTOR).astype(bf16), dvalues[at[b], :].astype(bf16)], axis=0
        )
        pair = dot(together[...], pair).astype(bf16)
        near_grad[mine[b], :, :] = pair[:BLOCK].reshape(units, 2 * UNIT, HEAD_DIM)
        far_grad[mine[b], :, :] = pair[BLOCK:].reshape(units, 2 * UNIT, HEAD_DIM)


def local(queries, key_states, value_states, out_grad, destinations, documents):
    contexts = lax.axis_size("ctx")
    pairs = lax.axis_size("pair")
    packs = 2 * pairs
    kv_heads = key_states.shape[2] // HEAD_DIM
    swap = [(0, 1), (1, 0)]
    core = lax.axis_index("core")

    shape = jax.ShapeDtypeStruct
    whole = pl.BlockSpec(memory_space=pltpu.VMEM)
    away = pl.BlockSpec(memory_space=pl.ANY)
    scalars = pl.BlockSpec(memory_space=pltpu.SMEM)
    small = pltpu.CompilerParams(vmem_limit_bytes=40 * 1024 * 1024)
    moved_shape = shape((kv_heads * packs, ROWS, HEAD_DIM), bf16)
    sending = pl.pallas_call(
        send_kernel,
        in_specs=[whole] + [away] * 4,
        out_specs=away,
        out_shape=moved_shape,
        scratch_shapes=[
            pltpu.VMEM(queries.shape[1:], bf16),
            pltpu.VMEM(key_states.shape[1:], bf16),
            pltpu.VMEM(key_states.shape[1:], bf16),
            pltpu.VMEM(queries.shape[1:], bf16),
            pltpu.VMEM(moved_shape.shape, bf16),
            pltpu.SemaphoreType.DMA((2 * kv_heads + 2,)),
            pltpu.SemaphoreType.DMA((kv_heads,)),
        ],
        compiler_params=pltpu.CompilerParams(vmem_limit_bytes=63 * 1024 * 1024),
    )(destinations, queries, key_states, value_states, out_grad)

    received = lax.all_to_all(sending, ("ctx", "pair"), split_axis=0, concat_axis=0, tiled=True)
    near = received[:, 2 * HEADS :, :]
    far = lax.ppermute(near, "core", swap)

    other_documents = lax.ppermute(documents, "core", swap)
    length = contexts * BLOCK
    tall = GROUP * BLOCK // 2
    flags = jnp.stack([core, (lax.axis_index("ctx") % 2 == core).astype(core.dtype)])
    square = shape((2 * BLOCK, 2 * BLOCK), bf16)
    *prepared, move_q, move_kv = pl.pallas_call(
        prepare_kernel,
        in_specs=[scalars, whole, whole, whole, away],
        out_specs=[whole] * 8,
        out_shape=[
            shape((contexts, tall), f32),
            shape((length, HEAD_DIM), f32),
            shape((8, tall), f32),
            shape((BLOCK, HEAD_DIM), f32),
            square,
            square,
            shape((HALF * BLOCK, HALF * BLOCK), bf16),
            square,
        ],
        compiler_params=small,
    )(
        flags.astype(jnp.int32).reshape(1, 2),
        destinations,
        documents.reshape(contexts, BLOCK),
        other_documents.reshape(contexts, BLOCK),
        near,
    )

    grad_shape = shape((kv_heads * packs, 2 * UNIT, HEAD_DIM), bf16)
    window = min(contexts, (REACH + BLOCK - 2) // BLOCK + 1) * BLOCK
    results, near_grad, far_grad = pl.pallas_call(
        attend_kernel,
        in_specs=[whole] * 8,
        out_specs=[whole] * 3,
        out_shape=[moved_shape, grad_shape, grad_shape],
        scratch_shapes=[
            pltpu.VMEM((length, HEAD_DIM), bf16),
            pltpu.VMEM((length, HEAD_DIM), bf16),
            pltpu.VMEM((HEAD_DIM, length), bf16),
            pltpu.VMEM((HEAD_DIM, length), bf16),
            pltpu.VMEM((length, HEAD_DIM), f32),
            pltpu.VMEM((length, HEAD_DIM), f32),
            pltpu.VMEM((2, window, tall), f32),
            pltpu.VMEM((2, window, tall), f32),
            pltpu.VMEM((2, window, tall), bf16),
            pltpu.VMEM((2, window, tall), bf16),
        ],
        compiler_params=small,
    )(*prepared, received, far)

    grads = near_grad.astype(f32) + lax.ppermute(far_grad, "core", swap).astype(f32)
    results = lax.dynamic_update_slice(results, grads.astype(bf16), (0, 2 * HEADS, 0))
    returned = lax.all_to_all(results, ("ctx", "pair"), split_axis=0, concat_axis=0, tiled=True)

    outs = (queries, queries, key_states, value_states)
    return pl.pallas_call(
        return_kernel,
        in_specs=[whole] * 3,
        out_specs=[away] * 4,
        out_shape=[shape(out.shape, bf16) for out in outs],
        scratch_shapes=[pltpu.VMEM(out.shape[1:], bf16) for out in outs]
        + [pltpu.SemaphoreType.DMA((4 * kv_heads + 2,))],
        compiler_params=small,
    )(move_q, move_kv, returned)


def solution(mesh):
    split = jax.sharding.Mesh(
        mesh.devices.reshape(-1, 2, mesh.shape["ctx"]), ("pair", "core", "ctx")
    )
    spec = P(("pair", "core"), "ctx", None)
    return jax.shard_map(
        local,
        mesh=split,
        in_specs=(spec, spec, spec, spec, P(("pair", "core"), "ctx"), P(("pair", "core"), None)),
        out_specs=(spec, spec, spec, spec),
        check_vma=False,
    )
```

```python
import jax
import jax.numpy as jnp
from jax import lax
from jax.experimental import pallas as pl
from jax.experimental.pallas import tpu as pltpu
from jax.sharding import PartitionSpec as P

HEAD_DIM = 128
GROUP = 8
HALF = 4
UNIT = 4
BLOCK = 128
REACH = 512
HEADS = GROUP * UNIT
ROWS = 2 * HEADS + 2 * UNIT
FAR_BELOW = -1e30
FACTOR = HEAD_DIM**-0.5
LOG2E = 1.4426950408889634

f32 = jnp.float32
bf16 = jnp.bfloat16


def dot(a, b):
    return jnp.dot(a, b, preferred_element_type=f32)


def dot_nt(a, b):
    return lax.dot_general(a, b, (((1,), (1,)), ((), ())), preferred_element_type=f32)


def sending_matrix(slots, heads):
    units = BLOCK // UNIT
    size = heads * BLOCK
    unit = lax.broadcasted_iota(jnp.int32, (units, size), 0)
    col = lax.broadcasted_iota(jnp.int32, (units, size), 1)
    spread = ((col % BLOCK) // UNIT == unit).astype(f32).astype(bf16)
    packs = jnp.broadcast_to(slots.astype(f32), (8, units)).astype(bf16)
    where = dot(packs, spread)
    col = lax.broadcasted_iota(jnp.int32, (8, size), 1)
    inner = (col // BLOCK) * UNIT + col % UNIT
    place = where * (heads * UNIT) + inner.astype(f32)
    rows = lax.broadcasted_iota(jnp.int32, (size, size), 0).astype(f32)
    return (place[0:1] == rows).astype(f32).astype(bf16)


def returning_matrix(slots, heads):
    units = BLOCK // UNIT
    size = heads * BLOCK
    row = lax.broadcasted_iota(jnp.int32, (size, units), 0)
    unit = lax.broadcasted_iota(jnp.int32, (size, units), 1)
    packs = jnp.broadcast_to(slots.astype(f32), (size, units))
    where = jnp.sum(
        jnp.where((row % BLOCK) // UNIT == unit, packs, 0.0), axis=1, keepdims=True
    )
    row = lax.broadcasted_iota(jnp.int32, (size, 1), 0)
    inner = (row // BLOCK) * UNIT + row % UNIT
    place = where * (heads * UNIT) + inner.astype(f32)
    cols = lax.broadcasted_iota(jnp.int32, (size, size), 1).astype(f32)
    return (place == cols).astype(f32).astype(bf16)


def slots_of(route):
    return (route % 2) * (BLOCK // UNIT // 2) + route // 2


def send_kernel(
    route_ref, q_hbm, k_hbm, v_hbm, do_hbm, out_hbm,
    q_buf, k_buf, v_buf, do_buf, out_buf, in_sems, out_sems,
):
    packs = BLOCK // UNIT
    kv_heads = k_buf.shape[1] // HEAD_DIM
    group = GROUP * HEAD_DIM
    cut = 2
    share = kv_heads // cut
    loads = []
    for n in range(cut):
        at = pl.ds(n * share * group, share * group)
        pair = [
            pltpu.make_async_copy(q_hbm.at[0, :, at], q_buf.at[:, at], in_sems.at[2 * n]),
            pltpu.make_async_copy(do_hbm.at[0, :, at], do_buf.at[:, at], in_sems.at[2 * n + 1]),
        ]
        if n == 0:
            pair += [
                pltpu.make_async_copy(k_hbm.at[0], k_buf, in_sems.at[2 * cut]),
                pltpu.make_async_copy(v_hbm.at[0], v_buf, in_sems.at[2 * cut + 1]),
            ]
        for copy in pair:
            copy.start()
        loads.append(pair)
    slots = slots_of(route_ref[...])
    move_q = sending_matrix(slots, HALF)
    move_kv = sending_matrix(slots, 2)
    wide = HALF * UNIT
    stores = []
    for m in range(kv_heads):
        if m % share == 0:
            for copy in loads[m // share]:
                copy.wait()
        out = out_buf.at[pl.ds(m * packs, packs)]
        for half in range(2):
            first = m * group + half * HALF * HEAD_DIM
            heads = [slice(first + h * HEAD_DIM, first + (h + 1) * HEAD_DIM) for h in range(HALF)]
            both = jnp.concatenate(
                [
                    jnp.concatenate([q_buf[:, at] for at in heads], axis=0),
                    jnp.concatenate([do_buf[:, at] for at in heads], axis=0),
                ],
                axis=1,
            )
            moved = dot(move_q, both).astype(bf16)
            low = half * wide
            out[:, low : low + wide, :] = moved[:, :HEAD_DIM].reshape(packs, wide, HEAD_DIM)
            low = HEADS + half * wide
            out[:, low : low + wide, :] = moved[:, HEAD_DIM:].reshape(packs, wide, HEAD_DIM)
        at = slice(m * HEAD_DIM, (m + 1) * HEAD_DIM)
        pair = jnp.concatenate([k_buf[:, at], v_buf[:, at]], axis=0)
        out[:, 2 * HEADS :, :] = (
            dot(move_kv, pair).astype(bf16).reshape(packs, 2 * UNIT, HEAD_DIM)
        )
        store = pltpu.make_async_copy(out, out_hbm.at[pl.ds(m * packs, packs)], out_sems.at[m])
        store.start()
        stores.append(store)
    for store in stores:
        store.wait()


def return_kernel(
    move_q, move_kv, in_ref, o_hbm, dq_hbm, dk_hbm, dv_hbm, o_buf, dq_buf, dk_buf, dv_buf, sems
):
    packs = BLOCK // UNIT
    wide = HALF * UNIT
    kv_heads = dk_buf.shape[1] // HEAD_DIM
    stores = []

    def store(buf, hbm, at):
        copy = pltpu.make_async_copy(buf.at[:, at], hbm.at[0, :, at], sems.at[len(stores)])
        copy.start()
        stores.append(copy)

    for m in range(kv_heads):
        block = in_ref.at[pl.ds(m * packs, packs)]
        kv = block[:, 2 * HEADS :, :].reshape(2 * BLOCK, HEAD_DIM)
        pair = dot(move_kv[...], kv).astype(bf16)
        at = slice(m * HEAD_DIM, (m + 1) * HEAD_DIM)
        dk_buf[:, at] = pair[:BLOCK]
        dv_buf[:, at] = pair[BLOCK:]
        if m == kv_heads - 1:
            every = pl.ds(0, dk_buf.shape[1])
            store(dk_buf, dk_hbm, every)
            store(dv_buf, dv_hbm, every)
        for half in range(2):
            low = half * wide
            o = block[:, low : low + wide, :].reshape(packs * wide, HEAD_DIM)
            low = HEADS + half * wide
            dq = block[:, low : low + wide, :].reshape(packs * wide, HEAD_DIM)
            back = dot(move_q[...], jnp.concatenate([o, dq], axis=1)).astype(bf16)
            first = (m * GROUP + half * HALF) * HEAD_DIM
            for h in range(HALF):
                at = slice(first + h * HEAD_DIM, first + (h + 1) * HEAD_DIM)
                rows = slice(h * BLOCK, (h + 1) * BLOCK)
                o_buf[:, at] = back[rows, :HEAD_DIM]
                dq_buf[:, at] = back[rows, HEAD_DIM:]
        at = pl.ds(m * GROUP * HEAD_DIM, GROUP * HEAD_DIM)
        store(o_buf, o_hbm, at)
        store(dq_buf, dq_hbm, at)
    for copy in stores:
        copy.wait()


def prepare_kernel(
    flags, route_ref, docs_ref, other_ref, near_hbm,
    row_docs, col_docs, row_pos, key_pos, apart, together, move_q, move_kv,
):
    slots = slots_of(route_ref[...])
    move_q[...] = returning_matrix(slots, HALF)
    move_kv[...] = returning_matrix(slots, 2)
    r = lax.broadcasted_iota(jnp.int32, (2 * BLOCK, 2 * BLOCK), 0)
    c = lax.broadcasted_iota(jnp.int32, (2 * BLOCK, 2 * BLOCK), 1)

    def place(x):
        inside = x % BLOCK
        unit = (inside % (BLOCK // 2)) // UNIT
        return (inside // (BLOCK // 2)) * BLOCK + unit * 2 * UNIT + (x // BLOCK) * UNIT + x % UNIT

    apart[...] = (place(r) == c).astype(f32).astype(bf16)
    together[...] = (place(c) == r).astype(f32).astype(bf16)
    core = flags[0, 0]
    half = BLOCK // 2

    def key_at(x):
        owner = jnp.where(x < half, core, 1 - core)
        return (2 * ((x % half) // UNIT) + owner) * UNIT + x % UNIT

    def row_at(x):
        return (2 * (x // HEADS) + core) * UNIT + x % UNIT

    key_pos[...] = key_at(lax.broadcasted_iota(jnp.int32, key_pos.shape, 0)).astype(f32)
    row_pos[...] = row_at(lax.broadcasted_iota(jnp.int32, row_pos.shape, 1)).astype(f32)
    docs = jnp.where(flags[0, 1] == 1, docs_ref[...], other_ref[...])
    high = (docs // 32).astype(f32).astype(bf16)
    low = (docs % 32).astype(f32).astype(bf16)
    tall = row_docs.shape[1]
    pos = lax.broadcasted_iota(jnp.int32, (BLOCK, tall), 0)
    to_row = (row_at(lax.broadcasted_iota(jnp.int32, (BLOCK, tall), 1)) == pos).astype(f32).astype(bf16)
    row_docs[...] = dot(high, to_row) * 32 + dot(low, to_row)
    pos = lax.broadcasted_iota(jnp.int32, (BLOCK, BLOCK), 1)
    to_key = (key_at(lax.broadcasted_iota(jnp.int32, (BLOCK, BLOCK), 0)) == pos).astype(f32).astype(bf16)
    for b in range(docs.shape[0]):
        wide_high = jnp.broadcast_to(high[b : b + 1, :], (BLOCK, BLOCK))
        wide_low = jnp.broadcast_to(low[b : b + 1, :], (BLOCK, BLOCK))
        col_docs[b * BLOCK : (b + 1) * BLOCK, :] = (
            dot_nt(to_key, wide_high) * 32 + dot_nt(to_key, wide_low)
        )


def attend_kernel(
    row_docs, col_docs, row_pos, key_pos, apart, together, in_ref, far_ref,
    out_ref, near_grad, far_grad,
    keys, values, keys_t, values_t, dkeys, dvalues, held, pushed, rounded, slopes,
):
    blocks = row_docs.shape[0]
    units = BLOCK // UNIT // 2
    tall = units * HEADS
    back = (REACH + BLOCK - 2) // BLOCK
    at = [slice(b * BLOCK, (b + 1) * BLOCK) for b in range(blocks)]
    mine = [slice(b * units, (b + 1) * units) for b in range(blocks)]
    across = lax.broadcasted_iota(jnp.int32, (BLOCK, BLOCK), 1)
    eye = (lax.broadcasted_iota(jnp.int32, (BLOCK, BLOCK), 0) == across).astype(f32).astype(bf16)

    for b in range(blocks):
        kv = jnp.concatenate(
            [
                in_ref[mine[b], 2 * HEADS :, :].reshape(BLOCK, HEAD_DIM),
                far_ref[mine[b], :, :].reshape(BLOCK, HEAD_DIM),
            ],
            axis=0,
        )
        kv = dot(apart[...], kv)
        keys[at[b], :] = kv[:BLOCK].astype(bf16)
        values[at[b], :] = kv[BLOCK:].astype(bf16)
        keys_t[:, at[b]] = dot_nt(eye, keys[at[b], :]).astype(bf16)
        values_t[:, at[b]] = dot_nt(eye, values[at[b], :]).astype(bf16)
    dkeys[...] = jnp.zeros_like(dkeys)
    dvalues[...] = jnp.zeros_like(dvalues)

    def scores_of(b):
        low = max(0, b - back)
        q = in_ref[mine[b], 0:HEADS, :].reshape(tall, HEAD_DIM)
        docs = row_docs[b : b + 1, :]
        row_max = jnp.full((8, tall), FAR_BELOW, f32)
        for n in range(b + 1 - low):
            scores = dot_nt(keys[at[low + n], :], q)
            allowed = col_docs[at[low + n], 0:1] == docs
            if low + n == b:
                allowed = allowed & (key_pos[:, 0:1] <= row_pos[0:1, :])
            scores = jnp.where(allowed, scores, FAR_BELOW)
            held[b % 2, at[n], :] = scores
            row_max = jnp.maximum(row_max, jnp.max(scores.reshape(BLOCK // 8, 8, tall), axis=0))
        return jnp.max(row_max, axis=0, keepdims=True)

    def weights_of(b, row_max):
        low = max(0, b - back)
        do = in_ref[mine[b], HEADS : 2 * HEADS, :].reshape(tall, HEAD_DIM)
        weight_sum = jnp.zeros((8, tall), f32)
        row_dot = jnp.zeros((8, tall), f32)
        for n in range(b + 1 - low):
            pushes = dot_nt(values[at[low + n], :], do)
            pushed[b % 2, at[n], :] = pushes
            weights = jnp.exp2((held[b % 2, at[n], :] - row_max) * (FACTOR * LOG2E))
            held[b % 2, at[n], :] = weights
            weight_sum = weight_sum + jnp.sum(weights.reshape(BLOCK // 8, 8, tall), axis=0)
            row_dot = row_dot + jnp.sum((weights * pushes).reshape(BLOCK // 8, 8, tall), axis=0)
        inverse = 1.0 / jnp.sum(weight_sum, axis=0, keepdims=True)
        return inverse, jnp.sum(row_dot, axis=0, keepdims=True) * inverse

    def grads_of(b, inverse, row_dot):
        low = max(0, b - back)
        seen = slice(low * BLOCK, (b + 1) * BLOCK)
        count = b + 1 - low
        slot = b % 2
        q = in_ref[mine[b], 0:HEADS, :].reshape(tall, HEAD_DIM)
        do = in_ref[mine[b], HEADS : 2 * HEADS, :].reshape(tall, HEAD_DIM)
        for n in range(count):
            chances = held[slot, at[n], :] * inverse
            rounded[slot, at[n], :] = chances.astype(bf16)
            slopes[slot, at[n], :] = (chances * (pushed[slot, at[n], :] - row_dot)).astype(bf16)
        chances = rounded.at[slot, pl.ds(0, count * BLOCK), :]
        slope = slopes.at[slot, pl.ds(0, count * BLOCK), :]
        out_t = dot(values_t[:, seen], chances[...]).astype(bf16)
        dq_t = (dot(keys_t[:, seen], slope[...]) * FACTOR).astype(bf16)
        dkeys[seen, :] += dot(slope[...], q)
        dvalues[seen, :] += dot(chances[...], do)
        out_ref[mine[b], 0:HEADS, :] = out_t.T.reshape(units, HEADS, HEAD_DIM)
        out_ref[mine[b], HEADS : 2 * HEADS, :] = dq_t.T.reshape(units, HEADS, HEAD_DIM)

    row_max = scores_of(0)
    state = weights_of(0, row_max)
    row_max = scores_of(1)
    for b in range(blocks):
        after = weights_of(b + 1, row_max) if b + 1 < blocks else None
        grads_of(b, *state)
        row_max = scores_of(b + 2) if b + 2 < blocks else None
        state = after

    for b in range(blocks):
        pair = jnp.concatenate(
            [(dkeys[at[b], :] * FACTOR).astype(bf16), dvalues[at[b], :].astype(bf16)], axis=0
        )
        pair = dot(together[...], pair).astype(bf16)
        near_grad[mine[b], :, :] = pair[:BLOCK].reshape(units, 2 * UNIT, HEAD_DIM)
        far_grad[mine[b], :, :] = pair[BLOCK:].reshape(units, 2 * UNIT, HEAD_DIM)


def local(queries, key_states, value_states, out_grad, destinations, documents):
    contexts = lax.axis_size("ctx")
    pairs = lax.axis_size("pair")
    packs = 2 * pairs
    kv_heads = key_states.shape[2] // HEAD_DIM
    swap = [(0, 1), (1, 0)]
    core = lax.axis_index("core")

    shape = jax.ShapeDtypeStruct
    whole = pl.BlockSpec(memory_space=pltpu.VMEM)
    away = pl.BlockSpec(memory_space=pl.ANY)
    scalars = pl.BlockSpec(memory_space=pltpu.SMEM)
    small = pltpu.CompilerParams(vmem_limit_bytes=40 * 1024 * 1024)
    moved_shape = shape((kv_heads * packs, ROWS, HEAD_DIM), bf16)
    sending = pl.pallas_call(
        send_kernel,
        in_specs=[whole] + [away] * 4,
        out_specs=away,
        out_shape=moved_shape,
        scratch_shapes=[
            pltpu.VMEM(queries.shape[1:], bf16),
            pltpu.VMEM(key_states.shape[1:], bf16),
            pltpu.VMEM(key_states.shape[1:], bf16),
            pltpu.VMEM(queries.shape[1:], bf16),
            pltpu.VMEM(moved_shape.shape, bf16),
            pltpu.SemaphoreType.DMA((2 * kv_heads + 2,)),
            pltpu.SemaphoreType.DMA((kv_heads,)),
        ],
        compiler_params=pltpu.CompilerParams(vmem_limit_bytes=63 * 1024 * 1024),
    )(destinations, queries, key_states, value_states, out_grad)

    sending, other_documents = lax.optimization_barrier(
        (sending, lax.ppermute(documents, "core", swap))
    )
    received = lax.all_to_all(sending, ("ctx", "pair"), split_axis=0, concat_axis=0, tiled=True)
    near = received[:, 2 * HEADS :, :]
    far = lax.ppermute(near, "core", swap)

    length = contexts * BLOCK
    tall = GROUP * BLOCK // 2
    flags = jnp.stack([core, (lax.axis_index("ctx") % 2 == core).astype(core.dtype)])
    square = shape((2 * BLOCK, 2 * BLOCK), bf16)
    *prepared, move_q, move_kv = pl.pallas_call(
        prepare_kernel,
        in_specs=[scalars, whole, whole, whole, away],
        out_specs=[whole] * 8,
        out_shape=[
            shape((contexts, tall), f32),
            shape((length, HEAD_DIM), f32),
            shape((8, tall), f32),
            shape((BLOCK, HEAD_DIM), f32),
            square,
            square,
            shape((HALF * BLOCK, HALF * BLOCK), bf16),
            square,
        ],
        compiler_params=small,
    )(
        flags.astype(jnp.int32).reshape(1, 2),
        destinations,
        documents.reshape(contexts, BLOCK),
        other_documents.reshape(contexts, BLOCK),
        near,
    )

    grad_shape = shape((kv_heads * packs, 2 * UNIT, HEAD_DIM), bf16)
    window = min(contexts, (REACH + BLOCK - 2) // BLOCK + 1) * BLOCK
    results, near_grad, far_grad = pl.pallas_call(
        attend_kernel,
        in_specs=[whole] * 8,
        out_specs=[whole] * 3,
        out_shape=[moved_shape, grad_shape, grad_shape],
        scratch_shapes=[
            pltpu.VMEM((length, HEAD_DIM), bf16),
            pltpu.VMEM((length, HEAD_DIM), bf16),
            pltpu.VMEM((HEAD_DIM, length), bf16),
            pltpu.VMEM((HEAD_DIM, length), bf16),
            pltpu.VMEM((length, HEAD_DIM), f32),
            pltpu.VMEM((length, HEAD_DIM), f32),
            pltpu.VMEM((2, window, tall), f32),
            pltpu.VMEM((2, window, tall), f32),
            pltpu.VMEM((2, window, tall), bf16),
            pltpu.VMEM((2, window, tall), bf16),
        ],
        compiler_params=small,
    )(*prepared, received, far)

    grads = near_grad.astype(f32) + lax.ppermute(far_grad, "core", swap).astype(f32)
    results = lax.dynamic_update_slice(results, grads.astype(bf16), (0, 2 * HEADS, 0))
    returned = lax.all_to_all(results, ("ctx", "pair"), split_axis=0, concat_axis=0, tiled=True)

    outs = (queries, queries, key_states, value_states)
    return pl.pallas_call(
        return_kernel,
        in_specs=[whole] * 3,
        out_specs=[away] * 4,
        out_shape=[shape(out.shape, bf16) for out in outs],
        scratch_shapes=[pltpu.VMEM(out.shape[1:], bf16) for out in outs]
        + [pltpu.SemaphoreType.DMA((4 * kv_heads + 2,))],
        compiler_params=small,
    )(move_q, move_kv, returned)


def solution(mesh):
    split = jax.sharding.Mesh(
        mesh.devices.reshape(-1, 2, mesh.shape["ctx"]), ("pair", "core", "ctx")
    )
    spec = P(("pair", "core"), "ctx", None)
    return jax.shard_map(
        local,
        mesh=split,
        in_specs=(spec, spec, spec, spec, P(("pair", "core"), "ctx"), P(("pair", "core"), None)),
        out_specs=(spec, spec, spec, spec),
        check_vma=False,
    )
```

```python
import jax
import jax.numpy as jnp
from jax import lax
from jax.experimental import pallas as pl
from jax.experimental.pallas import tpu as pltpu
from jax.sharding import PartitionSpec as P

HEAD_DIM = 128
GROUP = 8
PAIR = 2
UNIT = 4
BLOCK = 128
REACH = 512
HEADS = GROUP * UNIT
ROWS = 2 * HEADS + 2 * UNIT
FAR_BELOW = -1e30
FACTOR = HEAD_DIM**-0.5
LOG2E = 1.4426950408889634

f32 = jnp.float32
bf16 = jnp.bfloat16


def dot(a, b):
    return jnp.dot(a, b, preferred_element_type=f32)


def dot_nt(a, b):
    return lax.dot_general(a, b, (((1,), (1,)), ((), ())), preferred_element_type=f32)


def sending_matrix(slots):
    units = BLOCK // UNIT
    size = PAIR * BLOCK
    unit = lax.broadcasted_iota(jnp.int32, (units, size), 0)
    col = lax.broadcasted_iota(jnp.int32, (units, size), 1)
    spread = ((col % BLOCK) // UNIT == unit).astype(f32).astype(bf16)
    packs = jnp.broadcast_to(slots.astype(f32), (8, units)).astype(bf16)
    where = dot(packs, spread)
    col = lax.broadcasted_iota(jnp.int32, (8, size), 1)
    inner = (col // BLOCK) * UNIT + col % UNIT
    place = where * (PAIR * UNIT) + inner.astype(f32)
    rows = lax.broadcasted_iota(jnp.int32, (size, size), 0).astype(f32)
    return (place[0:1] == rows).astype(f32).astype(bf16)


def returning_matrix(slots):
    units = BLOCK // UNIT
    size = PAIR * BLOCK
    row = lax.broadcasted_iota(jnp.int32, (size, units), 0)
    unit = lax.broadcasted_iota(jnp.int32, (size, units), 1)
    packs = jnp.broadcast_to(slots.astype(f32), (size, units))
    where = jnp.sum(
        jnp.where((row % BLOCK) // UNIT == unit, packs, 0.0), axis=1, keepdims=True
    )
    row = lax.broadcasted_iota(jnp.int32, (size, 1), 0)
    inner = (row // BLOCK) * UNIT + row % UNIT
    place = where * (PAIR * UNIT) + inner.astype(f32)
    cols = lax.broadcasted_iota(jnp.int32, (size, size), 1).astype(f32)
    return (place == cols).astype(f32).astype(bf16)


def slots_of(route):
    return (route % 2) * (BLOCK // UNIT // 2) + route // 2


def send_kernel(
    route_ref, q_hbm, k_hbm, v_hbm, do_hbm, out_hbm,
    q_buf, k_buf, v_buf, do_buf, out_buf, in_sems, out_sems,
):
    packs = BLOCK // UNIT
    kv_heads = k_buf.shape[1] // HEAD_DIM
    group = GROUP * HEAD_DIM
    cut = 2
    share = kv_heads // cut
    loads = []
    for n in range(cut):
        at = pl.ds(n * share * group, share * group)
        pair = [
            pltpu.make_async_copy(q_hbm.at[0, :, at], q_buf.at[:, at], in_sems.at[2 * n]),
            pltpu.make_async_copy(do_hbm.at[0, :, at], do_buf.at[:, at], in_sems.at[2 * n + 1]),
        ]
        if n == 0:
            pair += [
                pltpu.make_async_copy(k_hbm.at[0], k_buf, in_sems.at[2 * cut]),
                pltpu.make_async_copy(v_hbm.at[0], v_buf, in_sems.at[2 * cut + 1]),
            ]
        for copy in pair:
            copy.start()
        loads.append(pair)
    slots = slots_of(route_ref[...])
    move = sending_matrix(slots)
    wide = PAIR * UNIT
    stores = []
    for m in range(kv_heads):
        if m % share == 0:
            for copy in loads[m // share]:
                copy.wait()
        out = out_buf.at[pl.ds(m * packs, packs)]
        for some in range(0, GROUP, 2 * PAIR):
            moved = []
            for h in (some, some + PAIR):
                heads = [pl.ds(m * group + (h + j) * HEAD_DIM, HEAD_DIM) for j in range(PAIR)]
                both = jnp.concatenate(
                    [
                        jnp.concatenate([q_buf[:, at] for at in heads], axis=0),
                        jnp.concatenate([do_buf[:, at] for at in heads], axis=0),
                    ],
                    axis=1,
                )
                moved.append(dot(move, both).reshape(packs, wide, 2 * HEAD_DIM))
            moved = jnp.concatenate(moved, axis=1).astype(bf16)
            low = some * UNIT
            out[:, low : low + 2 * wide, :] = moved[:, :, :HEAD_DIM]
            low = HEADS + some * UNIT
            out[:, low : low + 2 * wide, :] = moved[:, :, HEAD_DIM:]
        at = slice(m * HEAD_DIM, (m + 1) * HEAD_DIM)
        pair = jnp.concatenate([k_buf[:, at], v_buf[:, at]], axis=0)
        out[:, 2 * HEADS :, :] = (
            dot(move, pair).astype(bf16).reshape(packs, wide, HEAD_DIM)
        )
        store = pltpu.make_async_copy(out, out_hbm.at[pl.ds(m * packs, packs)], out_sems.at[m])
        store.start()
        stores.append(store)
    for store in stores:
        store.wait()


def return_kernel(
    move, in_ref, o_hbm, dq_hbm, dk_hbm, dv_hbm, o_buf, dq_buf, dk_buf, dv_buf, sems
):
    packs = BLOCK // UNIT
    wide = PAIR * UNIT
    kv_heads = dk_buf.shape[1] // HEAD_DIM
    stores = []

    def store(buf, hbm, at):
        copy = pltpu.make_async_copy(buf.at[:, at], hbm.at[0, :, at], sems.at[len(stores)])
        copy.start()
        stores.append(copy)

    for m in range(kv_heads):
        block = in_ref.at[pl.ds(m * packs, packs)]
        kv = block[:, 2 * HEADS :, :].reshape(2 * BLOCK, HEAD_DIM)
        pair = dot(move[...], kv).astype(bf16)
        at = slice(m * HEAD_DIM, (m + 1) * HEAD_DIM)
        dk_buf[:, at] = pair[:BLOCK]
        dv_buf[:, at] = pair[BLOCK:]
        if m == kv_heads - 1:
            every = pl.ds(0, dk_buf.shape[1])
            store(dk_buf, dk_hbm, every)
            store(dv_buf, dv_hbm, every)
        for h in range(0, GROUP, PAIR):
            low = h * UNIT
            o = block[:, low : low + wide, :].reshape(packs * wide, HEAD_DIM)
            low = HEADS + h * UNIT
            dq = block[:, low : low + wide, :].reshape(packs * wide, HEAD_DIM)
            back = dot(move[...], jnp.concatenate([o, dq], axis=1)).astype(bf16)
            for j in range(PAIR):
                first = (m * GROUP + h + j) * HEAD_DIM
                at = slice(first, first + HEAD_DIM)
                rows = slice(j * BLOCK, (j + 1) * BLOCK)
                o_buf[:, at] = back[rows, :HEAD_DIM]
                dq_buf[:, at] = back[rows, HEAD_DIM:]
        at = pl.ds(m * GROUP * HEAD_DIM, GROUP * HEAD_DIM)
        store(o_buf, o_hbm, at)
        store(dq_buf, dq_hbm, at)
    for copy in stores:
        copy.wait()


def prepare_kernel(
    flags, route_ref, docs_ref, other_ref, near_hbm,
    row_docs, col_docs, row_pos, key_pos, apart, together, move,
):
    slots = slots_of(route_ref[...])
    move[...] = returning_matrix(slots)
    r = lax.broadcasted_iota(jnp.int32, (2 * BLOCK, 2 * BLOCK), 0)
    c = lax.broadcasted_iota(jnp.int32, (2 * BLOCK, 2 * BLOCK), 1)

    def place(x):
        inside = x % BLOCK
        unit = (inside % (BLOCK // 2)) // UNIT
        return (inside // (BLOCK // 2)) * BLOCK + unit * 2 * UNIT + (x // BLOCK) * UNIT + x % UNIT

    apart[...] = (place(r) == c).astype(f32).astype(bf16)
    r = lax.broadcasted_iota(jnp.int32, (BLOCK, BLOCK), 0)
    c = lax.broadcasted_iota(jnp.int32, (BLOCK, BLOCK), 1)
    inside = c % (BLOCK // 2)
    to = (inside // UNIT) * 2 * UNIT + (c // (BLOCK // 2)) * UNIT + c % UNIT
    together[...] = (to == r).astype(f32).astype(bf16)
    core = flags[0, 0]
    half = BLOCK // 2

    def key_at(x):
        owner = jnp.where(x < half, core, 1 - core)
        return (2 * ((x % half) // UNIT) + owner) * UNIT + x % UNIT

    def row_at(x):
        return (2 * (x // HEADS) + core) * UNIT + x % UNIT

    key_pos[...] = key_at(lax.broadcasted_iota(jnp.int32, key_pos.shape, 0)).astype(f32)
    row_pos[...] = row_at(lax.broadcasted_iota(jnp.int32, row_pos.shape, 1)).astype(f32)
    docs = jnp.where(flags[0, 1] == 1, docs_ref[...], other_ref[...])
    high = (docs // 32).astype(f32).astype(bf16)
    low = (docs % 32).astype(f32).astype(bf16)
    tall = row_docs.shape[1]
    pos = lax.broadcasted_iota(jnp.int32, (BLOCK, tall), 0)
    to_row = (row_at(lax.broadcasted_iota(jnp.int32, (BLOCK, tall), 1)) == pos).astype(f32).astype(bf16)
    row_docs[...] = dot(high, to_row) * 32 + dot(low, to_row)
    pos = lax.broadcasted_iota(jnp.int32, (BLOCK, BLOCK), 1)
    to_key = (key_at(lax.broadcasted_iota(jnp.int32, (BLOCK, BLOCK), 0)) == pos).astype(f32).astype(bf16)
    for b in range(docs.shape[0]):
        wide_high = jnp.broadcast_to(high[b : b + 1, :], (BLOCK, BLOCK))
        wide_low = jnp.broadcast_to(low[b : b + 1, :], (BLOCK, BLOCK))
        col_docs[b * BLOCK : (b + 1) * BLOCK, :] = (
            dot_nt(to_key, wide_high) * 32 + dot_nt(to_key, wide_low)
        )


def attend_kernel(
    row_docs, col_docs, row_pos, key_pos, apart, together, in_ref, far_ref,
    out_ref, far_grad, near_slopes, near_chances,
    keys, values, keys_t, values_t, dkeys, dvalues, held, pushed, rounded, slopes,
):
    blocks = row_docs.shape[0]
    units = BLOCK // UNIT // 2
    tall = units * HEADS
    back = (REACH + BLOCK - 2) // BLOCK
    at = [slice(b * BLOCK, (b + 1) * BLOCK) for b in range(blocks)]
    mine = [slice(b * units, (b + 1) * units) for b in range(blocks)]
    across = lax.broadcasted_iota(jnp.int32, (BLOCK, BLOCK), 1)
    eye = (lax.broadcasted_iota(jnp.int32, (BLOCK, BLOCK), 0) == across).astype(f32).astype(bf16)

    for b in range(blocks):
        kv = jnp.concatenate(
            [
                in_ref[mine[b], 2 * HEADS :, :].reshape(BLOCK, HEAD_DIM),
                far_ref[mine[b], :, :].reshape(BLOCK, HEAD_DIM),
            ],
            axis=0,
        )
        kv = dot(apart[...], kv)
        keys[at[b], :] = kv[:BLOCK].astype(bf16)
        values[at[b], :] = kv[BLOCK:].astype(bf16)
        keys_t[:, at[b]] = dot_nt(eye, keys[at[b], :]).astype(bf16)
        values_t[:, at[b]] = dot_nt(eye, values[at[b], :]).astype(bf16)
    dkeys[...] = jnp.zeros_like(dkeys)
    dvalues[...] = jnp.zeros_like(dvalues)
    half = BLOCK // 2
    near = [slice(b * BLOCK, b * BLOCK + half) for b in range(blocks)]
    other = [slice(b * BLOCK + half, (b + 1) * BLOCK) for b in range(blocks)]
    firsts = near_firsts(blocks)

    def scores_of(b):
        low = max(0, b - back)
        q = in_ref[mine[b], 0:HEADS, :].reshape(tall, HEAD_DIM)
        docs = row_docs[b : b + 1, :]
        row_max = jnp.full((8, tall), FAR_BELOW, f32)
        for n in range(b + 1 - low):
            scores = dot_nt(keys[at[low + n], :], q)
            allowed = col_docs[at[low + n], 0:1] == docs
            if low + n == b:
                allowed = allowed & (key_pos[:, 0:1] <= row_pos[0:1, :])
            scores = jnp.where(allowed, scores, FAR_BELOW)
            held[b % 2, at[n], :] = scores
            row_max = jnp.maximum(row_max, jnp.max(scores.reshape(BLOCK // 8, 8, tall), axis=0))
        return jnp.max(row_max, axis=0, keepdims=True)

    def weights_of(b, row_max):
        low = max(0, b - back)
        do = in_ref[mine[b], HEADS : 2 * HEADS, :].reshape(tall, HEAD_DIM)
        weight_sum = jnp.zeros((8, tall), f32)
        row_dot = jnp.zeros((8, tall), f32)
        for n in range(b + 1 - low):
            pushes = dot_nt(values[at[low + n], :], do)
            pushed[b % 2, at[n], :] = pushes
            weights = jnp.exp2((held[b % 2, at[n], :] - row_max) * (FACTOR * LOG2E))
            held[b % 2, at[n], :] = weights
            weight_sum = weight_sum + jnp.sum(weights.reshape(BLOCK // 8, 8, tall), axis=0)
            row_dot = row_dot + jnp.sum((weights * pushes).reshape(BLOCK // 8, 8, tall), axis=0)
        inverse = 1.0 / jnp.sum(weight_sum, axis=0, keepdims=True)
        return inverse, jnp.sum(row_dot, axis=0, keepdims=True) * inverse

    def grads_of(b, inverse, row_dot):
        low = max(0, b - back)
        seen = slice(low * BLOCK, (b + 1) * BLOCK)
        count = b + 1 - low
        slot = b % 2
        q = in_ref[mine[b], 0:HEADS, :].reshape(tall, HEAD_DIM)
        do = in_ref[mine[b], HEADS : 2 * HEADS, :].reshape(tall, HEAD_DIM)
        for n in range(count):
            chances = held[slot, at[n], :] * inverse
            slope = (chances * (pushed[slot, at[n], :] - row_dot)).astype(bf16)
            chances = chances.astype(bf16)
            rounded[slot, at[n], :] = chances
            slopes[slot, at[n], :] = slope
            mine_at = slice(firsts[b] + n * half, firsts[b] + (n + 1) * half)
            near_slopes[mine_at, :] = slope[:half]
            near_chances[mine_at, :] = chances[:half]
        chances = rounded.at[slot, pl.ds(0, count * BLOCK), :]
        slope = slopes.at[slot, pl.ds(0, count * BLOCK), :]
        out_t = dot(values_t[:, seen], chances[...]).astype(bf16)
        dq_t = (dot(keys_t[:, seen], slope[...]) * FACTOR).astype(bf16)
        seen = slice(low * half, (b + 1) * half)
        slope = jnp.concatenate([slopes[slot, other[n], :] for n in range(count)], axis=0)
        chances = jnp.concatenate([rounded[slot, other[n], :] for n in range(count)], axis=0)
        dkeys[seen, :] += dot(slope, q)
        dvalues[seen, :] += dot(chances, do)
        out_ref[mine[b], 0:HEADS, :] = out_t.T.reshape(units, HEADS, HEAD_DIM)
        out_ref[mine[b], HEADS : 2 * HEADS, :] = dq_t.T.reshape(units, HEADS, HEAD_DIM)

    row_max = scores_of(0)
    state = weights_of(0, row_max)
    row_max = scores_of(1)
    for b in range(blocks):
        after = weights_of(b + 1, row_max) if b + 1 < blocks else None
        grads_of(b, *state)
        row_max = scores_of(b + 2) if b + 2 < blocks else None
        state = after

    write_grads(together, dkeys, dvalues, far_grad)


def near_firsts(blocks):
    back = (REACH + BLOCK - 2) // BLOCK
    firsts = [0]
    for b in range(blocks):
        firsts.append(firsts[-1] + (min(b, back) + 1) * (BLOCK // 2))
    return firsts


def write_grads(together, dkeys, dvalues, grad):
    half = BLOCK // 2
    for b in range(dkeys.shape[0] // half):
        at = slice(b * half, (b + 1) * half)
        pair = jnp.concatenate(
            [(dkeys[at, :] * FACTOR).astype(bf16), dvalues[at, :].astype(bf16)], axis=0
        )
        units = half // UNIT
        grad[b * units : (b + 1) * units, :, :] = (
            dot(together[...], pair).astype(bf16).reshape(units, 2 * UNIT, HEAD_DIM)
        )


def near_kernel(together, in_ref, near_slopes, near_chances, near_grad, dkeys, dvalues):
    half = BLOCK // 2
    units = half // UNIT
    blocks = in_ref.shape[0] // units
    firsts = near_firsts(blocks)
    dkeys[...] = jnp.zeros_like(dkeys)
    dvalues[...] = jnp.zeros_like(dvalues)
    for b in range(blocks):
        mine = slice(b * units, (b + 1) * units)
        q = in_ref[mine, 0:HEADS, :].reshape(units * HEADS, HEAD_DIM)
        do = in_ref[mine, HEADS : 2 * HEADS, :].reshape(units * HEADS, HEAD_DIM)
        rows = slice(firsts[b], firsts[b + 1])
        seen = slice((b + 1) * half - (firsts[b + 1] - firsts[b]), (b + 1) * half)
        dkeys[seen, :] += dot(near_slopes[rows, :], q)
        dvalues[seen, :] += dot(near_chances[rows, :], do)
    write_grads(together, dkeys, dvalues, near_grad)


def local(queries, key_states, value_states, out_grad, destinations, documents):
    contexts = lax.axis_size("ctx")
    pairs = lax.axis_size("pair")
    packs = 2 * pairs
    kv_heads = key_states.shape[2] // HEAD_DIM
    swap = [(0, 1), (1, 0)]
    core = lax.axis_index("core")

    shape = jax.ShapeDtypeStruct
    whole = pl.BlockSpec(memory_space=pltpu.VMEM)
    away = pl.BlockSpec(memory_space=pl.ANY)
    scalars = pl.BlockSpec(memory_space=pltpu.SMEM)
    small = pltpu.CompilerParams(vmem_limit_bytes=40 * 1024 * 1024)
    moved_shape = shape((kv_heads * packs, ROWS, HEAD_DIM), bf16)
    sending = pl.pallas_call(
        send_kernel,
        in_specs=[whole] + [away] * 4,
        out_specs=away,
        out_shape=moved_shape,
        scratch_shapes=[
            pltpu.VMEM(queries.shape[1:], bf16),
            pltpu.VMEM(key_states.shape[1:], bf16),
            pltpu.VMEM(key_states.shape[1:], bf16),
            pltpu.VMEM(queries.shape[1:], bf16),
            pltpu.VMEM(moved_shape.shape, bf16),
            pltpu.SemaphoreType.DMA((2 * kv_heads + 2,)),
            pltpu.SemaphoreType.DMA((kv_heads,)),
        ],
        compiler_params=pltpu.CompilerParams(vmem_limit_bytes=63 * 1024 * 1024),
    )(destinations, queries, key_states, value_states, out_grad)

    sending, other_documents = lax.optimization_barrier(
        (sending, lax.ppermute(documents, "core", swap))
    )
    received = lax.all_to_all(sending, ("ctx", "pair"), split_axis=0, concat_axis=0, tiled=True)
    near = received[:, 2 * HEADS :, :]
    far = lax.ppermute(near, "core", swap)

    length = contexts * BLOCK
    tall = GROUP * BLOCK // 2
    flags = jnp.stack([core, (lax.axis_index("ctx") % 2 == core).astype(core.dtype)])
    square = shape((2 * BLOCK, 2 * BLOCK), bf16)
    *prepared, move = pl.pallas_call(
        prepare_kernel,
        in_specs=[scalars, whole, whole, whole, away],
        out_specs=[whole] * 7,
        out_shape=[
            shape((contexts, tall), f32),
            shape((length, HEAD_DIM), f32),
            shape((8, tall), f32),
            shape((BLOCK, HEAD_DIM), f32),
            square,
            shape((BLOCK, BLOCK), bf16),
            square,
        ],
        compiler_params=small,
    )(
        flags.astype(jnp.int32).reshape(1, 2),
        destinations,
        documents.reshape(contexts, BLOCK),
        other_documents.reshape(contexts, BLOCK),
        near,
    )

    grad_shape = shape((kv_heads * packs, 2 * UNIT, HEAD_DIM), bf16)
    window = min(contexts, (REACH + BLOCK - 2) // BLOCK + 1) * BLOCK
    near_shape = shape((near_firsts(contexts)[-1], tall), bf16)
    results, far_grad, near_slopes, near_chances = pl.pallas_call(
        attend_kernel,
        in_specs=[whole] * 8,
        out_specs=[whole] * 4,
        out_shape=[moved_shape, grad_shape, near_shape, near_shape],
        scratch_shapes=[
            pltpu.VMEM((length, HEAD_DIM), bf16),
            pltpu.VMEM((length, HEAD_DIM), bf16),
            pltpu.VMEM((HEAD_DIM, length), bf16),
            pltpu.VMEM((HEAD_DIM, length), bf16),
            pltpu.VMEM((length // 2, HEAD_DIM), f32),
            pltpu.VMEM((length // 2, HEAD_DIM), f32),
            pltpu.VMEM((2, window, tall), f32),
            pltpu.VMEM((2, window, tall), f32),
            pltpu.VMEM((2, window, tall), bf16),
            pltpu.VMEM((2, window, tall), bf16),
        ],
        compiler_params=small,
    )(*prepared, received, far)

    far_grad = lax.ppermute(far_grad, "core", swap)
    near_grad = pl.pallas_call(
        near_kernel,
        in_specs=[whole] * 4,
        out_specs=whole,
        out_shape=grad_shape,
        scratch_shapes=[pltpu.VMEM((length // 2, HEAD_DIM), f32)] * 2,
        compiler_params=small,
    )(prepared[-1], received, near_slopes, near_chances)
    grads = near_grad.astype(f32) + far_grad.astype(f32)
    results = lax.dynamic_update_slice(results, grads.astype(bf16), (0, 2 * HEADS, 0))
    returned = lax.all_to_all(results, ("ctx", "pair"), split_axis=0, concat_axis=0, tiled=True)

    outs = (queries, queries, key_states, value_states)
    return pl.pallas_call(
        return_kernel,
        in_specs=[whole] * 2,
        out_specs=[away] * 4,
        out_shape=[shape(out.shape, bf16) for out in outs],
        scratch_shapes=[pltpu.VMEM(out.shape[1:], bf16) for out in outs]
        + [pltpu.SemaphoreType.DMA((4 * kv_heads + 2,))],
        compiler_params=small,
    )(move, returned)


def solution(mesh):
    split = jax.sharding.Mesh(
        mesh.devices.reshape(-1, 2, mesh.shape["ctx"]), ("pair", "core", "ctx")
    )
    spec = P(("pair", "core"), "ctx", None)
    return jax.shard_map(
        local,
        mesh=split,
        in_specs=(spec, spec, spec, spec, P(("pair", "core"), "ctx"), P(("pair", "core"), None)),
        out_specs=(spec, spec, spec, spec),
        check_vma=False,
    )
```

```python
import jax
import jax.numpy as jnp
from jax import lax
from jax.experimental import pallas as pl
from jax.experimental.pallas import tpu as pltpu
from jax.sharding import PartitionSpec as P

HEAD_DIM = 128
GROUP = 8
PAIR = 2
UNIT = 4
BLOCK = 128
REACH = 512
HEADS = GROUP * UNIT
ROWS = 2 * HEADS + 2 * UNIT
FAR_BELOW = -1e30
FACTOR = HEAD_DIM**-0.5
LOG2E = 1.4426950408889634

f32 = jnp.float32
bf16 = jnp.bfloat16


def dot(a, b):
    return jnp.dot(a, b, preferred_element_type=f32)


def dot_nt(a, b):
    return lax.dot_general(a, b, (((1,), (1,)), ((), ())), preferred_element_type=f32)


def sending_matrix(slots):
    units = BLOCK // UNIT
    size = PAIR * BLOCK
    unit = lax.broadcasted_iota(jnp.int32, (units, size), 0)
    col = lax.broadcasted_iota(jnp.int32, (units, size), 1)
    spread = ((col % BLOCK) // UNIT == unit).astype(f32).astype(bf16)
    packs = jnp.broadcast_to(slots.astype(f32), (8, units)).astype(bf16)
    where = dot(packs, spread)
    col = lax.broadcasted_iota(jnp.int32, (8, size), 1)
    inner = (col // BLOCK) * UNIT + col % UNIT
    place = where * (PAIR * UNIT) + inner.astype(f32)
    rows = lax.broadcasted_iota(jnp.int32, (size, size), 0).astype(f32)
    return (place[0:1] == rows).astype(f32).astype(bf16)


def returning_matrix(slots):
    units = BLOCK // UNIT
    size = PAIR * BLOCK
    row = lax.broadcasted_iota(jnp.int32, (size, units), 0)
    unit = lax.broadcasted_iota(jnp.int32, (size, units), 1)
    packs = jnp.broadcast_to(slots.astype(f32), (size, units))
    where = jnp.sum(
        jnp.where((row % BLOCK) // UNIT == unit, packs, 0.0), axis=1, keepdims=True
    )
    row = lax.broadcasted_iota(jnp.int32, (size, 1), 0)
    inner = (row // BLOCK) * UNIT + row % UNIT
    place = where * (PAIR * UNIT) + inner.astype(f32)
    cols = lax.broadcasted_iota(jnp.int32, (size, size), 1).astype(f32)
    return (place == cols).astype(f32).astype(bf16)


def slots_of(route):
    return (route % 2) * (BLOCK // UNIT // 2) + route // 2


def send_kernel(
    route_hbm, q_hbm, k_hbm, v_hbm, do_hbm, out_ref, route, q_buf, k_buf, v_buf, do_buf, in_sems
):
    packs = BLOCK // UNIT
    kv_heads = k_buf.shape[1] // HEAD_DIM
    group = GROUP * HEAD_DIM
    cut = 2
    share = kv_heads // cut
    asked = pltpu.make_async_copy(route_hbm, route, in_sems.at[2 * cut + 2])
    asked.start()
    loads = []
    for n in range(cut):
        at = pl.ds(n * share * group, share * group)
        pair = [
            pltpu.make_async_copy(q_hbm.at[0, :, at], q_buf.at[:, at], in_sems.at[2 * n]),
            pltpu.make_async_copy(do_hbm.at[0, :, at], do_buf.at[:, at], in_sems.at[2 * n + 1]),
        ]
        if n == 0:
            pair += [
                pltpu.make_async_copy(k_hbm.at[0], k_buf, in_sems.at[2 * cut]),
                pltpu.make_async_copy(v_hbm.at[0], v_buf, in_sems.at[2 * cut + 1]),
            ]
        for copy in pair:
            copy.start()
        loads.append(pair)
    asked.wait()
    slots = slots_of(route[...])
    move = sending_matrix(slots)
    wide = PAIR * UNIT
    for m in range(kv_heads):
        if m % share == 0:
            for copy in loads[m // share]:
                copy.wait()
        out = out_ref.at[pl.ds(m * packs, packs)]
        for some in range(0, GROUP, 2 * PAIR):
            moved = []
            for h in (some, some + PAIR):
                heads = [pl.ds(m * group + (h + j) * HEAD_DIM, HEAD_DIM) for j in range(PAIR)]
                both = jnp.concatenate(
                    [
                        jnp.concatenate([q_buf[:, at] for at in heads], axis=0),
                        jnp.concatenate([do_buf[:, at] for at in heads], axis=0),
                    ],
                    axis=1,
                )
                moved.append(dot(move, both).reshape(packs, wide, 2 * HEAD_DIM))
            moved = jnp.concatenate(moved, axis=1).astype(bf16)
            low = some * UNIT
            out[:, low : low + 2 * wide, :] = moved[:, :, :HEAD_DIM]
            low = HEADS + some * UNIT
            out[:, low : low + 2 * wide, :] = moved[:, :, HEAD_DIM:]
        at = slice(m * HEAD_DIM, (m + 1) * HEAD_DIM)
        pair = jnp.concatenate([k_buf[:, at], v_buf[:, at]], axis=0)
        out[:, 2 * HEADS :, :] = (
            dot(move, pair).astype(bf16).reshape(packs, wide, HEAD_DIM)
        )


def return_kernel(
    move, in_ref, o_hbm, dq_hbm, dk_hbm, dv_hbm, o_buf, dq_buf, dk_buf, dv_buf, sems
):
    packs = BLOCK // UNIT
    wide = PAIR * UNIT
    kv_heads = dk_buf.shape[1] // HEAD_DIM
    stores = []

    def store(buf, hbm, at):
        copy = pltpu.make_async_copy(buf.at[:, at], hbm.at[0, :, at], sems.at[len(stores)])
        copy.start()
        stores.append(copy)

    for m in range(kv_heads):
        block = in_ref.at[pl.ds(m * packs, packs)]
        kv = block[:, 2 * HEADS :, :].reshape(2 * BLOCK, HEAD_DIM)
        pair = dot(move[...], kv).astype(bf16)
        at = slice(m * HEAD_DIM, (m + 1) * HEAD_DIM)
        dk_buf[:, at] = pair[:BLOCK]
        dv_buf[:, at] = pair[BLOCK:]
        if m == kv_heads - 1:
            every = pl.ds(0, dk_buf.shape[1])
            store(dk_buf, dk_hbm, every)
            store(dv_buf, dv_hbm, every)
        for h in range(0, GROUP, PAIR):
            low = h * UNIT
            o = block[:, low : low + wide, :].reshape(packs * wide, HEAD_DIM)
            low = HEADS + h * UNIT
            dq = block[:, low : low + wide, :].reshape(packs * wide, HEAD_DIM)
            back = dot(move[...], jnp.concatenate([o, dq], axis=1)).astype(bf16)
            for j in range(PAIR):
                first = (m * GROUP + h + j) * HEAD_DIM
                at = slice(first, first + HEAD_DIM)
                rows = slice(j * BLOCK, (j + 1) * BLOCK)
                o_buf[:, at] = back[rows, :HEAD_DIM]
                dq_buf[:, at] = back[rows, HEAD_DIM:]
        at = pl.ds(m * GROUP * HEAD_DIM, GROUP * HEAD_DIM)
        store(o_buf, o_hbm, at)
        store(dq_buf, dq_hbm, at)
    for copy in stores:
        copy.wait()


def prepare_kernel(
    flags, route_ref, docs_ref, other_ref, near_hbm,
    row_docs, col_docs, row_pos, key_pos, apart, together, move,
):
    slots = slots_of(route_ref[...])
    move[...] = returning_matrix(slots)
    r = lax.broadcasted_iota(jnp.int32, (2 * BLOCK, 2 * BLOCK), 0)
    c = lax.broadcasted_iota(jnp.int32, (2 * BLOCK, 2 * BLOCK), 1)

    def place(x):
        inside = x % BLOCK
        unit = (inside % (BLOCK // 2)) // UNIT
        return (inside // (BLOCK // 2)) * BLOCK + unit * 2 * UNIT + (x // BLOCK) * UNIT + x % UNIT

    apart[...] = (place(r) == c).astype(f32).astype(bf16)
    r = lax.broadcasted_iota(jnp.int32, (BLOCK, BLOCK), 0)
    c = lax.broadcasted_iota(jnp.int32, (BLOCK, BLOCK), 1)
    inside = c % (BLOCK // 2)
    to = (inside // UNIT) * 2 * UNIT + (c // (BLOCK // 2)) * UNIT + c % UNIT
    together[...] = (to == r).astype(f32).astype(bf16)
    core = flags[0, 0]
    half = BLOCK // 2

    def key_at(x):
        owner = jnp.where(x < half, core, 1 - core)
        return (2 * ((x % half) // UNIT) + owner) * UNIT + x % UNIT

    def row_at(x):
        return (2 * (x // HEADS) + core) * UNIT + x % UNIT

    key_pos[...] = key_at(lax.broadcasted_iota(jnp.int32, key_pos.shape, 0)).astype(f32)
    row_pos[...] = row_at(lax.broadcasted_iota(jnp.int32, row_pos.shape, 1)).astype(f32)
    docs = jnp.where(flags[0, 1] == 1, docs_ref[...], other_ref[...])
    high = (docs // 32).astype(f32).astype(bf16)
    low = (docs % 32).astype(f32).astype(bf16)
    tall = row_docs.shape[1]
    pos = lax.broadcasted_iota(jnp.int32, (BLOCK, tall), 0)
    to_row = (row_at(lax.broadcasted_iota(jnp.int32, (BLOCK, tall), 1)) == pos).astype(f32).astype(bf16)
    row_docs[...] = dot(high, to_row) * 32 + dot(low, to_row)
    pos = lax.broadcasted_iota(jnp.int32, (BLOCK, BLOCK), 1)
    to_key = (key_at(lax.broadcasted_iota(jnp.int32, (BLOCK, BLOCK), 0)) == pos).astype(f32).astype(bf16)
    for b in range(docs.shape[0]):
        wide_high = jnp.broadcast_to(high[b : b + 1, :], (BLOCK, BLOCK))
        wide_low = jnp.broadcast_to(low[b : b + 1, :], (BLOCK, BLOCK))
        col_docs[b * BLOCK : (b + 1) * BLOCK, :] = (
            dot_nt(to_key, wide_high) * 32 + dot_nt(to_key, wide_low)
        )


def attend_kernel(
    row_docs, col_docs, row_pos, key_pos, apart, together, in_ref, far_ref,
    out_ref, far_grad, near_slopes, near_chances,
    keys, values, keys_t, values_t, dkeys, dvalues, held, pushed, rounded, slopes,
):
    blocks = row_docs.shape[0]
    units = BLOCK // UNIT // 2
    tall = units * HEADS
    back = (REACH + BLOCK - 2) // BLOCK
    at = [slice(b * BLOCK, (b + 1) * BLOCK) for b in range(blocks)]
    mine = [slice(b * units, (b + 1) * units) for b in range(blocks)]
    across = lax.broadcasted_iota(jnp.int32, (BLOCK, BLOCK), 1)
    eye = (lax.broadcasted_iota(jnp.int32, (BLOCK, BLOCK), 0) == across).astype(f32).astype(bf16)

    for b in range(blocks):
        kv = jnp.concatenate(
            [
                in_ref[mine[b], 2 * HEADS :, :].reshape(BLOCK, HEAD_DIM),
                far_ref[mine[b], :, :].reshape(BLOCK, HEAD_DIM),
            ],
            axis=0,
        )
        kv = dot(apart[...], kv)
        keys[at[b], :] = kv[:BLOCK].astype(bf16)
        values[at[b], :] = kv[BLOCK:].astype(bf16)
        keys_t[:, at[b]] = dot_nt(eye, keys[at[b], :]).astype(bf16)
        values_t[:, at[b]] = dot_nt(eye, values[at[b], :]).astype(bf16)
    dkeys[...] = jnp.zeros_like(dkeys)
    dvalues[...] = jnp.zeros_like(dvalues)
    half = BLOCK // 2
    near = [slice(b * BLOCK, b * BLOCK + half) for b in range(blocks)]
    other = [slice(b * BLOCK + half, (b + 1) * BLOCK) for b in range(blocks)]
    firsts = near_firsts(blocks)

    def scores_of(b):
        low = max(0, b - back)
        q = in_ref[mine[b], 0:HEADS, :].reshape(tall, HEAD_DIM)
        docs = row_docs[b : b + 1, :]
        row_max = jnp.full((8, tall), FAR_BELOW, f32)
        for n in range(b + 1 - low):
            scores = dot_nt(keys[at[low + n], :], q)
            allowed = col_docs[at[low + n], 0:1] == docs
            if low + n == b:
                allowed = allowed & (key_pos[:, 0:1] <= row_pos[0:1, :])
            scores = jnp.where(allowed, scores, FAR_BELOW)
            held[b % 2, at[n], :] = scores
            row_max = jnp.maximum(row_max, jnp.max(scores.reshape(BLOCK // 8, 8, tall), axis=0))
        return jnp.max(row_max, axis=0, keepdims=True)

    def weights_of(b, row_max):
        low = max(0, b - back)
        do = in_ref[mine[b], HEADS : 2 * HEADS, :].reshape(tall, HEAD_DIM)
        weight_sum = jnp.zeros((8, tall), f32)
        row_dot = jnp.zeros((8, tall), f32)
        for n in range(b + 1 - low):
            pushes = dot_nt(values[at[low + n], :], do)
            pushed[b % 2, at[n], :] = pushes
            weights = jnp.exp2((held[b % 2, at[n], :] - row_max) * (FACTOR * LOG2E))
            held[b % 2, at[n], :] = weights
            weight_sum = weight_sum + jnp.sum(weights.reshape(BLOCK // 8, 8, tall), axis=0)
            row_dot = row_dot + jnp.sum((weights * pushes).reshape(BLOCK // 8, 8, tall), axis=0)
        inverse = 1.0 / jnp.sum(weight_sum, axis=0, keepdims=True)
        return inverse, jnp.sum(row_dot, axis=0, keepdims=True) * inverse

    def grads_of(b, inverse, row_dot):
        low = max(0, b - back)
        seen = slice(low * BLOCK, (b + 1) * BLOCK)
        count = b + 1 - low
        slot = b % 2
        q = in_ref[mine[b], 0:HEADS, :].reshape(tall, HEAD_DIM)
        do = in_ref[mine[b], HEADS : 2 * HEADS, :].reshape(tall, HEAD_DIM)
        for n in range(count):
            chances = held[slot, at[n], :] * inverse
            slope = (chances * (pushed[slot, at[n], :] - row_dot)).astype(bf16)
            chances = chances.astype(bf16)
            rounded[slot, at[n], :] = chances
            slopes[slot, at[n], :] = slope
            mine_at = slice(firsts[b] + n * half, firsts[b] + (n + 1) * half)
            near_slopes[mine_at, :] = slope[:half]
            near_chances[mine_at, :] = chances[:half]
        chances = rounded.at[slot, pl.ds(0, count * BLOCK), :]
        slope = slopes.at[slot, pl.ds(0, count * BLOCK), :]
        out_t = dot(values_t[:, seen], chances[...]).astype(bf16)
        dq_t = (dot(keys_t[:, seen], slope[...]) * FACTOR).astype(bf16)
        seen = slice(low * half, (b + 1) * half)
        slope = jnp.concatenate([slopes[slot, other[n], :] for n in range(count)], axis=0)
        chances = jnp.concatenate([rounded[slot, other[n], :] for n in range(count)], axis=0)
        dkeys[seen, :] += dot(slope, q)
        dvalues[seen, :] += dot(chances, do)
        out_ref[mine[b], 0:HEADS, :] = out_t.T.reshape(units, HEADS, HEAD_DIM)
        out_ref[mine[b], HEADS : 2 * HEADS, :] = dq_t.T.reshape(units, HEADS, HEAD_DIM)

    row_max = scores_of(0)
    state = weights_of(0, row_max)
    row_max = scores_of(1)
    for b in range(blocks):
        after = weights_of(b + 1, row_max) if b + 1 < blocks else None
        grads_of(b, *state)
        row_max = scores_of(b + 2) if b + 2 < blocks else None
        state = after

    write_grads(together, dkeys, dvalues, far_grad)


def near_firsts(blocks):
    back = (REACH + BLOCK - 2) // BLOCK
    firsts = [0]
    for b in range(blocks):
        firsts.append(firsts[-1] + (min(b, back) + 1) * (BLOCK // 2))
    return firsts


def write_grads(together, dkeys, dvalues, grad):
    half = BLOCK // 2
    for b in range(dkeys.shape[0] // half):
        at = slice(b * half, (b + 1) * half)
        pair = jnp.concatenate(
            [(dkeys[at, :] * FACTOR).astype(bf16), dvalues[at, :].astype(bf16)], axis=0
        )
        units = half // UNIT
        grad[b * units : (b + 1) * units, :, :] = (
            dot(together[...], pair).astype(bf16).reshape(units, 2 * UNIT, HEAD_DIM)
        )


def near_kernel(together, in_ref, near_slopes, near_chances, near_grad, dkeys, dvalues):
    half = BLOCK // 2
    units = half // UNIT
    blocks = in_ref.shape[0] // units
    firsts = near_firsts(blocks)
    dkeys[...] = jnp.zeros_like(dkeys)
    dvalues[...] = jnp.zeros_like(dvalues)
    for b in range(blocks):
        mine = slice(b * units, (b + 1) * units)
        q = in_ref[mine, 0:HEADS, :].reshape(units * HEADS, HEAD_DIM)
        do = in_ref[mine, HEADS : 2 * HEADS, :].reshape(units * HEADS, HEAD_DIM)
        rows = slice(firsts[b], firsts[b + 1])
        seen = slice((b + 1) * half - (firsts[b + 1] - firsts[b]), (b + 1) * half)
        dkeys[seen, :] += dot(near_slopes[rows, :], q)
        dvalues[seen, :] += dot(near_chances[rows, :], do)
    write_grads(together, dkeys, dvalues, near_grad)


def local(queries, key_states, value_states, out_grad, destinations, documents):
    contexts = lax.axis_size("ctx")
    pairs = lax.axis_size("pair")
    packs = 2 * pairs
    kv_heads = key_states.shape[2] // HEAD_DIM
    swap = [(0, 1), (1, 0)]
    core = lax.axis_index("core")

    shape = jax.ShapeDtypeStruct
    whole = pl.BlockSpec(memory_space=pltpu.VMEM)
    away = pl.BlockSpec(memory_space=pl.ANY)

    def stay(x):
        return pltpu.with_memory_space_constraint(x, pltpu.HBM)

    scalars = pl.BlockSpec(memory_space=pltpu.SMEM)
    small = pltpu.CompilerParams(vmem_limit_bytes=40 * 1024 * 1024)
    moved_shape = shape((kv_heads * packs, ROWS, HEAD_DIM), bf16)
    sending = pl.pallas_call(
        send_kernel,
        in_specs=[away] * 5,
        out_specs=whole,
        out_shape=moved_shape,
        scratch_shapes=[
            pltpu.VMEM(destinations.shape, jnp.int32),
            pltpu.VMEM(queries.shape[1:], bf16),
            pltpu.VMEM(key_states.shape[1:], bf16),
            pltpu.VMEM(key_states.shape[1:], bf16),
            pltpu.VMEM(queries.shape[1:], bf16),
            pltpu.SemaphoreType.DMA((2 * kv_heads + 3,)),
        ],
        compiler_params=small,
    )(*map(stay, (destinations, queries, key_states, value_states, out_grad)))

    sending, other_documents = lax.optimization_barrier(
        (sending, lax.ppermute(documents, "core", swap))
    )
    received = lax.all_to_all(sending, ("ctx", "pair"), split_axis=0, concat_axis=0, tiled=True)
    near = received[:, 2 * HEADS :, :]
    far = lax.ppermute(near, "core", swap)

    length = contexts * BLOCK
    tall = GROUP * BLOCK // 2
    flags = jnp.stack([core, (lax.axis_index("ctx") % 2 == core).astype(core.dtype)])
    square = shape((2 * BLOCK, 2 * BLOCK), bf16)
    *prepared, move = pl.pallas_call(
        prepare_kernel,
        in_specs=[scalars, whole, whole, whole, away],
        out_specs=[whole] * 7,
        out_shape=[
            shape((contexts, tall), f32),
            shape((length, HEAD_DIM), f32),
            shape((8, tall), f32),
            shape((BLOCK, HEAD_DIM), f32),
            square,
            shape((BLOCK, BLOCK), bf16),
            square,
        ],
        compiler_params=small,
    )(
        flags.astype(jnp.int32).reshape(1, 2),
        destinations,
        documents.reshape(contexts, BLOCK),
        other_documents.reshape(contexts, BLOCK),
        near,
    )

    grad_shape = shape((kv_heads * packs, 2 * UNIT, HEAD_DIM), bf16)
    window = min(contexts, (REACH + BLOCK - 2) // BLOCK + 1) * BLOCK
    near_shape = shape((near_firsts(contexts)[-1], tall), bf16)
    results, far_grad, near_slopes, near_chances = pl.pallas_call(
        attend_kernel,
        in_specs=[whole] * 8,
        out_specs=[whole] * 4,
        out_shape=[moved_shape, grad_shape, near_shape, near_shape],
        scratch_shapes=[
            pltpu.VMEM((length, HEAD_DIM), bf16),
            pltpu.VMEM((length, HEAD_DIM), bf16),
            pltpu.VMEM((HEAD_DIM, length), bf16),
            pltpu.VMEM((HEAD_DIM, length), bf16),
            pltpu.VMEM((length // 2, HEAD_DIM), f32),
            pltpu.VMEM((length // 2, HEAD_DIM), f32),
            pltpu.VMEM((2, window, tall), f32),
            pltpu.VMEM((2, window, tall), f32),
            pltpu.VMEM((2, window, tall), bf16),
            pltpu.VMEM((2, window, tall), bf16),
        ],
        compiler_params=small,
    )(*prepared, received, far)

    far_grad = lax.ppermute(far_grad, "core", swap)
    near_grad = pl.pallas_call(
        near_kernel,
        in_specs=[whole] * 4,
        out_specs=whole,
        out_shape=grad_shape,
        scratch_shapes=[pltpu.VMEM((length // 2, HEAD_DIM), f32)] * 2,
        compiler_params=small,
    )(prepared[-1], received, near_slopes, near_chances)
    grads = near_grad.astype(f32) + far_grad.astype(f32)
    results = lax.dynamic_update_slice(results, grads.astype(bf16), (0, 2 * HEADS, 0))
    returned = lax.all_to_all(results, ("ctx", "pair"), split_axis=0, concat_axis=0, tiled=True)

    outs = (queries, queries, key_states, value_states)
    return pl.pallas_call(
        return_kernel,
        in_specs=[whole] * 2,
        out_specs=[away] * 4,
        out_shape=[shape(out.shape, bf16) for out in outs],
        scratch_shapes=[pltpu.VMEM(out.shape[1:], bf16) for out in outs]
        + [pltpu.SemaphoreType.DMA((4 * kv_heads + 2,))],
        compiler_params=small,
    )(move, returned)


def solution(mesh):
    split = jax.sharding.Mesh(
        mesh.devices.reshape(-1, 2, mesh.shape["ctx"]), ("pair", "core", "ctx")
    )
    spec = P(("pair", "core"), "ctx", None)
    return jax.shard_map(
        local,
        mesh=split,
        in_specs=(spec, spec, spec, spec, P(("pair", "core"), "ctx"), P(("pair", "core"), None)),
        out_specs=(spec, spec, spec, spec),
        check_vma=False,
    )
```

```python
import jax
import jax.numpy as jnp
from jax import lax
from jax.experimental import pallas as pl
from jax.experimental.pallas import tpu as pltpu
from jax.sharding import PartitionSpec as P

HEAD_DIM = 128
GROUP = 8
PAIR = 2
UNIT = 4
BLOCK = 128
REACH = 512
HEADS = GROUP * UNIT
ROWS = 2 * HEADS + 2 * UNIT
FAR_BELOW = -1e30
FACTOR = HEAD_DIM**-0.5
LOG2E = 1.4426950408889634

f32 = jnp.float32
bf16 = jnp.bfloat16


def dot(a, b):
    return jnp.dot(a, b, preferred_element_type=f32)


def dot_nt(a, b):
    return lax.dot_general(a, b, (((1,), (1,)), ((), ())), preferred_element_type=f32)


def sending_matrix(slots):
    units = BLOCK // UNIT
    size = PAIR * BLOCK
    unit = lax.broadcasted_iota(jnp.int32, (units, size), 0)
    col = lax.broadcasted_iota(jnp.int32, (units, size), 1)
    spread = ((col % BLOCK) // UNIT == unit).astype(f32).astype(bf16)
    packs = jnp.broadcast_to(slots.astype(f32), (8, units)).astype(bf16)
    where = dot(packs, spread)
    col = lax.broadcasted_iota(jnp.int32, (8, size), 1)
    inner = (col // BLOCK) * UNIT + col % UNIT
    place = where * (PAIR * UNIT) + inner.astype(f32)
    rows = lax.broadcasted_iota(jnp.int32, (size, size), 0).astype(f32)
    return (place[0:1] == rows).astype(f32).astype(bf16)


def returning_matrix(slots):
    units = BLOCK // UNIT
    size = PAIR * BLOCK
    row = lax.broadcasted_iota(jnp.int32, (size, units), 0)
    unit = lax.broadcasted_iota(jnp.int32, (size, units), 1)
    packs = jnp.broadcast_to(slots.astype(f32), (size, units))
    where = jnp.sum(
        jnp.where((row % BLOCK) // UNIT == unit, packs, 0.0), axis=1, keepdims=True
    )
    row = lax.broadcasted_iota(jnp.int32, (size, 1), 0)
    inner = (row // BLOCK) * UNIT + row % UNIT
    place = where * (PAIR * UNIT) + inner.astype(f32)
    cols = lax.broadcasted_iota(jnp.int32, (size, size), 1).astype(f32)
    return (place == cols).astype(f32).astype(bf16)


def slots_of(route):
    return (route % 2) * (BLOCK // UNIT // 2) + route // 2


def send_kernel(
    route_hbm, q_hbm, k_hbm, v_hbm, do_hbm, out_ref, route, q_buf, k_buf, v_buf, do_buf, in_sems
):
    packs = BLOCK // UNIT
    kv_heads = k_buf.shape[1] // HEAD_DIM
    group = GROUP * HEAD_DIM
    cut = 2
    share = kv_heads // cut
    asked = pltpu.make_async_copy(route_hbm, route, in_sems.at[2 * cut + 2])
    asked.start()
    loads = []
    for n in range(cut):
        at = pl.ds(n * share * group, share * group)
        pair = [
            pltpu.make_async_copy(q_hbm.at[0, :, at], q_buf.at[:, at], in_sems.at[2 * n]),
            pltpu.make_async_copy(do_hbm.at[0, :, at], do_buf.at[:, at], in_sems.at[2 * n + 1]),
        ]
        if n == 0:
            pair += [
                pltpu.make_async_copy(k_hbm.at[0], k_buf, in_sems.at[2 * cut]),
                pltpu.make_async_copy(v_hbm.at[0], v_buf, in_sems.at[2 * cut + 1]),
            ]
        for copy in pair:
            copy.start()
        loads.append(pair)
    asked.wait()
    slots = slots_of(route[...])
    move = sending_matrix(slots)
    wide = PAIR * UNIT
    for m in range(kv_heads):
        if m % share == 0:
            for copy in loads[m // share]:
                copy.wait()
        out = out_ref.at[pl.ds(m * packs, packs)]
        for some in range(0, GROUP, 2 * PAIR):
            moved = []
            for h in (some, some + PAIR):
                heads = [pl.ds(m * group + (h + j) * HEAD_DIM, HEAD_DIM) for j in range(PAIR)]
                both = jnp.concatenate(
                    [
                        jnp.concatenate([q_buf[:, at] for at in heads], axis=0),
                        jnp.concatenate([do_buf[:, at] for at in heads], axis=0),
                    ],
                    axis=1,
                )
                moved.append(dot(move, both).reshape(packs, wide, 2 * HEAD_DIM))
            moved = jnp.concatenate(moved, axis=1).astype(bf16)
            low = some * UNIT
            out[:, low : low + 2 * wide, :] = moved[:, :, :HEAD_DIM]
            low = HEADS + some * UNIT
            out[:, low : low + 2 * wide, :] = moved[:, :, HEAD_DIM:]
        at = slice(m * HEAD_DIM, (m + 1) * HEAD_DIM)
        pair = jnp.concatenate([k_buf[:, at], v_buf[:, at]], axis=0)
        out[:, 2 * HEADS :, :] = (
            dot(move, pair).astype(bf16).reshape(packs, wide, HEAD_DIM)
        )


def return_kernel(
    move, in_ref, o_hbm, dq_hbm, dk_hbm, dv_hbm, o_buf, dq_buf, dk_buf, dv_buf, sems
):
    packs = BLOCK // UNIT
    wide = PAIR * UNIT
    kv_heads = dk_buf.shape[1] // HEAD_DIM
    stores = []

    def store(buf, hbm, at):
        copy = pltpu.make_async_copy(buf.at[:, at], hbm.at[0, :, at], sems.at[len(stores)])
        copy.start()
        stores.append(copy)

    for m in range(kv_heads):
        block = in_ref.at[pl.ds(m * packs, packs)]
        kv = block[:, 2 * HEADS :, :].reshape(2 * BLOCK, HEAD_DIM)
        pair = dot(move[...], kv).astype(bf16)
        at = slice(m * HEAD_DIM, (m + 1) * HEAD_DIM)
        dk_buf[:, at] = pair[:BLOCK]
        dv_buf[:, at] = pair[BLOCK:]
        if m == kv_heads - 1:
            every = pl.ds(0, dk_buf.shape[1])
            store(dk_buf, dk_hbm, every)
            store(dv_buf, dv_hbm, every)
        for h in range(0, GROUP, PAIR):
            low = h * UNIT
            o = block[:, low : low + wide, :].reshape(packs * wide, HEAD_DIM)
            low = HEADS + h * UNIT
            dq = block[:, low : low + wide, :].reshape(packs * wide, HEAD_DIM)
            back = dot(move[...], jnp.concatenate([o, dq], axis=1)).astype(bf16)
            for j in range(PAIR):
                first = (m * GROUP + h + j) * HEAD_DIM
                at = slice(first, first + HEAD_DIM)
                rows = slice(j * BLOCK, (j + 1) * BLOCK)
                o_buf[:, at] = back[rows, :HEAD_DIM]
                dq_buf[:, at] = back[rows, HEAD_DIM:]
        at = pl.ds(m * GROUP * HEAD_DIM, GROUP * HEAD_DIM)
        store(o_buf, o_hbm, at)
        store(dq_buf, dq_hbm, at)
    for copy in stores:
        copy.wait()


def prepare_kernel(
    flags, route_ref, docs_ref, other_ref, near_hbm,
    row_docs, col_docs, row_pos, key_pos, apart, together, move,
):
    slots = slots_of(route_ref[...])
    move[...] = returning_matrix(slots)
    r = lax.broadcasted_iota(jnp.int32, (2 * BLOCK, 2 * BLOCK), 0)
    c = lax.broadcasted_iota(jnp.int32, (2 * BLOCK, 2 * BLOCK), 1)

    def place(x):
        inside = x % BLOCK
        unit = (inside % (BLOCK // 2)) // UNIT
        return (inside // (BLOCK // 2)) * BLOCK + unit * 2 * UNIT + (x // BLOCK) * UNIT + x % UNIT

    apart[...] = (place(r) == c).astype(f32).astype(bf16)
    r = lax.broadcasted_iota(jnp.int32, (BLOCK, BLOCK), 0)
    c = lax.broadcasted_iota(jnp.int32, (BLOCK, BLOCK), 1)
    inside = c % (BLOCK // 2)
    to = (inside // UNIT) * 2 * UNIT + (c // (BLOCK // 2)) * UNIT + c % UNIT
    together[...] = (to == r).astype(f32).astype(bf16)
    core = flags[0, 0]
    half = BLOCK // 2

    def key_at(x):
        owner = jnp.where(x < half, core, 1 - core)
        return (2 * ((x % half) // UNIT) + owner) * UNIT + x % UNIT

    def row_at(x):
        return (2 * (x // HEADS) + core) * UNIT + x % UNIT

    key_pos[...] = key_at(lax.broadcasted_iota(jnp.int32, key_pos.shape, 0)).astype(f32)
    row_pos[...] = row_at(lax.broadcasted_iota(jnp.int32, row_pos.shape, 1)).astype(f32)
    docs = jnp.where(flags[0, 1] == 1, docs_ref[...], other_ref[...])
    high = (docs // 32).astype(f32).astype(bf16)
    low = (docs % 32).astype(f32).astype(bf16)
    tall = row_docs.shape[1]
    pos = lax.broadcasted_iota(jnp.int32, (BLOCK, tall), 0)
    to_row = (row_at(lax.broadcasted_iota(jnp.int32, (BLOCK, tall), 1)) == pos).astype(f32).astype(bf16)
    row_docs[...] = dot(high, to_row) * 32 + dot(low, to_row)
    pos = lax.broadcasted_iota(jnp.int32, (BLOCK, BLOCK), 1)
    to_key = (key_at(lax.broadcasted_iota(jnp.int32, (BLOCK, BLOCK), 0)) == pos).astype(f32).astype(bf16)
    for b in range(docs.shape[0]):
        wide_high = jnp.broadcast_to(high[b : b + 1, :], (BLOCK, BLOCK))
        wide_low = jnp.broadcast_to(low[b : b + 1, :], (BLOCK, BLOCK))
        col_docs[b * BLOCK : (b + 1) * BLOCK, :] = (
            dot_nt(to_key, wide_high) * 32 + dot_nt(to_key, wide_low)
        )


def attend_kernel(
    row_docs, col_docs, row_pos, key_pos, apart, together, in_ref, far_ref,
    out_ref, far_grad, near_slopes, near_chances,
    keys, values, keys_t, values_t, dkeys, dvalues, held, pushed, rounded, slopes,
):
    blocks = row_docs.shape[0]
    units = BLOCK // UNIT // 2
    tall = units * HEADS
    back = (REACH + BLOCK - 2) // BLOCK
    at = [slice(b * BLOCK, (b + 1) * BLOCK) for b in range(blocks)]
    mine = [slice(b * units, (b + 1) * units) for b in range(blocks)]
    across = lax.broadcasted_iota(jnp.int32, (BLOCK, BLOCK), 1)
    eye = (lax.broadcasted_iota(jnp.int32, (BLOCK, BLOCK), 0) == across).astype(f32).astype(bf16)

    for b in range(blocks):
        kv = jnp.concatenate(
            [
                in_ref[mine[b], 2 * HEADS :, :].reshape(BLOCK, HEAD_DIM),
                far_ref[mine[b], :, :].reshape(BLOCK, HEAD_DIM),
            ],
            axis=0,
        )
        kv = dot(apart[...], kv)
        keys[at[b], :] = kv[:BLOCK].astype(bf16)
        values[at[b], :] = kv[BLOCK:].astype(bf16)
        keys_t[:, at[b]] = dot_nt(eye, keys[at[b], :]).astype(bf16)
        values_t[:, at[b]] = dot_nt(eye, values[at[b], :]).astype(bf16)
    dkeys[...] = jnp.zeros_like(dkeys)
    dvalues[...] = jnp.zeros_like(dvalues)
    half = BLOCK // 2
    near = [slice(b * BLOCK, b * BLOCK + half) for b in range(blocks)]
    other = [slice(b * BLOCK + half, (b + 1) * BLOCK) for b in range(blocks)]
    firsts = near_firsts(blocks)

    def scores_of(b):
        low = max(0, b - back)
        q = in_ref[mine[b], 0:HEADS, :].reshape(tall, HEAD_DIM)
        docs = row_docs[b : b + 1, :]
        row_max = jnp.full((8, tall), FAR_BELOW, f32)
        every = dot_nt(keys[low * BLOCK : (b + 1) * BLOCK, :], q)
        for n in range(b + 1 - low):
            scores = every[at[n], :]
            allowed = col_docs[at[low + n], 0:1] == docs
            if low + n == b:
                allowed = allowed & (key_pos[:, 0:1] <= row_pos[0:1, :])
            scores = jnp.where(allowed, scores, FAR_BELOW)
            held[b % 3, at[n], :] = scores
            row_max = jnp.maximum(row_max, jnp.max(scores.reshape(BLOCK // 8, 8, tall), axis=0))
        return jnp.max(row_max, axis=0, keepdims=True)

    def weights_of(b, row_max):
        low = max(0, b - back)
        do = in_ref[mine[b], HEADS : 2 * HEADS, :].reshape(tall, HEAD_DIM)
        weight_sum = jnp.zeros((8, tall), f32)
        row_dot = jnp.zeros((8, tall), f32)
        every = dot_nt(values[low * BLOCK : (b + 1) * BLOCK, :], do)
        for n in range(b + 1 - low):
            pushes = every[at[n], :]
            pushed[b % 3, at[n], :] = pushes
            weights = jnp.exp2((held[b % 3, at[n], :] - row_max) * (FACTOR * LOG2E))
            held[b % 3, at[n], :] = weights
            weight_sum = weight_sum + jnp.sum(weights.reshape(BLOCK // 8, 8, tall), axis=0)
            row_dot = row_dot + jnp.sum((weights * pushes).reshape(BLOCK // 8, 8, tall), axis=0)
        inverse = 1.0 / jnp.sum(weight_sum, axis=0, keepdims=True)
        return inverse, jnp.sum(row_dot, axis=0, keepdims=True) * inverse

    def grads_of(b, inverse, row_dot):
        low = max(0, b - back)
        seen = slice(low * BLOCK, (b + 1) * BLOCK)
        count = b + 1 - low
        slot = b % 3
        q = in_ref[mine[b], 0:HEADS, :].reshape(tall, HEAD_DIM)
        do = in_ref[mine[b], HEADS : 2 * HEADS, :].reshape(tall, HEAD_DIM)
        for n in range(count):
            chances = held[slot, at[n], :] * inverse
            slope = (chances * (pushed[slot, at[n], :] - row_dot)).astype(bf16)
            chances = chances.astype(bf16)
            rounded[slot, at[n], :] = chances
            slopes[slot, at[n], :] = slope
            mine_at = slice(firsts[b] + n * half, firsts[b] + (n + 1) * half)
            near_slopes[mine_at, :] = slope[:half]
            near_chances[mine_at, :] = chances[:half]
        chances = rounded.at[slot, pl.ds(0, count * BLOCK), :]
        slope = slopes.at[slot, pl.ds(0, count * BLOCK), :]
        out_t = dot(values_t[:, seen], chances[...]).astype(bf16)
        dq_t = (dot(keys_t[:, seen], slope[...]) * FACTOR).astype(bf16)
        seen = slice(low * half, (b + 1) * half)
        slope = jnp.concatenate([slopes[slot, other[n], :] for n in range(count)], axis=0)
        chances = jnp.concatenate([rounded[slot, other[n], :] for n in range(count)], axis=0)
        dkeys[seen, :] += dot(slope, q)
        dvalues[seen, :] += dot(chances, do)
        out_ref[mine[b], 0:HEADS, :] = out_t.T.reshape(units, HEADS, HEAD_DIM)
        out_ref[mine[b], HEADS : 2 * HEADS, :] = dq_t.T.reshape(units, HEADS, HEAD_DIM)

    row_max = scores_of(0)
    state = weights_of(0, row_max)
    row_max = scores_of(1)
    for b in range(blocks):
        later = scores_of(b + 2) if b + 2 < blocks else None
        after = weights_of(b + 1, row_max) if b + 1 < blocks else None
        grads_of(b, *state)
        row_max = later
        state = after

    write_grads(together, dkeys, dvalues, far_grad)


def near_firsts(blocks):
    back = (REACH + BLOCK - 2) // BLOCK
    firsts = [0]
    for b in range(blocks):
        firsts.append(firsts[-1] + (min(b, back) + 1) * (BLOCK // 2))
    return firsts


def write_grads(together, dkeys, dvalues, grad):
    half = BLOCK // 2
    for b in range(dkeys.shape[0] // half):
        at = slice(b * half, (b + 1) * half)
        pair = jnp.concatenate(
            [(dkeys[at, :] * FACTOR).astype(bf16), dvalues[at, :].astype(bf16)], axis=0
        )
        units = half // UNIT
        grad[b * units : (b + 1) * units, :, :] = (
            dot(together[...], pair).astype(bf16).reshape(units, 2 * UNIT, HEAD_DIM)
        )


def near_kernel(together, in_ref, near_slopes, near_chances, near_grad, dkeys, dvalues):
    half = BLOCK // 2
    units = half // UNIT
    blocks = in_ref.shape[0] // units
    firsts = near_firsts(blocks)
    dkeys[...] = jnp.zeros_like(dkeys)
    dvalues[...] = jnp.zeros_like(dvalues)
    for b in range(blocks):
        mine = slice(b * units, (b + 1) * units)
        q = in_ref[mine, 0:HEADS, :].reshape(units * HEADS, HEAD_DIM)
        do = in_ref[mine, HEADS : 2 * HEADS, :].reshape(units * HEADS, HEAD_DIM)
        rows = slice(firsts[b], firsts[b + 1])
        seen = slice((b + 1) * half - (firsts[b + 1] - firsts[b]), (b + 1) * half)
        dkeys[seen, :] += dot(near_slopes[rows, :], q)
        dvalues[seen, :] += dot(near_chances[rows, :], do)
    write_grads(together, dkeys, dvalues, near_grad)


def local(queries, key_states, value_states, out_grad, destinations, documents):
    contexts = lax.axis_size("ctx")
    pairs = lax.axis_size("pair")
    packs = 2 * pairs
    kv_heads = key_states.shape[2] // HEAD_DIM
    swap = [(0, 1), (1, 0)]
    core = lax.axis_index("core")

    shape = jax.ShapeDtypeStruct
    whole = pl.BlockSpec(memory_space=pltpu.VMEM)
    away = pl.BlockSpec(memory_space=pl.ANY)

    def stay(x):
        return pltpu.with_memory_space_constraint(x, pltpu.HBM)

    scalars = pl.BlockSpec(memory_space=pltpu.SMEM)
    small = pltpu.CompilerParams(vmem_limit_bytes=40 * 1024 * 1024)
    moved_shape = shape((kv_heads * packs, ROWS, HEAD_DIM), bf16)
    sending = pl.pallas_call(
        send_kernel,
        in_specs=[away] * 5,
        out_specs=whole,
        out_shape=moved_shape,
        scratch_shapes=[
            pltpu.VMEM(destinations.shape, jnp.int32),
            pltpu.VMEM(queries.shape[1:], bf16),
            pltpu.VMEM(key_states.shape[1:], bf16),
            pltpu.VMEM(key_states.shape[1:], bf16),
            pltpu.VMEM(queries.shape[1:], bf16),
            pltpu.SemaphoreType.DMA((2 * kv_heads + 3,)),
        ],
        compiler_params=small,
    )(*map(stay, (destinations, queries, key_states, value_states, out_grad)))

    sending, other_documents = lax.optimization_barrier(
        (sending, lax.ppermute(documents, "core", swap))
    )
    received = lax.all_to_all(sending, ("ctx", "pair"), split_axis=0, concat_axis=0, tiled=True)
    near = received[:, 2 * HEADS :, :]
    far = lax.ppermute(near, "core", swap)

    length = contexts * BLOCK
    tall = GROUP * BLOCK // 2
    flags = jnp.stack([core, (lax.axis_index("ctx") % 2 == core).astype(core.dtype)])
    square = shape((2 * BLOCK, 2 * BLOCK), bf16)
    *prepared, move = pl.pallas_call(
        prepare_kernel,
        in_specs=[scalars, whole, whole, whole, away],
        out_specs=[whole] * 7,
        out_shape=[
            shape((contexts, tall), f32),
            shape((length, HEAD_DIM), f32),
            shape((8, tall), f32),
            shape((BLOCK, HEAD_DIM), f32),
            square,
            shape((BLOCK, BLOCK), bf16),
            square,
        ],
        compiler_params=small,
    )(
        flags.astype(jnp.int32).reshape(1, 2),
        destinations,
        documents.reshape(contexts, BLOCK),
        other_documents.reshape(contexts, BLOCK),
        near,
    )

    grad_shape = shape((kv_heads * packs, 2 * UNIT, HEAD_DIM), bf16)
    window = min(contexts, (REACH + BLOCK - 2) // BLOCK + 1) * BLOCK
    near_shape = shape((near_firsts(contexts)[-1], tall), bf16)
    results, far_grad, near_slopes, near_chances = pl.pallas_call(
        attend_kernel,
        in_specs=[whole] * 8,
        out_specs=[whole] * 4,
        out_shape=[moved_shape, grad_shape, near_shape, near_shape],
        scratch_shapes=[
            pltpu.VMEM((length, HEAD_DIM), bf16),
            pltpu.VMEM((length, HEAD_DIM), bf16),
            pltpu.VMEM((HEAD_DIM, length), bf16),
            pltpu.VMEM((HEAD_DIM, length), bf16),
            pltpu.VMEM((length // 2, HEAD_DIM), f32),
            pltpu.VMEM((length // 2, HEAD_DIM), f32),
            pltpu.VMEM((3, window, tall), f32),
            pltpu.VMEM((3, window, tall), f32),
            pltpu.VMEM((3, window, tall), bf16),
            pltpu.VMEM((3, window, tall), bf16),
        ],
        compiler_params=small,
    )(*prepared, received, far)

    far_grad = lax.ppermute(far_grad, "core", swap)
    near_grad = pl.pallas_call(
        near_kernel,
        in_specs=[whole] * 4,
        out_specs=whole,
        out_shape=grad_shape,
        scratch_shapes=[pltpu.VMEM((length // 2, HEAD_DIM), f32)] * 2,
        compiler_params=small,
    )(prepared[-1], received, near_slopes, near_chances)
    grads = near_grad.astype(f32) + far_grad.astype(f32)
    results = lax.dynamic_update_slice(results, grads.astype(bf16), (0, 2 * HEADS, 0))
    returned = lax.all_to_all(results, ("ctx", "pair"), split_axis=0, concat_axis=0, tiled=True)

    outs = (queries, queries, key_states, value_states)
    return pl.pallas_call(
        return_kernel,
        in_specs=[whole] * 2,
        out_specs=[away] * 4,
        out_shape=[shape(out.shape, bf16) for out in outs],
        scratch_shapes=[pltpu.VMEM(out.shape[1:], bf16) for out in outs]
        + [pltpu.SemaphoreType.DMA((4 * kv_heads + 2,))],
        compiler_params=small,
    )(move, returned)


def solution(mesh):
    split = jax.sharding.Mesh(
        mesh.devices.reshape(-1, 2, mesh.shape["ctx"]), ("pair", "core", "ctx")
    )
    spec = P(("pair", "core"), "ctx", None)
    return jax.shard_map(
        local,
        mesh=split,
        in_specs=(spec, spec, spec, spec, P(("pair", "core"), "ctx"), P(("pair", "core"), None)),
        out_specs=(spec, spec, spec, spec),
        check_vma=False,
    )
```

```python
import jax
import jax.numpy as jnp
from jax import lax
from jax.experimental import pallas as pl
from jax.experimental.pallas import tpu as pltpu
from jax.sharding import PartitionSpec as P

HEAD_DIM = 128
GROUP = 8
PAIR = 2
UNIT = 4
BLOCK = 128
REACH = 512
HEADS = GROUP * UNIT
ROWS = 2 * HEADS + 2 * UNIT
FAR_BELOW = -1e30
FACTOR = HEAD_DIM**-0.5
LOG2E = 1.4426950408889634

f32 = jnp.float32
bf16 = jnp.bfloat16


def dot(a, b):
    return jnp.dot(a, b, preferred_element_type=f32)


def dot_nt(a, b):
    return lax.dot_general(a, b, (((1,), (1,)), ((), ())), preferred_element_type=f32)


def sending_matrix(slots):
    units = BLOCK // UNIT
    size = PAIR * BLOCK
    unit = lax.broadcasted_iota(jnp.int32, (units, size), 0)
    col = lax.broadcasted_iota(jnp.int32, (units, size), 1)
    spread = ((col % BLOCK) // UNIT == unit).astype(f32).astype(bf16)
    packs = jnp.broadcast_to(slots.astype(f32), (8, units)).astype(bf16)
    where = dot(packs, spread)
    col = lax.broadcasted_iota(jnp.int32, (8, size), 1)
    inner = (col // BLOCK) * UNIT + col % UNIT
    place = where * (PAIR * UNIT) + inner.astype(f32)
    rows = lax.broadcasted_iota(jnp.int32, (size, size), 0).astype(f32)
    return (place[0:1] == rows).astype(f32).astype(bf16)


def returning_matrix(slots):
    units = BLOCK // UNIT
    size = PAIR * BLOCK
    row = lax.broadcasted_iota(jnp.int32, (size, units), 0)
    unit = lax.broadcasted_iota(jnp.int32, (size, units), 1)
    packs = jnp.broadcast_to(slots.astype(f32), (size, units))
    where = jnp.sum(
        jnp.where((row % BLOCK) // UNIT == unit, packs, 0.0), axis=1, keepdims=True
    )
    row = lax.broadcasted_iota(jnp.int32, (size, 1), 0)
    inner = (row // BLOCK) * UNIT + row % UNIT
    place = where * (PAIR * UNIT) + inner.astype(f32)
    cols = lax.broadcasted_iota(jnp.int32, (size, size), 1).astype(f32)
    return (place == cols).astype(f32).astype(bf16)


def slots_of(route):
    return (route % 2) * (BLOCK // UNIT // 2) + route // 2


def send_kernel(
    route_hbm, q_hbm, k_hbm, v_hbm, do_hbm, out_ref, route, q_buf, k_buf, v_buf, do_buf, in_sems
):
    packs = BLOCK // UNIT
    kv_heads = k_buf.shape[1] // HEAD_DIM
    group = GROUP * HEAD_DIM
    cut = 2
    share = kv_heads // cut
    asked = pltpu.make_async_copy(route_hbm, route, in_sems.at[2 * cut + 2])
    asked.start()
    loads = []
    for n in range(cut):
        at = pl.ds(n * share * group, share * group)
        pair = [
            pltpu.make_async_copy(q_hbm.at[0, :, at], q_buf.at[:, at], in_sems.at[2 * n]),
            pltpu.make_async_copy(do_hbm.at[0, :, at], do_buf.at[:, at], in_sems.at[2 * n + 1]),
        ]
        if n == 0:
            pair += [
                pltpu.make_async_copy(k_hbm.at[0], k_buf, in_sems.at[2 * cut]),
                pltpu.make_async_copy(v_hbm.at[0], v_buf, in_sems.at[2 * cut + 1]),
            ]
        for copy in pair:
            copy.start()
        loads.append(pair)
    asked.wait()
    slots = slots_of(route[...])
    move = sending_matrix(slots)
    wide = PAIR * UNIT
    for m in range(kv_heads):
        if m % share == 0:
            for copy in loads[m // share]:
                copy.wait()
        out = out_ref.at[pl.ds(m * packs, packs)]
        for some in range(0, GROUP, 2 * PAIR):
            moved = []
            for h in (some, some + PAIR):
                heads = [pl.ds(m * group + (h + j) * HEAD_DIM, HEAD_DIM) for j in range(PAIR)]
                both = jnp.concatenate(
                    [
                        jnp.concatenate([q_buf[:, at] for at in heads], axis=0),
                        jnp.concatenate([do_buf[:, at] for at in heads], axis=0),
                    ],
                    axis=1,
                )
                moved.append(dot(move, both).reshape(packs, wide, 2 * HEAD_DIM))
            moved = jnp.concatenate(moved, axis=1).astype(bf16)
            low = some * UNIT
            out[:, low : low + 2 * wide, :] = moved[:, :, :HEAD_DIM]
            low = HEADS + some * UNIT
            out[:, low : low + 2 * wide, :] = moved[:, :, HEAD_DIM:]
        at = slice(m * HEAD_DIM, (m + 1) * HEAD_DIM)
        pair = jnp.concatenate([k_buf[:, at], v_buf[:, at]], axis=0)
        out[:, 2 * HEADS :, :] = (
            dot(move, pair).astype(bf16).reshape(packs, wide, HEAD_DIM)
        )


def return_kernel(
    move, in_ref, o_hbm, dq_hbm, dk_hbm, dv_hbm, o_buf, dq_buf, dk_buf, dv_buf, sems
):
    packs = BLOCK // UNIT
    wide = PAIR * UNIT
    kv_heads = dk_buf.shape[1] // HEAD_DIM
    stores = []

    def store(buf, hbm, at):
        copy = pltpu.make_async_copy(buf.at[:, at], hbm.at[0, :, at], sems.at[len(stores)])
        copy.start()
        stores.append(copy)

    for m in range(kv_heads):
        block = in_ref.at[pl.ds(m * packs, packs)]
        kv = block[:, 2 * HEADS :, :].reshape(2 * BLOCK, HEAD_DIM)
        pair = dot(move[...], kv).astype(bf16)
        at = slice(m * HEAD_DIM, (m + 1) * HEAD_DIM)
        dk_buf[:, at] = pair[:BLOCK]
        dv_buf[:, at] = pair[BLOCK:]
        if m == kv_heads - 1:
            every = pl.ds(0, dk_buf.shape[1])
            store(dk_buf, dk_hbm, every)
            store(dv_buf, dv_hbm, every)
        for h in range(0, GROUP, PAIR):
            low = h * UNIT
            o = block[:, low : low + wide, :].reshape(packs * wide, HEAD_DIM)
            low = HEADS + h * UNIT
            dq = block[:, low : low + wide, :].reshape(packs * wide, HEAD_DIM)
            back = dot(move[...], jnp.concatenate([o, dq], axis=1)).astype(bf16)
            for j in range(PAIR):
                first = (m * GROUP + h + j) * HEAD_DIM
                at = slice(first, first + HEAD_DIM)
                rows = slice(j * BLOCK, (j + 1) * BLOCK)
                o_buf[:, at] = back[rows, :HEAD_DIM]
                dq_buf[:, at] = back[rows, HEAD_DIM:]
        at = pl.ds(m * GROUP * HEAD_DIM, GROUP * HEAD_DIM)
        store(o_buf, o_hbm, at)
        store(dq_buf, dq_hbm, at)
    for copy in stores:
        copy.wait()


def prepare_kernel(
    flags, route_ref, docs_ref, other_ref, near_hbm,
    row_docs, col_docs, row_pos, key_pos, apart, together, move,
):
    slots = slots_of(route_ref[...])
    move[...] = returning_matrix(slots)
    r = lax.broadcasted_iota(jnp.int32, (2 * BLOCK, 2 * BLOCK), 0)
    c = lax.broadcasted_iota(jnp.int32, (2 * BLOCK, 2 * BLOCK), 1)

    def place(x):
        inside = x % BLOCK
        unit = (inside % (BLOCK // 2)) // UNIT
        return (inside // (BLOCK // 2)) * BLOCK + unit * 2 * UNIT + (x // BLOCK) * UNIT + x % UNIT

    apart[...] = (place(r) == c).astype(f32).astype(bf16)
    r = lax.broadcasted_iota(jnp.int32, (BLOCK, BLOCK), 0)
    c = lax.broadcasted_iota(jnp.int32, (BLOCK, BLOCK), 1)
    inside = c % (BLOCK // 2)
    to = (inside // UNIT) * 2 * UNIT + (c // (BLOCK // 2)) * UNIT + c % UNIT
    together[...] = (to == r).astype(f32).astype(bf16)
    core = flags[0, 0]
    half = BLOCK // 2

    def key_at(x):
        owner = jnp.where(x < half, core, 1 - core)
        return (2 * ((x % half) // UNIT) + owner) * UNIT + x % UNIT

    def row_at(x):
        return (2 * (x // HEADS) + core) * UNIT + x % UNIT

    key_pos[...] = key_at(lax.broadcasted_iota(jnp.int32, key_pos.shape, 0)).astype(f32)
    row_pos[...] = row_at(lax.broadcasted_iota(jnp.int32, row_pos.shape, 1)).astype(f32)
    docs = jnp.where(flags[0, 1] == 1, docs_ref[...], other_ref[...])
    high = (docs // 32).astype(f32).astype(bf16)
    low = (docs % 32).astype(f32).astype(bf16)
    tall = row_docs.shape[1]
    pos = lax.broadcasted_iota(jnp.int32, (BLOCK, tall), 0)
    to_row = (row_at(lax.broadcasted_iota(jnp.int32, (BLOCK, tall), 1)) == pos).astype(f32).astype(bf16)
    row_docs[...] = dot(high, to_row) * 32 + dot(low, to_row)
    pos = lax.broadcasted_iota(jnp.int32, (BLOCK, BLOCK), 1)
    to_key = (key_at(lax.broadcasted_iota(jnp.int32, (BLOCK, BLOCK), 0)) == pos).astype(f32).astype(bf16)
    for b in range(docs.shape[0]):
        wide_high = jnp.broadcast_to(high[b : b + 1, :], (BLOCK, BLOCK))
        wide_low = jnp.broadcast_to(low[b : b + 1, :], (BLOCK, BLOCK))
        col_docs[b * BLOCK : (b + 1) * BLOCK, :] = (
            dot_nt(to_key, wide_high) * 32 + dot_nt(to_key, wide_low)
        )


def attend_kernel(
    row_docs, col_docs, row_pos, key_pos, apart, together, in_ref, far_ref,
    out_ref, far_grad, near_slopes, near_chances,
    keys, values, keys_t, values_t, dkeys, dvalues, held, pushed, rounded, slopes,
):
    blocks = row_docs.shape[0]
    units = BLOCK // UNIT // 2
    tall = units * HEADS
    back = (REACH + BLOCK - 2) // BLOCK
    at = [slice(b * BLOCK, (b + 1) * BLOCK) for b in range(blocks)]
    mine = [slice(b * units, (b + 1) * units) for b in range(blocks)]
    across = lax.broadcasted_iota(jnp.int32, (BLOCK, BLOCK), 1)
    eye = (lax.broadcasted_iota(jnp.int32, (BLOCK, BLOCK), 0) == across).astype(f32).astype(bf16)

    for b in range(blocks):
        kv = jnp.concatenate(
            [
                in_ref[mine[b], 2 * HEADS :, :].reshape(BLOCK, HEAD_DIM),
                far_ref[mine[b], :, :].reshape(BLOCK, HEAD_DIM),
            ],
            axis=0,
        )
        kv = dot(apart[...], kv)
        keys[at[b], :] = kv[:BLOCK].astype(bf16)
        values[at[b], :] = kv[BLOCK:].astype(bf16)
        keys_t[:, at[b]] = dot_nt(eye, keys[at[b], :]).astype(bf16)
        values_t[:, at[b]] = dot_nt(eye, values[at[b], :]).astype(bf16)
    dkeys[...] = jnp.zeros_like(dkeys)
    dvalues[...] = jnp.zeros_like(dvalues)
    half = BLOCK // 2
    near = [slice(b * BLOCK, b * BLOCK + half) for b in range(blocks)]
    other = [slice(b * BLOCK + half, (b + 1) * BLOCK) for b in range(blocks)]
    firsts = near_firsts(blocks)

    def scores_of(b):
        low = max(0, b - back)
        q = in_ref[mine[b], 0:HEADS, :].reshape(tall, HEAD_DIM)
        docs = row_docs[b : b + 1, :]
        row_max = jnp.full((8, tall), FAR_BELOW, f32)
        every = dot_nt(keys[low * BLOCK : (b + 1) * BLOCK, :], q)
        for n in range(b + 1 - low):
            scores = every[at[n], :]
            allowed = col_docs[at[low + n], 0:1] == docs
            if low + n == b:
                allowed = allowed & (key_pos[:, 0:1] <= row_pos[0:1, :])
            scores = jnp.where(allowed, scores, FAR_BELOW)
            held[b % 3, at[n], :] = scores
            row_max = jnp.maximum(row_max, jnp.max(scores.reshape(BLOCK // 8, 8, tall), axis=0))
            yield
        maxima[b] = jnp.max(row_max, axis=0, keepdims=True)

    def weights_of(b):
        low = max(0, b - back)
        do = in_ref[mine[b], HEADS : 2 * HEADS, :].reshape(tall, HEAD_DIM)
        weight_sum = jnp.zeros((8, tall), f32)
        row_dot = jnp.zeros((8, tall), f32)
        every = dot_nt(values[low * BLOCK : (b + 1) * BLOCK, :], do)
        for n in range(b + 1 - low):
            pushes = every[at[n], :]
            pushed[b % 3, at[n], :] = pushes
            weights = jnp.exp2((held[b % 3, at[n], :] - maxima[b]) * (FACTOR * LOG2E))
            held[b % 3, at[n], :] = weights
            weight_sum = weight_sum + jnp.sum(weights.reshape(BLOCK // 8, 8, tall), axis=0)
            row_dot = row_dot + jnp.sum((weights * pushes).reshape(BLOCK // 8, 8, tall), axis=0)
            yield
        inverse = 1.0 / jnp.sum(weight_sum, axis=0, keepdims=True)
        sums[b] = inverse, jnp.sum(row_dot, axis=0, keepdims=True) * inverse

    def grads_of(b):
        inverse, row_dot = sums[b]
        low = max(0, b - back)
        seen = slice(low * BLOCK, (b + 1) * BLOCK)
        count = b + 1 - low
        slot = b % 3
        q = in_ref[mine[b], 0:HEADS, :].reshape(tall, HEAD_DIM)
        do = in_ref[mine[b], HEADS : 2 * HEADS, :].reshape(tall, HEAD_DIM)
        for n in range(count):
            chances = held[slot, at[n], :] * inverse
            slope = (chances * (pushed[slot, at[n], :] - row_dot)).astype(bf16)
            chances = chances.astype(bf16)
            rounded[slot, at[n], :] = chances
            slopes[slot, at[n], :] = slope
            mine_at = slice(firsts[b] + n * half, firsts[b] + (n + 1) * half)
            near_slopes[mine_at, :] = slope[:half]
            near_chances[mine_at, :] = chances[:half]
            yield
        chances = rounded.at[slot, pl.ds(0, count * BLOCK), :]
        slope = slopes.at[slot, pl.ds(0, count * BLOCK), :]
        out_t = dot(values_t[:, seen], chances[...]).astype(bf16)
        yield
        dq_t = (dot(keys_t[:, seen], slope[...]) * FACTOR).astype(bf16)
        yield
        seen = slice(low * half, (b + 1) * half)
        slope = jnp.concatenate([slopes[slot, other[n], :] for n in range(count)], axis=0)
        chances = jnp.concatenate([rounded[slot, other[n], :] for n in range(count)], axis=0)
        dkeys[seen, :] += dot(slope, q)
        yield
        dvalues[seen, :] += dot(chances, do)
        yield
        out_ref[mine[b], 0:HEADS, :] = out_t.T.reshape(units, HEADS, HEAD_DIM)
        out_ref[mine[b], HEADS : 2 * HEADS, :] = dq_t.T.reshape(units, HEADS, HEAD_DIM)

    maxima, sums = {}, {}

    def together_run(*parts):
        parts = list(parts)
        while parts:
            parts = [part for part in parts if next(part, parts) is None]

    together_run(scores_of(0))
    together_run(scores_of(1), weights_of(0))
    for b in range(blocks):
        parts = [grads_of(b)]
        if b + 1 < blocks:
            parts.append(weights_of(b + 1))
        if b + 2 < blocks:
            parts.append(scores_of(b + 2))
        together_run(*parts)
    write_grads(together, dkeys, dvalues, far_grad)


def near_firsts(blocks):
    back = (REACH + BLOCK - 2) // BLOCK
    firsts = [0]
    for b in range(blocks):
        firsts.append(firsts[-1] + (min(b, back) + 1) * (BLOCK // 2))
    return firsts


def write_grads(together, dkeys, dvalues, grad):
    half = BLOCK // 2
    for b in range(dkeys.shape[0] // half):
        at = slice(b * half, (b + 1) * half)
        pair = jnp.concatenate(
            [(dkeys[at, :] * FACTOR).astype(bf16), dvalues[at, :].astype(bf16)], axis=0
        )
        units = half // UNIT
        grad[b * units : (b + 1) * units, :, :] = (
            dot(together[...], pair).astype(bf16).reshape(units, 2 * UNIT, HEAD_DIM)
        )


def near_kernel(together, in_ref, near_slopes, near_chances, near_grad, dkeys, dvalues):
    half = BLOCK // 2
    units = half // UNIT
    blocks = in_ref.shape[0] // units
    firsts = near_firsts(blocks)
    dkeys[...] = jnp.zeros_like(dkeys)
    dvalues[...] = jnp.zeros_like(dvalues)
    for b in range(blocks):
        mine = slice(b * units, (b + 1) * units)
        q = in_ref[mine, 0:HEADS, :].reshape(units * HEADS, HEAD_DIM)
        do = in_ref[mine, HEADS : 2 * HEADS, :].reshape(units * HEADS, HEAD_DIM)
        rows = slice(firsts[b], firsts[b + 1])
        seen = slice((b + 1) * half - (firsts[b + 1] - firsts[b]), (b + 1) * half)
        dkeys[seen, :] += dot(near_slopes[rows, :], q)
        dvalues[seen, :] += dot(near_chances[rows, :], do)
    write_grads(together, dkeys, dvalues, near_grad)


def local(queries, key_states, value_states, out_grad, destinations, documents):
    contexts = lax.axis_size("ctx")
    pairs = lax.axis_size("pair")
    packs = 2 * pairs
    kv_heads = key_states.shape[2] // HEAD_DIM
    swap = [(0, 1), (1, 0)]
    core = lax.axis_index("core")

    shape = jax.ShapeDtypeStruct
    whole = pl.BlockSpec(memory_space=pltpu.VMEM)
    away = pl.BlockSpec(memory_space=pl.ANY)

    def stay(x):
        return pltpu.with_memory_space_constraint(x, pltpu.HBM)

    scalars = pl.BlockSpec(memory_space=pltpu.SMEM)
    small = pltpu.CompilerParams(vmem_limit_bytes=40 * 1024 * 1024)
    moved_shape = shape((kv_heads * packs, ROWS, HEAD_DIM), bf16)
    sending = pl.pallas_call(
        send_kernel,
        in_specs=[away] * 5,
        out_specs=whole,
        out_shape=moved_shape,
        scratch_shapes=[
            pltpu.VMEM(destinations.shape, jnp.int32),
            pltpu.VMEM(queries.shape[1:], bf16),
            pltpu.VMEM(key_states.shape[1:], bf16),
            pltpu.VMEM(key_states.shape[1:], bf16),
            pltpu.VMEM(queries.shape[1:], bf16),
            pltpu.SemaphoreType.DMA((2 * kv_heads + 3,)),
        ],
        compiler_params=small,
    )(*map(stay, (destinations, queries, key_states, value_states, out_grad)))

    sending, other_documents = lax.optimization_barrier(
        (sending, lax.ppermute(documents, "core", swap))
    )
    received = lax.all_to_all(sending, ("ctx", "pair"), split_axis=0, concat_axis=0, tiled=True)
    near = received[:, 2 * HEADS :, :]
    far = lax.ppermute(near, "core", swap)

    length = contexts * BLOCK
    tall = GROUP * BLOCK // 2
    flags = jnp.stack([core, (lax.axis_index("ctx") % 2 == core).astype(core.dtype)])
    square = shape((2 * BLOCK, 2 * BLOCK), bf16)
    *prepared, move = pl.pallas_call(
        prepare_kernel,
        in_specs=[scalars, whole, whole, whole, away],
        out_specs=[whole] * 7,
        out_shape=[
            shape((contexts, tall), f32),
            shape((length, HEAD_DIM), f32),
            shape((8, tall), f32),
            shape((BLOCK, HEAD_DIM), f32),
            square,
            shape((BLOCK, BLOCK), bf16),
            square,
        ],
        compiler_params=small,
    )(
        flags.astype(jnp.int32).reshape(1, 2),
        destinations,
        documents.reshape(contexts, BLOCK),
        other_documents.reshape(contexts, BLOCK),
        near,
    )

    grad_shape = shape((kv_heads * packs, 2 * UNIT, HEAD_DIM), bf16)
    window = min(contexts, (REACH + BLOCK - 2) // BLOCK + 1) * BLOCK
    near_shape = shape((near_firsts(contexts)[-1], tall), bf16)
    results, far_grad, near_slopes, near_chances = pl.pallas_call(
        attend_kernel,
        in_specs=[whole] * 8,
        out_specs=[whole] * 4,
        out_shape=[moved_shape, grad_shape, near_shape, near_shape],
        scratch_shapes=[
            pltpu.VMEM((length, HEAD_DIM), bf16),
            pltpu.VMEM((length, HEAD_DIM), bf16),
            pltpu.VMEM((HEAD_DIM, length), bf16),
            pltpu.VMEM((HEAD_DIM, length), bf16),
            pltpu.VMEM((length // 2, HEAD_DIM), f32),
            pltpu.VMEM((length // 2, HEAD_DIM), f32),
            pltpu.VMEM((3, window, tall), f32),
            pltpu.VMEM((3, window, tall), f32),
            pltpu.VMEM((3, window, tall), bf16),
            pltpu.VMEM((3, window, tall), bf16),
        ],
        compiler_params=small,
    )(*prepared, received, far)

    far_grad = lax.ppermute(far_grad, "core", swap)
    near_grad = pl.pallas_call(
        near_kernel,
        in_specs=[whole] * 4,
        out_specs=whole,
        out_shape=grad_shape,
        scratch_shapes=[pltpu.VMEM((length // 2, HEAD_DIM), f32)] * 2,
        compiler_params=small,
    )(prepared[-1], received, near_slopes, near_chances)
    grads = near_grad.astype(f32) + far_grad.astype(f32)
    results = lax.dynamic_update_slice(results, grads.astype(bf16), (0, 2 * HEADS, 0))
    returned = lax.all_to_all(results, ("ctx", "pair"), split_axis=0, concat_axis=0, tiled=True)

    outs = (queries, queries, key_states, value_states)
    return pl.pallas_call(
        return_kernel,
        in_specs=[whole] * 2,
        out_specs=[away] * 4,
        out_shape=[shape(out.shape, bf16) for out in outs],
        scratch_shapes=[pltpu.VMEM(out.shape[1:], bf16) for out in outs]
        + [pltpu.SemaphoreType.DMA((4 * kv_heads + 2,))],
        compiler_params=small,
    )(move, returned)


def solution(mesh):
    split = jax.sharding.Mesh(
        mesh.devices.reshape(-1, 2, mesh.shape["ctx"]), ("pair", "core", "ctx")
    )
    spec = P(("pair", "core"), "ctx", None)
    return jax.shard_map(
        local,
        mesh=split,
        in_specs=(spec, spec, spec, spec, P(("pair", "core"), "ctx"), P(("pair", "core"), None)),
        out_specs=(spec, spec, spec, spec),
        check_vma=False,
    )
```

```python
import jax
import jax.numpy as jnp
from jax import lax
from jax.experimental import pallas as pl
from jax.experimental.pallas import tpu as pltpu
from jax.sharding import PartitionSpec as P

HEAD_DIM = 128
GROUP = 8
PAIR = 2
UNIT = 4
BLOCK = 128
REACH = 512
HEADS = GROUP * UNIT
ROWS = 2 * HEADS + 2 * UNIT
FAR_BELOW = -1e30
FACTOR = HEAD_DIM**-0.5
LOG2E = 1.4426950408889634

f32 = jnp.float32
bf16 = jnp.bfloat16


def dot(a, b):
    return jnp.dot(a, b, preferred_element_type=f32)


def dot_nt(a, b):
    return lax.dot_general(a, b, (((1,), (1,)), ((), ())), preferred_element_type=f32)


def sending_matrix(slots):
    units = BLOCK // UNIT
    size = PAIR * BLOCK
    unit = lax.broadcasted_iota(jnp.int32, (units, size), 0)
    col = lax.broadcasted_iota(jnp.int32, (units, size), 1)
    spread = ((col % BLOCK) // UNIT == unit).astype(f32).astype(bf16)
    packs = jnp.broadcast_to(slots.astype(f32), (8, units)).astype(bf16)
    where = dot(packs, spread)
    col = lax.broadcasted_iota(jnp.int32, (8, size), 1)
    inner = (col // BLOCK) * UNIT + col % UNIT
    place = where * (PAIR * UNIT) + inner.astype(f32)
    rows = lax.broadcasted_iota(jnp.int32, (size, size), 0).astype(f32)
    return (place[0:1] == rows).astype(f32).astype(bf16)


def returning_matrix(slots):
    units = BLOCK // UNIT
    size = PAIR * BLOCK
    row = lax.broadcasted_iota(jnp.int32, (size, units), 0)
    unit = lax.broadcasted_iota(jnp.int32, (size, units), 1)
    packs = jnp.broadcast_to(slots.astype(f32), (size, units))
    where = jnp.sum(
        jnp.where((row % BLOCK) // UNIT == unit, packs, 0.0), axis=1, keepdims=True
    )
    row = lax.broadcasted_iota(jnp.int32, (size, 1), 0)
    inner = (row // BLOCK) * UNIT + row % UNIT
    place = where * (PAIR * UNIT) + inner.astype(f32)
    cols = lax.broadcasted_iota(jnp.int32, (size, size), 1).astype(f32)
    return (place == cols).astype(f32).astype(bf16)


def slots_of(route):
    return (route % 2) * (BLOCK // UNIT // 2) + route // 2


def send_kernel(
    route_hbm, q_hbm, k_hbm, v_hbm, do_hbm, out_ref, route, q_buf, k_buf, v_buf, do_buf, in_sems
):
    packs = BLOCK // UNIT
    kv_heads = k_buf.shape[1] // HEAD_DIM
    group = GROUP * HEAD_DIM
    cut = 2
    share = kv_heads // cut
    asked = pltpu.make_async_copy(route_hbm, route, in_sems.at[2 * cut + 2])
    asked.start()
    loads = []
    for n in range(cut):
        at = pl.ds(n * share * group, share * group)
        pair = [
            pltpu.make_async_copy(q_hbm.at[0, :, at], q_buf.at[:, at], in_sems.at[2 * n]),
            pltpu.make_async_copy(do_hbm.at[0, :, at], do_buf.at[:, at], in_sems.at[2 * n + 1]),
        ]
        if n == 0:
            pair += [
                pltpu.make_async_copy(k_hbm.at[0], k_buf, in_sems.at[2 * cut]),
                pltpu.make_async_copy(v_hbm.at[0], v_buf, in_sems.at[2 * cut + 1]),
            ]
        for copy in pair:
            copy.start()
        loads.append(pair)
    asked.wait()
    slots = slots_of(route[...])
    move = sending_matrix(slots)
    wide = PAIR * UNIT
    for m in range(kv_heads):
        if m % share == 0:
            for copy in loads[m // share]:
                copy.wait()
        out = out_ref.at[pl.ds(m * packs, packs)]
        for some in range(0, GROUP, 2 * PAIR):
            moved = []
            for h in (some, some + PAIR):
                heads = [pl.ds(m * group + (h + j) * HEAD_DIM, HEAD_DIM) for j in range(PAIR)]
                both = jnp.concatenate(
                    [
                        jnp.concatenate([q_buf[:, at] for at in heads], axis=0),
                        jnp.concatenate([do_buf[:, at] for at in heads], axis=0),
                    ],
                    axis=1,
                )
                moved.append(dot(move, both).reshape(packs, wide, 2 * HEAD_DIM))
            moved = jnp.concatenate(moved, axis=1).astype(bf16)
            low = some * UNIT
            out[:, low : low + 2 * wide, :] = moved[:, :, :HEAD_DIM]
            low = HEADS + some * UNIT
            out[:, low : low + 2 * wide, :] = moved[:, :, HEAD_DIM:]
        at = slice(m * HEAD_DIM, (m + 1) * HEAD_DIM)
        pair = jnp.concatenate([k_buf[:, at], v_buf[:, at]], axis=0)
        out[:, 2 * HEADS :, :] = (
            dot(move, pair).astype(bf16).reshape(packs, wide, HEAD_DIM)
        )


def return_kernel(
    move, in_ref, o_hbm, dq_hbm, dk_hbm, dv_hbm, o_buf, dq_buf, dk_buf, dv_buf, sems
):
    packs = BLOCK // UNIT
    wide = PAIR * UNIT
    kv_heads = dk_buf.shape[1] // HEAD_DIM
    stores = []

    def store(buf, hbm, at):
        copy = pltpu.make_async_copy(buf.at[:, at], hbm.at[0, :, at], sems.at[len(stores)])
        copy.start()
        stores.append(copy)

    for m in range(kv_heads):
        block = in_ref.at[pl.ds(m * packs, packs)]
        kv = block[:, 2 * HEADS :, :].reshape(2 * BLOCK, HEAD_DIM)
        pair = dot(move[...], kv).astype(bf16)
        at = slice(m * HEAD_DIM, (m + 1) * HEAD_DIM)
        dk_buf[:, at] = pair[:BLOCK]
        dv_buf[:, at] = pair[BLOCK:]
        if m == kv_heads - 1:
            every = pl.ds(0, dk_buf.shape[1])
            store(dk_buf, dk_hbm, every)
            store(dv_buf, dv_hbm, every)
        for h in range(0, GROUP, PAIR):
            low = h * UNIT
            o = block[:, low : low + wide, :].reshape(packs * wide, HEAD_DIM)
            low = HEADS + h * UNIT
            dq = block[:, low : low + wide, :].reshape(packs * wide, HEAD_DIM)
            back = dot(move[...], jnp.concatenate([o, dq], axis=1)).astype(bf16)
            for j in range(PAIR):
                first = (m * GROUP + h + j) * HEAD_DIM
                at = slice(first, first + HEAD_DIM)
                rows = slice(j * BLOCK, (j + 1) * BLOCK)
                o_buf[:, at] = back[rows, :HEAD_DIM]
                dq_buf[:, at] = back[rows, HEAD_DIM:]
        at = pl.ds(m * GROUP * HEAD_DIM, GROUP * HEAD_DIM)
        store(o_buf, o_hbm, at)
        store(dq_buf, dq_hbm, at)
    for copy in stores:
        copy.wait()


def prepare_kernel(
    flags, route_ref, docs_ref, other_ref, near_hbm,
    row_docs, col_docs, row_pos, key_pos, apart, together, move,
):
    slots = slots_of(route_ref[...])
    move[...] = returning_matrix(slots)
    r = lax.broadcasted_iota(jnp.int32, (2 * BLOCK, 2 * BLOCK), 0)
    c = lax.broadcasted_iota(jnp.int32, (2 * BLOCK, 2 * BLOCK), 1)

    def place(x):
        inside = x % BLOCK
        unit = (inside % (BLOCK // 2)) // UNIT
        return (inside // (BLOCK // 2)) * BLOCK + unit * 2 * UNIT + (x // BLOCK) * UNIT + x % UNIT

    apart[...] = (place(r) == c).astype(f32).astype(bf16)
    r = lax.broadcasted_iota(jnp.int32, (BLOCK, BLOCK), 0)
    c = lax.broadcasted_iota(jnp.int32, (BLOCK, BLOCK), 1)
    inside = c % (BLOCK // 2)
    to = (inside // UNIT) * 2 * UNIT + (c // (BLOCK // 2)) * UNIT + c % UNIT
    together[...] = (to == r).astype(f32).astype(bf16)
    core = flags[0, 0]
    half = BLOCK // 2

    def key_at(x):
        owner = jnp.where(x < half, core, 1 - core)
        return (2 * ((x % half) // UNIT) + owner) * UNIT + x % UNIT

    def row_at(x):
        return (2 * (x // HEADS) + core) * UNIT + x % UNIT

    key_pos[...] = key_at(lax.broadcasted_iota(jnp.int32, key_pos.shape, 0)).astype(f32)
    row_pos[...] = row_at(lax.broadcasted_iota(jnp.int32, row_pos.shape, 1)).astype(f32)
    docs = jnp.where(flags[0, 1] == 1, docs_ref[...], other_ref[...])
    high = (docs // 32).astype(f32).astype(bf16)
    low = (docs % 32).astype(f32).astype(bf16)
    tall = row_docs.shape[1]
    pos = lax.broadcasted_iota(jnp.int32, (BLOCK, tall), 0)
    to_row = (row_at(lax.broadcasted_iota(jnp.int32, (BLOCK, tall), 1)) == pos).astype(f32).astype(bf16)
    row_docs[...] = dot(high, to_row) * 32 + dot(low, to_row)
    pos = lax.broadcasted_iota(jnp.int32, (BLOCK, BLOCK), 1)
    to_key = (key_at(lax.broadcasted_iota(jnp.int32, (BLOCK, BLOCK), 0)) == pos).astype(f32).astype(bf16)
    for b in range(docs.shape[0]):
        wide_high = jnp.broadcast_to(high[b : b + 1, :], (BLOCK, BLOCK))
        wide_low = jnp.broadcast_to(low[b : b + 1, :], (BLOCK, BLOCK))
        col_docs[b * BLOCK : (b + 1) * BLOCK, :] = (
            dot_nt(to_key, wide_high) * 32 + dot_nt(to_key, wide_low)
        )


def attend_kernel(
    row_docs, col_docs, row_pos, key_pos, apart, together, in_ref, far_ref,
    out_ref, far_grad, near_slopes, near_chances,
    keys, values, keys_t, values_t, dkeys, dvalues, held, pushed, rounded, slopes,
):
    blocks = row_docs.shape[0]
    units = BLOCK // UNIT // 2
    tall = units * HEADS
    back = (REACH + BLOCK - 2) // BLOCK
    at = [slice(b * BLOCK, (b + 1) * BLOCK) for b in range(blocks)]
    mine = [slice(b * units, (b + 1) * units) for b in range(blocks)]
    across = lax.broadcasted_iota(jnp.int32, (BLOCK, BLOCK), 1)
    eye = (lax.broadcasted_iota(jnp.int32, (BLOCK, BLOCK), 0) == across).astype(f32).astype(bf16)

    for b in range(blocks):
        kv = jnp.concatenate(
            [
                in_ref[mine[b], 2 * HEADS :, :].reshape(BLOCK, HEAD_DIM),
                far_ref[mine[b], :, :].reshape(BLOCK, HEAD_DIM),
            ],
            axis=0,
        )
        kv = dot(apart[...], kv)
        keys[at[b], :] = kv[:BLOCK].astype(bf16)
        values[at[b], :] = kv[BLOCK:].astype(bf16)
        keys_t[:, at[b]] = dot_nt(eye, keys[at[b], :]).astype(bf16)
        values_t[:, at[b]] = dot_nt(eye, values[at[b], :]).astype(bf16)
    dkeys[...] = jnp.zeros_like(dkeys)
    dvalues[...] = jnp.zeros_like(dvalues)
    half = BLOCK // 2
    near = [slice(b * BLOCK, b * BLOCK + half) for b in range(blocks)]
    other = [slice(b * BLOCK + half, (b + 1) * BLOCK) for b in range(blocks)]
    firsts = near_firsts(blocks)

    def scores_of(b):
        low = max(0, b - back)
        q = in_ref[mine[b], 0:HEADS, :].reshape(tall, HEAD_DIM)
        docs = row_docs[b : b + 1, :]
        row_max = jnp.full((8, tall), FAR_BELOW, f32)
        every = dot_nt(keys[low * BLOCK : (b + 1) * BLOCK, :], q)
        for n in range(b + 1 - low):
            scores = every[at[n], :]
            allowed = col_docs[at[low + n], 0:1] == docs
            if low + n == b:
                allowed = allowed & (key_pos[:, 0:1] <= row_pos[0:1, :])
            scores = jnp.where(allowed, scores, FAR_BELOW)
            held[b % 3, at[n], :] = scores
            row_max = jnp.maximum(row_max, jnp.max(scores.reshape(BLOCK // 8, 8, tall), axis=0))
            yield
        maxima[b] = jnp.max(row_max, axis=0, keepdims=True)

    def weights_of(b):
        low = max(0, b - back)
        do = in_ref[mine[b], HEADS : 2 * HEADS, :].reshape(tall, HEAD_DIM)
        weight_sum = jnp.zeros((8, tall), f32)
        row_dot = jnp.zeros((8, tall), f32)
        every = dot_nt(values[low * BLOCK : (b + 1) * BLOCK, :], do)
        for n in range(b + 1 - low):
            pushes = every[at[n], :]
            pushed[b % 3, at[n], :] = pushes
            weights = jnp.exp2((held[b % 3, at[n], :] - maxima[b]) * (FACTOR * LOG2E))
            held[b % 3, at[n], :] = weights
            weight_sum = weight_sum + jnp.sum(weights.reshape(BLOCK // 8, 8, tall), axis=0)
            row_dot = row_dot + jnp.sum((weights * pushes).reshape(BLOCK // 8, 8, tall), axis=0)
            yield
        inverse = 1.0 / jnp.sum(weight_sum, axis=0, keepdims=True)
        sums[b] = inverse, jnp.sum(row_dot, axis=0, keepdims=True) * inverse

    def grads_of(b):
        inverse, row_dot = sums[b]
        low = max(0, b - back)
        seen = slice(low * BLOCK, (b + 1) * BLOCK)
        count = b + 1 - low
        slot = b % 3
        q = in_ref[mine[b], 0:HEADS, :].reshape(tall, HEAD_DIM)
        do = in_ref[mine[b], HEADS : 2 * HEADS, :].reshape(tall, HEAD_DIM)
        for n in range(count):
            chances = held[slot, at[n], :] * inverse
            slope = (chances * (pushed[slot, at[n], :] - row_dot)).astype(bf16)
            chances = chances.astype(bf16)
            rounded[slot, at[n], :] = chances
            slopes[slot, at[n], :] = slope
            mine_at = slice(firsts[b] + n * half, firsts[b] + (n + 1) * half)
            near_slopes[mine_at, :] = slope[:half]
            near_chances[mine_at, :] = chances[:half]
            yield
        chances = rounded.at[slot, pl.ds(0, count * BLOCK), :]
        slope = slopes.at[slot, pl.ds(0, count * BLOCK), :]
        out_t = dot(values_t[:, seen], chances[...]).astype(bf16)
        yield
        dq_t = (dot(keys_t[:, seen], slope[...]) * FACTOR).astype(bf16)
        yield
        seen = slice(low * half, (b + 1) * half)
        slope = jnp.concatenate([slopes[slot, other[n], :] for n in range(count)], axis=0)
        chances = jnp.concatenate([rounded[slot, other[n], :] for n in range(count)], axis=0)
        dkeys[seen, :] += dot(slope, q)
        yield
        dvalues[seen, :] += dot(chances, do)
        yield
        out_ref[mine[b], 0:HEADS, :] = out_t.T.reshape(units, HEADS, HEAD_DIM)
        out_ref[mine[b], HEADS : 2 * HEADS, :] = dq_t.T.reshape(units, HEADS, HEAD_DIM)

    maxima, sums = {}, {}

    def together_run(*parts):
        parts = list(parts)
        while parts:
            parts = [part for part in parts if next(part, parts) is None]

    together_run(scores_of(0))
    together_run(scores_of(1), weights_of(0))
    for b in range(blocks):
        parts = [grads_of(b)]
        if b + 1 < blocks:
            parts.append(weights_of(b + 1))
        if b + 2 < blocks:
            parts.append(scores_of(b + 2))
        together_run(*parts[::-1])
    write_grads(together, dkeys, dvalues, far_grad)


def near_firsts(blocks):
    back = (REACH + BLOCK - 2) // BLOCK
    firsts = [0]
    for b in range(blocks):
        firsts.append(firsts[-1] + (min(b, back) + 1) * (BLOCK // 2))
    return firsts


def write_grads(together, dkeys, dvalues, grad):
    half = BLOCK // 2
    for b in range(dkeys.shape[0] // half):
        at = slice(b * half, (b + 1) * half)
        pair = jnp.concatenate(
            [(dkeys[at, :] * FACTOR).astype(bf16), dvalues[at, :].astype(bf16)], axis=0
        )
        units = half // UNIT
        grad[b * units : (b + 1) * units, :, :] = (
            dot(together[...], pair).astype(bf16).reshape(units, 2 * UNIT, HEAD_DIM)
        )


def near_kernel(together, in_ref, near_slopes, near_chances, near_grad, dkeys, dvalues):
    half = BLOCK // 2
    units = half // UNIT
    blocks = in_ref.shape[0] // units
    firsts = near_firsts(blocks)
    dkeys[...] = jnp.zeros_like(dkeys)
    dvalues[...] = jnp.zeros_like(dvalues)
    for b in range(blocks):
        mine = slice(b * units, (b + 1) * units)
        q = in_ref[mine, 0:HEADS, :].reshape(units * HEADS, HEAD_DIM)
        do = in_ref[mine, HEADS : 2 * HEADS, :].reshape(units * HEADS, HEAD_DIM)
        rows = slice(firsts[b], firsts[b + 1])
        seen = slice((b + 1) * half - (firsts[b + 1] - firsts[b]), (b + 1) * half)
        dkeys[seen, :] += dot(near_slopes[rows, :], q)
        dvalues[seen, :] += dot(near_chances[rows, :], do)
    write_grads(together, dkeys, dvalues, near_grad)


def local(queries, key_states, value_states, out_grad, destinations, documents):
    contexts = lax.axis_size("ctx")
    pairs = lax.axis_size("pair")
    packs = 2 * pairs
    kv_heads = key_states.shape[2] // HEAD_DIM
    swap = [(0, 1), (1, 0)]
    core = lax.axis_index("core")

    shape = jax.ShapeDtypeStruct
    whole = pl.BlockSpec(memory_space=pltpu.VMEM)
    away = pl.BlockSpec(memory_space=pl.ANY)

    def stay(x):
        return pltpu.with_memory_space_constraint(x, pltpu.HBM)

    scalars = pl.BlockSpec(memory_space=pltpu.SMEM)
    small = pltpu.CompilerParams(vmem_limit_bytes=40 * 1024 * 1024)
    moved_shape = shape((kv_heads * packs, ROWS, HEAD_DIM), bf16)
    sending = pl.pallas_call(
        send_kernel,
        in_specs=[away] * 5,
        out_specs=whole,
        out_shape=moved_shape,
        scratch_shapes=[
            pltpu.VMEM(destinations.shape, jnp.int32),
            pltpu.VMEM(queries.shape[1:], bf16),
            pltpu.VMEM(key_states.shape[1:], bf16),
            pltpu.VMEM(key_states.shape[1:], bf16),
            pltpu.VMEM(queries.shape[1:], bf16),
            pltpu.SemaphoreType.DMA((2 * kv_heads + 3,)),
        ],
        compiler_params=small,
    )(*map(stay, (destinations, queries, key_states, value_states, out_grad)))

    sending, other_documents = lax.optimization_barrier(
        (sending, lax.ppermute(documents, "core", swap))
    )
    received = lax.all_to_all(sending, ("ctx", "pair"), split_axis=0, concat_axis=0, tiled=True)
    near = received[:, 2 * HEADS :, :]
    far = lax.ppermute(near, "core", swap)

    length = contexts * BLOCK
    tall = GROUP * BLOCK // 2
    flags = jnp.stack([core, (lax.axis_index("ctx") % 2 == core).astype(core.dtype)])
    square = shape((2 * BLOCK, 2 * BLOCK), bf16)
    *prepared, move = pl.pallas_call(
        prepare_kernel,
        in_specs=[scalars, whole, whole, whole, away],
        out_specs=[whole] * 7,
        out_shape=[
            shape((contexts, tall), f32),
            shape((length, HEAD_DIM), f32),
            shape((8, tall), f32),
            shape((BLOCK, HEAD_DIM), f32),
            square,
            shape((BLOCK, BLOCK), bf16),
            square,
        ],
        compiler_params=small,
    )(
        flags.astype(jnp.int32).reshape(1, 2),
        destinations,
        documents.reshape(contexts, BLOCK),
        other_documents.reshape(contexts, BLOCK),
        near,
    )

    grad_shape = shape((kv_heads * packs, 2 * UNIT, HEAD_DIM), bf16)
    window = min(contexts, (REACH + BLOCK - 2) // BLOCK + 1) * BLOCK
    near_shape = shape((near_firsts(contexts)[-1], tall), bf16)
    results, far_grad, near_slopes, near_chances = pl.pallas_call(
        attend_kernel,
        in_specs=[whole] * 8,
        out_specs=[whole] * 4,
        out_shape=[moved_shape, grad_shape, near_shape, near_shape],
        scratch_shapes=[
            pltpu.VMEM((length, HEAD_DIM), bf16),
            pltpu.VMEM((length, HEAD_DIM), bf16),
            pltpu.VMEM((HEAD_DIM, length), bf16),
            pltpu.VMEM((HEAD_DIM, length), bf16),
            pltpu.VMEM((length // 2, HEAD_DIM), f32),
            pltpu.VMEM((length // 2, HEAD_DIM), f32),
            pltpu.VMEM((3, window, tall), f32),
            pltpu.VMEM((3, window, tall), f32),
            pltpu.VMEM((3, window, tall), bf16),
            pltpu.VMEM((3, window, tall), bf16),
        ],
        compiler_params=small,
    )(*prepared, received, far)

    far_grad = lax.ppermute(far_grad, "core", swap)
    near_grad = pl.pallas_call(
        near_kernel,
        in_specs=[whole] * 4,
        out_specs=whole,
        out_shape=grad_shape,
        scratch_shapes=[pltpu.VMEM((length // 2, HEAD_DIM), f32)] * 2,
        compiler_params=small,
    )(prepared[-1], received, near_slopes, near_chances)
    grads = near_grad.astype(f32) + far_grad.astype(f32)
    results = lax.dynamic_update_slice(results, grads.astype(bf16), (0, 2 * HEADS, 0))
    returned = lax.all_to_all(results, ("ctx", "pair"), split_axis=0, concat_axis=0, tiled=True)

    outs = (queries, queries, key_states, value_states)
    return pl.pallas_call(
        return_kernel,
        in_specs=[whole] * 2,
        out_specs=[away] * 4,
        out_shape=[shape(out.shape, bf16) for out in outs],
        scratch_shapes=[pltpu.VMEM(out.shape[1:], bf16) for out in outs]
        + [pltpu.SemaphoreType.DMA((4 * kv_heads + 2,))],
        compiler_params=small,
    )(move, returned)


def solution(mesh):
    split = jax.sharding.Mesh(
        mesh.devices.reshape(-1, 2, mesh.shape["ctx"]), ("pair", "core", "ctx")
    )
    spec = P(("pair", "core"), "ctx", None)
    return jax.shard_map(
        local,
        mesh=split,
        in_specs=(spec, spec, spec, spec, P(("pair", "core"), "ctx"), P(("pair", "core"), None)),
        out_specs=(spec, spec, spec, spec),
        check_vma=False,
    )
```
